32 devices in a mesh: dp: 4 (over z), grad: 8 (over y, x, core).
Axes of the slice: x: 2, y: 2, z: 4, core: 2. Of those that a mesh axis runs over, the one named last changes fastest.
Arguments:
- factor_inputs: bfloat16 [512, 4, 1024], P('dp', None, 'grad'), may hold values from -6 to 6
- gradients: bfloat16 [4, 6144, 1024], P('dp', 'grad'), may hold values from -6 to 6
Outputs:
- preconditioned: bfloat16 [4, 6144, 1024], P('dp', 'grad')
The draws below stay inside these ranges and needn't reach their ends.
All inputs are finite; a program needn't handle non-finite values. Where the reference program divides by a largest or mean magnitude, that divisor is 1e-20 or more.
Results may differ from the reference program's by a relative error of at most 0.0065.
Values may be sent and summed in bfloat16 or wider, within the bound.
No kernel may reach another device: no remote copies, remote signals or barrier semaphores. Data moves between devices by JAX's collectives and lax.ppermute only.
A program may use at most 64 MiB of HBM per device.

```python
import jax
import jax.numpy as jnp
from jax import lax

MODEL = 6144
B = 1024
ITERS = 4
NF = 4
TOKENS = 512


def draw_factor_inputs(key, part):
    key = jax.random.fold_in(key, 11)
    noise_key, coef_key, sign_key = jax.random.split(key, 3)
    noise = jnp.clip(jax.random.normal(noise_key, (TOKENS, NF, B), jnp.float32), -4.5, 4.5)
    coefs = jnp.clip(jax.random.normal(coef_key, (TOKENS, NF, 1), jnp.float32), -3.0, 3.0)
    strength = 10.0
    signs = 2.0 * jax.random.randint(sign_key, (1, NF, B), 0, 2).astype(jnp.float32) - 1.0
    amplitude = jnp.sqrt(jnp.float32(strength) / B)
    return (noise + amplitude * coefs * signs).astype(jnp.bfloat16)


def block_scale(stream_key, shape, cuts, smallest, top_value):
    loudness = 1.0
    for axis_at, shards_of in cuts:
        draws = jax.random.uniform(jax.random.fold_in(jax.random.fold_in(stream_key, 6), axis_at), (shards_of,), jnp.float32, smallest / len(cuts), top_value / len(cuts))
        loudness = loudness * jnp.repeat(jnp.exp(draws), shape[axis_at] // shards_of).reshape((-1,) + (1,) * (len(shape) - 1 - axis_at))
    return loudness


def centred(own_key, extent, width, reach, cuts=(), kind=jnp.bfloat16):
    drawn = jax.random.normal(own_key, extent, jnp.float32) * width
    if len(cuts) > 0:
        drawn = block_scale(own_key, extent, cuts, -0.22, 0.18) * drawn
    return jnp.clip(drawn, min=-reach, max=reach).astype(kind)


def setup_inputs(seed: int = 0) -> dict:
    seeds = jax.random.split(jax.random.key(seed), 3)
    return {
        "factor_inputs": draw_factor_inputs(jax.random.fold_in(seeds[2], 71), 0),
        "gradients": centred(seeds[1], (NF, MODEL, B), 1.0, 6.0, ((0, 4), (1, 8))),
    }


DAMPING = 0.01


def one_factor(pair):
    columns, tile = pair
    covariance = jnp.dot(columns.T, columns, preferred_element_type=jnp.float32) * (1.0 / TOKENS)
    identity = jnp.eye(B, dtype=jnp.float32)
    damped = covariance + DAMPING * identity
    bound = jnp.max(jnp.sum(jnp.abs(damped), axis=1))
    iterate = (identity * (1.0 / bound)).astype(jnp.bfloat16)
    lowered = damped.astype(jnp.bfloat16)
    for step in range(ITERS):
        image = jnp.dot(lowered, iterate, preferred_element_type=jnp.float32).astype(jnp.bfloat16)
        product = jnp.dot(image, iterate, preferred_element_type=jnp.float32)
        iterate = (2.0 * iterate.astype(jnp.float32) - product).astype(jnp.bfloat16)
    return jnp.dot(tile, iterate, preferred_element_type=jnp.float32).astype(jnp.bfloat16)


def reference(factor_inputs, gradients):
    stacked = jnp.transpose(factor_inputs, (1, 0, 2))
    return lax.map(one_factor, (stacked, gradients))
```

```python
import jax
import jax.numpy as jnp
from jax import lax
from jax.sharding import PartitionSpec as P

ITERS = 4
DAMPING = 0.01
TERMS = 2**ITERS


def gather_block(factor_inputs):
    pieces = jnp.transpose(factor_inputs, (1, 0, 2))
    piece = lax.all_to_all(pieces, "dp", split_axis=0, concat_axis=1, tiled=True)[0]
    return lax.all_gather(piece, "grad", axis=1, tiled=True)


def gather_block_by_steps(factor_inputs):
    replicas, members = lax.axis_size("dp"), lax.axis_size("grad")
    here, member = lax.axis_index("dp"), lax.axis_index("grad")
    pieces = jnp.transpose(factor_inputs, (1, 0, 2))
    parts = []
    for step in range(replicas):
        there = lax.rem(here + step, replicas)
        part = lax.dynamic_index_in_dim(pieces, there, 0, keepdims=False)
        if step:
            part = lax.ppermute(part, "dp", [(i, (i + step) % replicas) for i in range(replicas)])
        parts.append(part)
    held = [jnp.concatenate(parts, axis=0)]
    for far in range(2, members, 2):
        held.append(lax.ppermute(held[0], "grad", [(i, i ^ far) for i in range(members)]))
    near = [lax.ppermute(one, "grad", [(i, i ^ 1) for i in range(members)]) for one in held]
    stacked = jnp.stack([one for pair in zip(held, near) for one in pair])
    ordered = stacked[jnp.arange(members) ^ member]
    return jnp.transpose(ordered, (1, 0, 2)).reshape(ordered.shape[1], -1)


def largest_row(columns, tokens):
    covariance = jnp.einsum("tr,tc->rc", columns, columns, preferred_element_type=jnp.float32)
    return jnp.max(jnp.sum(jnp.abs(covariance), axis=1)) * (1.0 / tokens) + DAMPING


def times(a, b):
    product = jnp.dot(a[1].astype(jnp.bfloat16), b[1].astype(jnp.bfloat16), preferred_element_type=jnp.float32)
    return a[0] * b[0], a[0] * b[1] + b[0] * a[1] + product


def by_tokens(columns, tile):
    tokens = columns.shape[0]
    scale = 1.0 / largest_row(columns, tokens)
    gram = jnp.einsum("sc,tc->st", columns, columns, preferred_element_type=jnp.float32)
    image = jnp.einsum("rc,tc->rt", tile, columns, preferred_element_type=jnp.float32).astype(jnp.bfloat16)
    eps = 1.0 - scale * DAMPING
    sums = [jnp.float32(1.0)]
    for _ in range(TERMS - 1):
        sums.append(sums[-1] * eps + 1.0)
    powers = [(jnp.float32(1.0), None), (eps, gram * (-scale / tokens))]
    powers.append(times(powers[1], powers[1]))
    powers.append(times(powers[2], powers[1]))
    fourth = times(powers[2], powers[2])

    def block(i):
        shift, rest = sums[14 - 4 * i], 0.0
        for j in range(1, 4):
            if 4 * i + j < TERMS - 1:
                weight = sums[14 - 4 * i - j]
                shift, rest = shift + weight * powers[j][0], rest + weight * powers[j][1]
        return shift, rest

    total = block(3)
    for i in (2, 1, 0):
        product, own = times(total, fourth), block(i)
        total = product[0] + own[0], product[1] + own[1]
    mixed = jnp.dot(image, total[1].astype(jnp.bfloat16), preferred_element_type=jnp.float32)
    mixed = (mixed + total[0] * image.astype(jnp.float32)) * (-scale * scale / tokens)
    moved = jnp.dot(mixed.astype(jnp.bfloat16), columns, preferred_element_type=jnp.float32)
    return scale * sums[TERMS - 1] * tile.astype(jnp.float32) + moved


def by_features(columns, tile):
    tokens, width = columns.shape
    scale = 1.0 / largest_row(columns, tokens)
    covariance = jnp.einsum("tr,tc->rc", columns, columns, preferred_element_type=jnp.float32) * (1.0 / tokens)
    image = scale * (covariance + DAMPING * jnp.eye(width, dtype=jnp.float32))
    result = scale * tile.astype(jnp.float32)
    for step in range(ITERS):
        low = image.astype(jnp.bfloat16)
        result = 2.0 * result - jnp.dot(result.astype(jnp.bfloat16), low, preferred_element_type=jnp.float32)
        if step < ITERS - 1:
            image = 2.0 * image - jnp.dot(low, low, preferred_element_type=jnp.float32)
    return result


def local(factor_inputs, gradients):
    rows, members = factor_inputs.shape[2], lax.axis_size("grad")
    tokens = factor_inputs.shape[0] * lax.axis_size("dp")
    tile = gradients[0]
    if tokens < rows * members:
        result = by_tokens(gather_block_by_steps(factor_inputs), tile)
    else:
        result = by_features(gather_block(factor_inputs), tile)
    return result.astype(jnp.bfloat16)[None]


def solution(mesh):
    placed = (P("dp", None, "grad"), P("dp", "grad", None))
    return jax.shard_map(
        local, mesh=mesh, in_specs=placed, out_specs=P("dp", "grad", None), check_vma=False
    )
```

```python
import functools

import jax
import jax.numpy as jnp
from jax import lax
from jax.experimental import pallas as pl
from jax.experimental.pallas import tpu as pltpu
from jax.sharding import PartitionSpec as P

ITERS = 4
DAMPING = 0.01
WHOLE = pl.BlockSpec(memory_space=pltpu.VMEM)
ANYWHERE = pl.BlockSpec(memory_space=pl.ANY)


def dot(a, b):
    return jnp.dot(a, b, preferred_element_type=jnp.float32)


def gather_block(factor_inputs):
    pieces = jnp.transpose(factor_inputs, (1, 0, 2))
    piece = lax.all_to_all(pieces, "dp", split_axis=0, concat_axis=1, tiled=True)[0]
    return lax.all_gather(piece, "grad", axis=1, tiled=True)


def by_features(columns, tile):
    tokens, width = columns.shape
    covariance = jnp.einsum("tr,tc->rc", columns, columns, preferred_element_type=jnp.float32) * (1.0 / tokens)
    damped = covariance + DAMPING * jnp.eye(width, dtype=jnp.float32)
    scale = 1.0 / jnp.max(jnp.sum(jnp.abs(damped), axis=1))
    image = scale * damped
    result = scale * tile.astype(jnp.float32)
    for step in range(ITERS):
        low = image.astype(jnp.bfloat16)
        result = 2.0 * result - dot(result.astype(jnp.bfloat16), low)
        if step < ITERS - 1:
            image = 2.0 * image - dot(low, low)
    return result


def split_blocks(factor_inputs):
    tokens, blocks, features = factor_inputs.shape

    def kernel(x_ref, out_ref):
        for block in range(blocks):
            out_ref[block] = x_ref[:, block, :]

    return pl.pallas_call(
        kernel,
        out_shape=jax.ShapeDtypeStruct((blocks, tokens, features), factor_inputs.dtype),
        in_specs=[WHOLE],
        out_specs=WHOLE,
    )(factor_inputs)


def block_kernel(count, *refs):
    pieces = refs[:count]
    tile_hbm, out_hbm = refs[count : count + 2]
    x, xt, tile, image, out, sems = refs[count + 2 :]
    tokens, width = x.shape
    rows = tile.shape[0]
    step = rows // 3
    features = width // count
    member = lax.axis_index("grad")
    load = pltpu.make_async_copy(tile_hbm, tile, sems.at[0])
    load.start()
    for far in range(count):
        at = pl.multiple_of((member ^ far) * features, features)
        piece = pieces[far][...]
        x[:, pl.ds(at, features)] = piece
        xt[pl.ds(at, features), :] = piece.T
    gram = dot(x[...], xt[...]) * (1.0 / tokens)
    low = gram.astype(jnp.bfloat16)
    second = dot(low, low)
    low2 = second.astype(jnp.bfloat16)
    largest = jnp.zeros((1, 1), jnp.float32)
    for at in range(0, width, 256):
        sums = jnp.sum(jnp.abs(dot(xt[...], x[:, at : at + 256])), axis=0, keepdims=True)
        largest = jnp.maximum(largest, jnp.max(sums, axis=1, keepdims=True))
    third, fourth = dot(low2, low), dot(low2, low2)
    load.wait()
    for at in range(0, rows, step):
        image[at : at + step, :] = dot(tile[at : at + step, :], xt[...]).astype(jnp.bfloat16)

    c = 1.0 / (largest * (1.0 / tokens) + DAMPING)
    eps = 1.0 - c * DAMPING
    eps2 = eps * eps
    eps3 = eps2 * eps
    eps4 = eps2 * eps2
    c2 = c * c
    c3 = c2 * c
    rows_id = lax.broadcasted_iota(jnp.int32, (tokens, tokens), 0)
    cols_id = lax.broadcasted_iota(jnp.int32, (tokens, tokens), 1)
    eye = (rows_id == cols_id).astype(jnp.float32)
    e1 = -c * gram
    e2 = -2.0 * eps * c * gram + c2 * second
    e3 = -3.0 * eps2 * c * gram + 3.0 * eps * c2 * second - c3 * third
    e4 = -4.0 * eps3 * c * gram + 6.0 * eps2 * c2 * second - 4.0 * eps * c3 * third + c2 * c2 * fourth
    u_m, u_n = 1.0 + eps + eps2 + eps3, e1 + e2 + e3
    w_m, w_n = 4.0 * eps3, eps2 * e1 + eps * e2 + e3
    a_m, a_n = u_m * w_m, u_m * w_n + w_m * u_n + dot(u_n.astype(jnp.bfloat16), w_n.astype(jnp.bfloat16))
    low4 = e4.astype(jnp.bfloat16)
    y_m = 1.0 + 2.0 * eps4 + 3.0 * eps4 * eps4
    y_n = (1.0 + 3.0 * eps4) * e4 + dot(low4, low4)
    q_m, q_n = a_m * y_m, a_m * y_n + y_m * a_n + dot(a_n.astype(jnp.bfloat16), y_n.astype(jnp.bfloat16))
    v = (1.0 + eps4) * (1.0 + eps4 * eps4)
    q_m = q_m + v * (1.0 + 2.0 * eps + 3.0 * eps2)
    q_n = q_n + v * ((1.0 + eps) * e1 + e2)
    q = ((q_m * eye + q_n) * (-c2 * (1.0 / tokens))).astype(jnp.bfloat16)
    p = c * (1.0 + eps) * (1.0 + eps2) * v
    stores = []
    for k, at in enumerate(range(0, rows, step)):
        mixed = dot(image[at : at + step, :], q).astype(jnp.bfloat16)
        moved = dot(mixed, x[...])
        out[at : at + step, :] = (p * tile[at : at + step, :].astype(jnp.float32) + moved).astype(jnp.bfloat16)
        store = pltpu.make_async_copy(out.at[pl.ds(at, step), :], out_hbm.at[pl.ds(at, step), :], sems.at[1 + k])
        store.start()
        stores.append(store)
    for store in stores:
        store.wait()


def by_tokens(pieces, tile):
    rows, width = tile.shape
    tokens = pieces[0].shape[0]
    return pl.pallas_call(
        functools.partial(block_kernel, len(pieces)),
        out_shape=jax.ShapeDtypeStruct((rows, width), jnp.bfloat16),
        in_specs=[WHOLE] * len(pieces) + [ANYWHERE],
        out_specs=ANYWHERE,
        scratch_shapes=[
            pltpu.VMEM((tokens, width), jnp.bfloat16),
            pltpu.VMEM((width, tokens), jnp.bfloat16),
            pltpu.VMEM((rows, width), jnp.bfloat16),
            pltpu.VMEM((rows, tokens), jnp.bfloat16),
            pltpu.VMEM((rows, width), jnp.bfloat16),
            pltpu.SemaphoreType.DMA((4,)),
        ],
        compiler_params=pltpu.CompilerParams(vmem_limit_bytes=40 * 2**20),
        name="whole_block",
    )(*pieces, tile)


def gather_pieces(factor_inputs):
    members = lax.axis_size("grad")
    parts = lax.all_to_all(split_blocks(factor_inputs), "dp", split_axis=0, concat_axis=0, tiled=True)
    held = [parts.reshape(-1, parts.shape[2])]
    for far in range(2, members, 2):
        held.append(lax.ppermute(held[0], "grad", [(i, i ^ far) for i in range(members)]))
    near = [lax.ppermute(one, "grad", [(i, i ^ 1) for i in range(members)]) for one in held]
    return [one for pair in zip(held, near) for one in pair]


def local(factor_inputs, gradients):
    features, members = factor_inputs.shape[2], lax.axis_size("grad")
    tokens = factor_inputs.shape[0] * lax.axis_size("dp")
    tile = gradients[0]
    if tokens < features * members and features % 128 == 0 and members & (members - 1) == 0:
        result = by_tokens(gather_pieces(factor_inputs), tile)
    else:
        result = by_features(gather_block(factor_inputs), tile)
    return result.astype(jnp.bfloat16)[None]


def solution(mesh):
    placed = (P("dp", None, "grad"), P("dp", "grad", None))
    return jax.shard_map(
        local, mesh=mesh, in_specs=placed, out_specs=P("dp", "grad", None), check_vma=False
    )
```

```python
import functools

import jax
import jax.numpy as jnp
from jax import lax
from jax.experimental import pallas as pl
from jax.experimental.pallas import tpu as pltpu
from jax.sharding import PartitionSpec as P

ITERS = 4
DAMPING = 0.01
WHOLE = pl.BlockSpec(memory_space=pltpu.VMEM)
ANYWHERE = pl.BlockSpec(memory_space=pl.ANY)


def dot(a, b):
    return jnp.dot(a, b, preferred_element_type=jnp.float32)


def gather_block(factor_inputs):
    pieces = jnp.transpose(factor_inputs, (1, 0, 2))
    piece = lax.all_to_all(pieces, "dp", split_axis=0, concat_axis=1, tiled=True)[0]
    return lax.all_gather(piece, "grad", axis=1, tiled=True)


def by_features(columns, tile):
    tokens, width = columns.shape
    covariance = jnp.einsum("tr,tc->rc", columns, columns, preferred_element_type=jnp.float32) * (1.0 / tokens)
    damped = covariance + DAMPING * jnp.eye(width, dtype=jnp.float32)
    scale = 1.0 / jnp.max(jnp.sum(jnp.abs(damped), axis=1))
    image = scale * damped
    result = scale * tile.astype(jnp.float32)
    for step in range(ITERS):
        low = image.astype(jnp.bfloat16)
        result = 2.0 * result - dot(result.astype(jnp.bfloat16), low)
        if step < ITERS - 1:
            image = 2.0 * image - dot(low, low)
    return result


def split_kernel(x_ref, *out_refs):
    replicas, tokens = len(out_refs), out_refs[0].shape[0]
    here = lax.axis_index("dp")
    x = x_ref[...]
    rows = lax.broadcasted_iota(jnp.int32, (tokens, tokens * replicas), 0)
    cols = lax.broadcasted_iota(jnp.int32, (tokens, tokens * replicas), 1)
    offset = cols - rows * replicas
    for far, out_ref in enumerate(out_refs):
        choice = jnp.where(offset == (here ^ far), 1.0, 0.0).astype(jnp.bfloat16)
        out_ref[...] = dot(choice, x).astype(jnp.bfloat16)


def split_blocks(factor_inputs):
    tokens, blocks, features = factor_inputs.shape
    return pl.pallas_call(
        split_kernel,
        out_shape=[jax.ShapeDtypeStruct((tokens, features), factor_inputs.dtype)] * blocks,
        in_specs=[WHOLE],
        out_specs=[WHOLE] * blocks,
        name="split_blocks",
    )(factor_inputs.reshape(tokens * blocks, features))


def column_sums(a, b):
    return jnp.sum(jnp.abs(dot(a, b)), axis=0, keepdims=True)


def absorb(fars, pieces, turned, tile, member):
    features = pieces[0].shape[1]
    pairs = [jnp.concatenate([a[...], b[...]], axis=1) for a, b in zip(pieces[::2], pieces[1::2])]
    columns = pairs[-1]
    columns_t = columns.T
    gram = dot(columns, columns_t)
    mine = jnp.concatenate([tile[:, place(member, fars[-1] + one, features)] for one in (0, 1)], axis=1)
    image = dot(mine, columns_t)
    sums = column_sums(columns_t, columns)
    before = []
    for earlier, earlier_t in zip(pairs, turned):
        sums = sums + column_sums(earlier_t[...], columns)
        before.append(column_sums(columns_t, earlier))
    return columns_t, gram, image, jnp.concatenate(before + [sums], axis=0)


def place(member, far, features):
    return pl.ds(pl.multiple_of((member ^ far) * features, features), features)


def first_kernel(fars, p0, p1, tile, turned, gram_out, image_out, sums_out):
    turned[...], gram_out[...], image_out[...], sums_out[...] = absorb(
        fars, (p0, p1), (), tile, lax.axis_index("grad")
    )


def take(fars, refs):
    count = len(fars)
    return refs[: 2 * count], refs[2 * count : 3 * count - 1], refs[3 * count - 1 :]


def next_kernel(fars, *refs):
    pieces, earlier, refs = take(fars, refs)
    tile, gram_in, image_in, sums_in, turned, gram_out, image_out, sums_out = refs
    done = len(fars) - 1
    turned[...], gram, image, sums = absorb(fars, pieces, earlier, tile, lax.axis_index("grad"))
    gram_out[...] = gram_in[...] + gram
    image_out[...] = image_in[...] + image
    sums_out[:done, :] = sums_in[...] + sums[:done]
    sums_out[done:, :] = sums[done:]


def last_kernel(fars, *refs):
    pieces, earlier, refs = take(fars, refs)
    tile, gram_in, image_in, sums_in, out_hbm, out, sems = refs
    done = len(fars) - 1
    member = lax.axis_index("grad")
    tokens, features = pieces[0].shape
    rows = tile.shape[0]
    step = rows // 3
    _, gram, image, sums = absorb(fars, pieces, earlier, tile, member)
    gram = (gram_in[...] + gram) * (1.0 / tokens)
    image = (image_in[...] + image).astype(jnp.bfloat16)
    low = gram.astype(jnp.bfloat16)
    second = dot(low, low)
    low2 = second.astype(jnp.bfloat16)
    third, fourth = dot(low2, low), dot(low2, low2)
    sums = jnp.concatenate([sums_in[...] + sums[:done], sums[done:]], axis=0)
    largest = jnp.max(jnp.max(sums, axis=0, keepdims=True), axis=1, keepdims=True)

    c = 1.0 / (largest * (1.0 / tokens) + DAMPING)
    eps = 1.0 - c * DAMPING
    eps2 = eps * eps
    eps3 = eps2 * eps
    eps4 = eps2 * eps2
    c2 = c * c
    c3 = c2 * c
    rows_id = lax.broadcasted_iota(jnp.int32, (tokens, tokens), 0)
    cols_id = lax.broadcasted_iota(jnp.int32, (tokens, tokens), 1)
    eye = (rows_id == cols_id).astype(jnp.float32)
    e1 = -c * gram
    e2 = -2.0 * eps * c * gram + c2 * second
    e3 = -3.0 * eps2 * c * gram + 3.0 * eps * c2 * second - c3 * third
    e4 = -4.0 * eps3 * c * gram + 6.0 * eps2 * c2 * second - 4.0 * eps * c3 * third + c2 * c2 * fourth
    u_m, u_n = 1.0 + eps + eps2 + eps3, e1 + e2 + e3
    w_m, w_n = 4.0 * eps3, eps2 * e1 + eps * e2 + e3
    a_m, a_n = u_m * w_m, u_m * w_n + w_m * u_n + dot(u_n.astype(jnp.bfloat16), w_n.astype(jnp.bfloat16))
    low4 = e4.astype(jnp.bfloat16)
    y_m = 1.0 + 2.0 * eps4 + 3.0 * eps4 * eps4
    y_n = (1.0 + 3.0 * eps4) * e4 + dot(low4, low4)
    q_m, q_n = a_m * y_m, a_m * y_n + y_m * a_n + dot(a_n.astype(jnp.bfloat16), y_n.astype(jnp.bfloat16))
    v = (1.0 + eps4) * (1.0 + eps4 * eps4)
    q_m = q_m + v * (1.0 + 2.0 * eps + 3.0 * eps2)
    q_n = q_n + v * ((1.0 + eps) * e1 + e2)
    q = ((q_m * eye + q_n) * (-c2 * (1.0 / tokens))).astype(jnp.bfloat16)
    p = c * (1.0 + eps) * (1.0 + eps2) * v
    stores = []
    for k, at in enumerate(range(0, rows, step)):
        some = pl.ds(at, step)
        mixed = dot(image[at : at + step, :], q).astype(jnp.bfloat16)
        for far, a, b in zip(fars, pieces[::2], pieces[1::2]):
            moved = dot(mixed, jnp.concatenate([a[...], b[...]], axis=1))
            for one in (0, 1):
                here = place(member, far + one, features)
                kept = p * tile[some, here].astype(jnp.float32)
                out[some, here] = (kept + moved[:, one * features : (one + 1) * features]).astype(jnp.bfloat16)
        store = pltpu.make_async_copy(out.at[some, :], out_hbm.at[some, :], sems.at[k])
        store.start()
        stores.append(store)
    for store in stores:
        store.wait()


def swap(value, axis, far):
    return lax.ppermute(value, axis, [(i, i ^ far) for i in range(lax.axis_size(axis))])


def by_tokens(factor_inputs, tile):
    members, replicas = lax.axis_size("grad"), lax.axis_size("dp")
    rows, width = tile.shape
    features = factor_inputs.shape[2]
    tokens = factor_inputs.shape[0] * replicas
    params = pltpu.CompilerParams(vmem_limit_bytes=24 * 2**20)

    def shape(*sizes, kind=jnp.float32):
        return jax.ShapeDtypeStruct(sizes, kind)

    parts = list(split_blocks(factor_inputs))
    arrived = [swap(parts[far], "dp", far) for far in range(replicas - 1, 0, -1)]
    own = jnp.concatenate(parts[:1] + arrived[::-1], axis=0)
    all_fars = [0] + list(range(members - 2, 0, -2))
    helds = [own] + [swap(own, "grad", far) for far in all_fars[1:]]
    pieces, turned, steps = [], [], [None]
    for count, held in enumerate(helds, 1):
        after = steps[min(count - 1, max(1, count - 2))]
        if after is None:
            near = swap(held, "grad", 1)
        else:
            near = swap(jnp.where(after[0, 0] >= 0.0, held, jnp.zeros_like(held)), "grad", 1)
        pieces += [held, near]
        fars = tuple(all_fars[:count])
        state = [
            shape(2 * features, tokens, kind=jnp.bfloat16),
            shape(tokens, tokens),
            shape(rows, tokens),
            shape(count, 2 * features),
        ]
        flops = 4 * features * tokens * (tokens + rows + 2 * features * (2 * count - 1))
        cost = pl.CostEstimate(flops=flops, bytes_accessed=0, transcendentals=0)
        if count == 1:
            one, *sums = pl.pallas_call(
                functools.partial(first_kernel, fars),
                out_shape=state,
                in_specs=[WHOLE] * 3,
                out_specs=[WHOLE] * 4,
                compiler_params=params,
                cost_estimate=cost,
                name="first_pair",
            )(*pieces, tile)
            turned.append(one)
        elif count < len(all_fars):
            one, *sums = pl.pallas_call(
                functools.partial(next_kernel, fars),
                out_shape=state,
                in_specs=[WHOLE] * (3 * count + 3),
                out_specs=[WHOLE] * 4,
                compiler_params=params,
                cost_estimate=cost,
                name="next_pair",
            )(*pieces, *turned, tile, *sums)
            turned.append(one)
        steps.append(sums[-1])
    return pl.pallas_call(
        functools.partial(last_kernel, fars),
        out_shape=shape(rows, width, kind=jnp.bfloat16),
        in_specs=[WHOLE] * (3 * count + 3),
        out_specs=ANYWHERE,
        scratch_shapes=[pltpu.VMEM((rows, width), jnp.bfloat16), pltpu.SemaphoreType.DMA((3,))],
        compiler_params=params,
        cost_estimate=pl.CostEstimate(flops=5 * 10**9, bytes_accessed=0, transcendentals=0),
        name="last_pair",
    )(*pieces, *turned, tile, *sums)


def local(factor_inputs, gradients):
    features, members = factor_inputs.shape[2], lax.axis_size("grad")
    tokens = factor_inputs.shape[0] * lax.axis_size("dp")
    tile = gradients[0]
    powers_of_two = all(size & (size - 1) == 0 for size in (members, lax.axis_size("dp")))
    if tokens < features * members and features % 128 == 0 and powers_of_two and members > 2:
        result = by_tokens(factor_inputs, tile)
    else:
        result = by_features(gather_block(factor_inputs), tile)
    return result.astype(jnp.bfloat16)[None]


def solution(mesh):
    placed = (P("dp", None, "grad"), P("dp", "grad", None))
    return jax.shard_map(
        local, mesh=mesh, in_specs=placed, out_specs=P("dp", "grad", None), check_vma=False
    )
```

```python
import functools

import jax
import jax.numpy as jnp
from jax import lax
from jax.experimental import pallas as pl
from jax.experimental.pallas import tpu as pltpu
from jax.sharding import PartitionSpec as P

ITERS = 4
DAMPING = 0.01
WHOLE = pl.BlockSpec(memory_space=pltpu.VMEM)
ANYWHERE = pl.BlockSpec(memory_space=pl.ANY)


def dot(a, b):
    return jnp.dot(a, b, preferred_element_type=jnp.float32)


def gather_block(factor_inputs):
    pieces = jnp.transpose(factor_inputs, (1, 0, 2))
    piece = lax.all_to_all(pieces, "dp", split_axis=0, concat_axis=1, tiled=True)[0]
    return lax.all_gather(piece, "grad", axis=1, tiled=True)


def by_features(columns, tile):
    tokens, width = columns.shape
    covariance = jnp.einsum("tr,tc->rc", columns, columns, preferred_element_type=jnp.float32) * (1.0 / tokens)
    damped = covariance + DAMPING * jnp.eye(width, dtype=jnp.float32)
    scale = 1.0 / jnp.max(jnp.sum(jnp.abs(damped), axis=1))
    image = scale * damped
    result = scale * tile.astype(jnp.float32)
    for step in range(ITERS):
        low = image.astype(jnp.bfloat16)
        result = 2.0 * result - dot(result.astype(jnp.bfloat16), low)
        if step < ITERS - 1:
            image = 2.0 * image - dot(low, low)
    return result


def split_kernel(x_ref, *out_refs):
    replicas, tokens = len(out_refs), out_refs[0].shape[0]
    here = lax.axis_index("dp")
    x = x_ref[...]
    rows = lax.broadcasted_iota(jnp.int32, (tokens, tokens * replicas), 0)
    cols = lax.broadcasted_iota(jnp.int32, (tokens, tokens * replicas), 1)
    offset = cols - rows * replicas
    for far, out_ref in enumerate(out_refs):
        choice = jnp.where(offset == lax.rem(here + far, replicas), 1.0, 0.0).astype(jnp.bfloat16)
        out_ref[...] = dot(choice, x).astype(jnp.bfloat16)


def split_blocks(factor_inputs):
    tokens, blocks, features = factor_inputs.shape
    return pl.pallas_call(
        split_kernel,
        out_shape=[jax.ShapeDtypeStruct((tokens, features), factor_inputs.dtype)] * blocks,
        in_specs=[WHOLE],
        out_specs=[WHOLE] * blocks,
        name="split_blocks",
    )(factor_inputs.reshape(tokens * blocks, features))


def place(member, far, features):
    return pl.ds(pl.multiple_of((member ^ far) * features, features), features)


def join(pieces):
    return [jnp.concatenate([a[...], b[...]], axis=1) for a, b in zip(pieces[::2], pieces[1::2])]


def column_sums(a, b):
    return jnp.sum(jnp.abs(dot(a, b)), axis=0, keepdims=True)


def absorb(fars, pairs, turned, tile, member):
    columns = pairs[-1]
    columns_t = columns.T
    features = columns.shape[1] // 2
    gram = dot(columns, columns_t)
    mine = jnp.concatenate([tile[:, place(member, fars[-1] + one, features)] for one in (0, 1)], axis=1)
    image = dot(mine, columns_t)
    sums = column_sums(columns_t, columns)
    before = []
    for earlier, earlier_t in zip(pairs, turned):
        sums = sums + column_sums(earlier_t[...], columns)
        before.append(column_sums(columns_t, earlier))
    return columns_t, gram, image, before + [sums]


def first_kernel(fars, p0, p1, tile, turned, gram_out, image_out, sums_out, zeros):
    turned[...], gram_out[...], image_out[...], sums = absorb(
        fars, join((p0, p1)), (), tile, lax.axis_index("grad")
    )
    sums_out[...] = sums[0]
    zeros[...] = jnp.zeros_like(zeros)


def take(fars, refs):
    count = 2 * len(fars)
    return refs[:count], refs[count:]


def next_kernel(fars, *refs):
    pieces, refs = take(fars, refs)
    done = len(fars) - 1
    earlier, (tile, gram_in, image_in, sums_in, turned, gram_out, image_out, sums_out, zeros) = refs[:done], refs[done:]
    turned[...], gram, image, sums = absorb(fars, join(pieces), earlier, tile, lax.axis_index("grad"))
    gram_out[...] = gram_in[...] + gram
    image_out[...] = image_in[...] + image
    for k in range(done):
        sums_out[k : k + 1, :] = sums_in[k : k + 1, :] + sums[k]
    sums_out[done:, :] = sums[done]
    zeros[...] = jnp.zeros_like(zeros)


def last_kernel(fars, *refs):
    pieces, refs = take(fars, refs)
    done = len(fars) - 2
    earlier, refs = refs[:done], refs[done:]
    tile, gram_in, image_in, sums_in, out_hbm, out, k1, k2, k3, k4, low1, low2, u, w, e4, image, mixed, sems = refs
    member = lax.axis_index("grad")
    tokens, features = pieces[0].shape
    rows = tile.shape[0]
    chunk = 16
    half = 2 * features
    halves = range(0, tokens, half)
    pairs = join(pieces)
    columns_t, gram, moved, sums = absorb(fars[:-1], pairs[:-1], earlier, tile, member)
    sums = [sums_in[k : k + 1, :] + sums[k] for k in range(done)] + [sums[done]]
    _, gram2, moved2, sums2 = absorb(fars, pairs, list(earlier) + [columns_t], tile, member)
    k1[...] = (gram_in[...] + gram + gram2) * (1.0 / tokens)
    low1[...] = k1[...].astype(jnp.bfloat16)
    image[...] = (image_in[...] + moved + moved2).astype(jnp.bfloat16)
    sums = [a + b for a, b in zip(sums, sums2)] + [sums2[-1]]
    largest = functools.reduce(jnp.maximum, sums)
    for at in halves:
        product = dot(low1[...], low1[:, at : at + half])
        k2[:, at : at + half] = product
        low2[:, at : at + half] = product.astype(jnp.bfloat16)
    for at in halves:
        k3[:, at : at + half] = dot(low2[...], low1[:, at : at + half])
        k4[:, at : at + half] = dot(low2[...], low2[:, at : at + half])

    c = 1.0 / (jnp.max(largest) * (1.0 / tokens) + DAMPING)
    eps = 1.0 - c * DAMPING
    eps2 = eps * eps
    eps3 = eps2 * eps
    eps4 = eps2 * eps2
    c2 = c * c
    c3 = c2 * c
    e1_ = (-c, 0.0, 0.0)
    e2_ = (-2.0 * eps * c, c2, 0.0)
    e3_ = (-3.0 * eps2 * c, 3.0 * eps * c2, -c3)
    e4_ = (-4.0 * eps3 * c, 6.0 * eps2 * c2, -4.0 * eps * c3, c2 * c2)
    u_m, u_ = 1.0 + eps + eps2 + eps3, [x + y + z for x, y, z in zip(e1_, e2_, e3_)]
    w_m, w_ = 4.0 * eps3, [eps2 * x + eps * y + z for x, y, z in zip(e1_, e2_, e3_)]
    a_m, a_ = u_m * w_m, [u_m * x + w_m * y for x, y in zip(w_, u_)]
    y_m, y_e = 1.0 + 2.0 * eps4 + 3.0 * eps4 * eps4, 1.0 + 3.0 * eps4
    v = (1.0 + eps4) * (1.0 + eps4 * eps4)
    q_m = a_m * y_m + v * (1.0 + 2.0 * eps + 3.0 * eps2)
    q_ = (v * (1.0 + eps) * e1_[0] + v * e2_[0], v * e2_[1])
    last = -c2 * (1.0 / tokens)
    p = c * (1.0 + eps) * (1.0 + eps2) * v

    def each_chunk(body):
        def step(i, carry):
            body(pl.ds(pl.multiple_of(i * chunk, chunk), chunk))
            return carry

        lax.fori_loop(0, tokens // chunk, step, 0, unroll=4)

    def mix(weights, some, *powers):
        return functools.reduce(jnp.add, [weight * power[some, :] for weight, power in zip(weights, powers)])

    def first(some):
        x1, x2, x3 = k1[some, :], k2[some, :], k3[some, :]
        u[some, :] = (u_[0] * x1 + u_[1] * x2 + u_[2] * x3).astype(jnp.bfloat16)
        w[some, :] = (w_[0] * x1 + w_[1] * x2 + w_[2] * x3).astype(jnp.bfloat16)
        e4[some, :] = (e4_[0] * x1 + e4_[1] * x2 + e4_[2] * x3 + e4_[3] * k4[some, :]).astype(jnp.bfloat16)

    each_chunk(first)
    for at in halves:
        k4[:, at : at + half] = dot(e4[...], e4[:, at : at + half])
    a_dot = [dot(u[...], w[:, at : at + half]) for at in halves]

    def second(some):
        y = k4[some, :] + y_e * e4[some, :].astype(jnp.float32)
        k4[some, :] = y
        low2[some, :] = y.astype(jnp.bfloat16)

    each_chunk(second)
    for at, product in zip(halves, a_dot):
        k3[:, at : at + half] = a_[2] * k3[:, at : at + half] + product

    def third(some):
        x1, x2 = k1[some, :], k2[some, :]
        a = k3[some, :] + a_[0] * x1 + a_[1] * x2
        k3[some, :] = a * y_m + a_m * k4[some, :] + q_[0] * x1 + q_[1] * x2
        low1[some, :] = a.astype(jnp.bfloat16)

    each_chunk(third)
    for at in halves:
        u[:, at : at + half] = ((k3[:, at : at + half] + dot(low1[...], low2[:, at : at + half])) * last).astype(jnp.bfloat16)
    q_m = q_m * last
    for at in halves:
        product = dot(image[...], u[:, at : at + half])
        mixed[:, at : at + half] = (product + q_m * image[:, at : at + half].astype(jnp.float32)).astype(jnp.bfloat16)
    stores = []
    for far, columns in zip(fars, pairs):
        moved = dot(mixed[...], columns)
        for one in (0, 1):
            here = place(member, far + one, features)
            kept = p * tile[:, here].astype(jnp.float32)
            out[:, here] = (kept + moved[:, one * features : (one + 1) * features]).astype(jnp.bfloat16)
            store = pltpu.make_async_copy(out.at[:, here], out_hbm.at[:, here], sems.at[len(stores)])
            store.start()
            stores.append(store)
    for store in stores:
        store.wait()


def swap(value, far):
    return lax.ppermute(value, "grad", [(i, i ^ far) for i in range(lax.axis_size("grad"))])


def by_tokens(factor_inputs, tile):
    members, replicas = lax.axis_size("grad"), lax.axis_size("dp")
    rows, width = tile.shape
    features = factor_inputs.shape[2]
    tokens = factor_inputs.shape[0] * replicas
    params = pltpu.CompilerParams(vmem_limit_bytes=24 * 2**20)

    def shape(*sizes, kind=jnp.float32):
        return jax.ShapeDtypeStruct(sizes, kind)

    def scratch(*sizes, kind=jnp.bfloat16):
        return pltpu.VMEM(sizes, kind)

    parts = list(split_blocks(factor_inputs))
    for far in range(1, replicas):
        parts[far] = lax.ppermute(parts[far], "dp", [(i, (i + far) % replicas) for i in range(replicas)])
    own = jnp.concatenate(parts, axis=0)
    all_fars = tuple(range(0, members, 2))
    helds = [own] + [swap(own, far) for far in all_fars[1:]]
    pieces, turned, sums, zeros = [], [], [], None
    for count, held in enumerate(helds, 1):
        pieces += [held, swap(held if zeros is None else held + zeros, 1)]
        if count > len(helds) - 2:
            continue
        fars = all_fars[:count]
        one, *sums, new_zeros = pl.pallas_call(
            functools.partial(first_kernel if count == 1 else next_kernel, fars),
            out_shape=[
                shape(2 * features, tokens, kind=jnp.bfloat16),
                shape(tokens, tokens),
                shape(rows, tokens),
                shape(count, 2 * features),
                shape(1, features, kind=jnp.bfloat16),
            ],
            in_specs=[WHOLE] * (3 * count + (0 if count == 1 else 3)),
            out_specs=[WHOLE] * 5,
            compiler_params=params,
            cost_estimate=pl.CostEstimate(
                flops=4 * features * tokens * (tokens + rows + 2 * features * (2 * count - 1)),
                bytes_accessed=0,
                transcendentals=0,
            ),
            name="add_pair",
        )(*pieces, *turned, tile, *sums)
        turned.append(one)
        zeros = new_zeros if zeros is None else zeros
    return pl.pallas_call(
        functools.partial(last_kernel, all_fars),
        out_shape=shape(rows, width, kind=jnp.bfloat16),
        in_specs=[WHOLE] * (len(pieces) + len(turned) + 1 + len(sums)),
        out_specs=ANYWHERE,
        scratch_shapes=[scratch(rows, width)]
        + [scratch(tokens, tokens, kind=jnp.float32)] * 4
        + [scratch(tokens, tokens)] * 5
        + [scratch(rows, tokens)] * 2
        + [pltpu.SemaphoreType.DMA((members,))],
        compiler_params=params,
        cost_estimate=pl.CostEstimate(flops=5 * 10**9, bytes_accessed=0, transcendentals=0),
        name="last_pairs",
    )(*pieces, *turned, tile, *sums)


def local(factor_inputs, gradients):
    features, members = factor_inputs.shape[2], lax.axis_size("grad")
    tokens = factor_inputs.shape[0] * lax.axis_size("dp")
    tile = gradients[0]
    powers_of_two = all(size & (size - 1) == 0 for size in (members, lax.axis_size("dp")))
    if tokens < features * members and features % 128 == 0 and powers_of_two and members > 2:
        result = by_tokens(factor_inputs, tile)
    else:
        result = by_features(gather_block(factor_inputs), tile)
    return result.astype(jnp.bfloat16)[None]


def solution(mesh):
    placed = (P("dp", None, "grad"), P("dp", "grad", None))
    return jax.shard_map(
        local, mesh=mesh, in_specs=placed, out_specs=P("dp", "grad", None), check_vma=False
    )
```

```python
import functools

import jax
import jax.numpy as jnp
from jax import lax
from jax.experimental import pallas as pl
from jax.experimental.pallas import tpu as pltpu
from jax.sharding import PartitionSpec as P

ITERS = 4
DAMPING = 0.01
WHOLE = pl.BlockSpec(memory_space=pltpu.VMEM)
ANYWHERE = pl.BlockSpec(memory_space=pl.ANY)


def dot(a, b):
    return jnp.dot(a, b, preferred_element_type=jnp.float32)


def gather_block(factor_inputs):
    pieces = jnp.transpose(factor_inputs, (1, 0, 2))
    piece = lax.all_to_all(pieces, "dp", split_axis=0, concat_axis=1, tiled=True)[0]
    return lax.all_gather(piece, "grad", axis=1, tiled=True)


def by_features(columns, tile):
    tokens, width = columns.shape
    covariance = jnp.einsum("tr,tc->rc", columns, columns, preferred_element_type=jnp.float32) * (1.0 / tokens)
    damped = covariance + DAMPING * jnp.eye(width, dtype=jnp.float32)
    scale = 1.0 / jnp.max(jnp.sum(jnp.abs(damped), axis=1))
    image = scale * damped
    result = scale * tile.astype(jnp.float32)
    for step in range(ITERS):
        low = image.astype(jnp.bfloat16)
        result = 2.0 * result - dot(result.astype(jnp.bfloat16), low)
        if step < ITERS - 1:
            image = 2.0 * image - dot(low, low)
    return result


def split_kernel(x_ref, tile_hbm, *refs):
    *out_refs, tile, sem = refs
    load = pltpu.make_async_copy(tile_hbm, tile, sem)
    load.start()
    replicas, tokens = len(out_refs), out_refs[0].shape[0]
    here = lax.axis_index("dp")
    x = x_ref[...]
    rows = lax.broadcasted_iota(jnp.int32, (tokens, tokens * replicas), 0)
    cols = lax.broadcasted_iota(jnp.int32, (tokens, tokens * replicas), 1)
    offset = cols - rows * replicas
    for far, out_ref in enumerate(out_refs):
        choice = jnp.where(offset == lax.rem(here + far, replicas), 1.0, 0.0).astype(jnp.bfloat16)
        out_ref[...] = dot(choice, x).astype(jnp.bfloat16)
    load.wait()


def split_blocks(factor_inputs, tile):
    tokens, blocks, features = factor_inputs.shape
    return pl.pallas_call(
        split_kernel,
        out_shape=[jax.ShapeDtypeStruct((tokens, features), factor_inputs.dtype)] * blocks
        + [jax.ShapeDtypeStruct(tile.shape, tile.dtype)],
        in_specs=[WHOLE, ANYWHERE],
        out_specs=[WHOLE] * (blocks + 1),
        scratch_shapes=[pltpu.SemaphoreType.DMA],
        compiler_params=pltpu.CompilerParams(vmem_limit_bytes=52 * 2**20),
        name="split_blocks",
    )(factor_inputs.reshape(tokens * blocks, features), tile)


def place(member, far, features):
    return pl.ds(pl.multiple_of((member ^ far) * features, features), features)


def chosen(tile, member, fars, features):
    return jnp.concatenate([tile[:, place(member, far, features)] for far in fars], axis=1)


def magnitudes(a, b):
    return jnp.abs(dot(a, b))


def first_kernel(own, near, tile, turned, gram, image, sums, zeros):
    member = lax.axis_index("grad")
    features = own.shape[1]
    columns = jnp.concatenate([own[...], near[...]], axis=1)
    turned[...] = columns.T
    gram[...] = dot(columns, turned[...])
    image[...] = dot(chosen(tile, member, (0, 1), features), turned[...])
    sums[...] = jnp.sum(magnitudes(turned[...], columns), axis=0, keepdims=True)
    zeros[...] = jnp.zeros_like(zeros)


def last_kernel(fars, *refs):
    count = len(fars)
    pieces, refs = refs[: 2 * count + 2], refs[2 * count + 2 :]
    turned, tile, gram_in, image_in, sums_in, out_hbm, *refs = refs
    out, x, xt, k1, k2, k3, k4, low1, low2, g, h, z, image, mixed, sems = refs
    member = lax.axis_index("grad")
    tokens, features = pieces[0].shape
    half = 2 * features
    halves = [slice(at, at + half) for at in range(0, tokens, half)]
    blocks = [slice(at, at + half) for at in range(0, x.shape[1], half)]
    chunks = [slice(at, at + 32) for at in range(0, tokens, 32)]
    all_fars = [far + one for far in (0,) + fars for one in (0, 1)]

    xt[:half, :] = turned[...]
    for k, piece in enumerate(pieces):
        some = slice(k * features, (k + 1) * features)
        x[:, some] = piece[...]
        if k > 1:
            xt[some, :] = piece[...].T
    for some in halves:
        gram = (gram_in[:, some] + dot(x[:, half:], xt[half:, some])) * (1.0 / tokens)
        k1[:, some] = gram
        low1[:, some] = gram.astype(jnp.bfloat16)

    column_sums = [sums_in[...]] + [0.0] * count
    row_sums = [0.0] * (count + 1)
    for j in range(1, count + 1):
        for i in range(j + 1):
            block = magnitudes(xt[blocks[i], :], x[:, blocks[j]])
            column_sums[j] = column_sums[j] + jnp.sum(block, axis=0, keepdims=True)
            if i < j:
                row_sums[i] = row_sums[i] + block[:, :features] + block[:, features:]
    largest = column_sums[count]
    for i in range(count):
        largest = jnp.maximum(largest, column_sums[i] + jnp.sum(row_sums[i].T, axis=0, keepdims=True))
    c = 1.0 / (jnp.max(largest) * (1.0 / tokens) + DAMPING)

    eps = 1.0 - c * DAMPING
    eps2 = eps * eps
    zeta = eps2 * eps2
    eps8 = zeta * zeta
    e2_1, e2_2 = -2.0 * eps * c, c * c
    g_1 = -(1.0 + eps) * c
    g_m = eps2 + (1.0 + eps) * eps + eps
    h_m = zeta + (1.0 + eps2) * eps2 + eps2
    k_m = eps8 + (1.0 + zeta) * zeta + zeta + 1.0 + eps8
    k_z = 1.0 + 3.0 * zeta
    a_m = g_m * h_m
    a_e2 = g_m * (1.0 + eps2) + h_m
    a_1 = h_m * g_1
    beta = (1.0 + zeta) * (1.0 + eps8)
    q_m = a_m * k_m + beta * g_m + (1.0 + eps2) * beta
    last = -c * c * (1.0 / tokens)
    p = c * (1.0 + eps) * (1.0 + eps2) * beta

    def move(some):
        product = dot(chosen(tile, member, all_fars[2:], features), xt[half:, some])
        image[:, some] = (image_in[:, some] + product).astype(jnp.bfloat16)

    for some in halves:
        product = dot(low1[...], low1[:, some])
        for r in chunks:
            x1 = k1[r, some]
            e2 = e2_1 * x1 + e2_2 * product[r]
            k2[r, some] = e2
            low2[r, some] = e2.astype(jnp.bfloat16)
            g[r, some] = (e2 + g_1 * x1).astype(jnp.bfloat16)
    move(halves[0])
    for some in halves:
        product = dot(low2[...], low2[:, some])
        for r in chunks:
            e2 = k2[r, some]
            fourth = 2.0 * eps2 * e2 + product[r]
            k3[r, some] = fourth
            z[r, some] = fourth.astype(jnp.bfloat16)
            h[r, some] = (fourth + (1.0 + eps2) * e2).astype(jnp.bfloat16)
    for some in halves[1:]:
        move(some)
    for some in halves:
        product = dot(z[...], z[:, some])
        for r in chunks:
            k = product[r] + k_z * k3[r, some]
            k4[r, some] = k
            low2[r, some] = k.astype(jnp.bfloat16)
    for some in halves:
        product = dot(g[...], h[:, some])
        for r in chunks:
            x1, e2 = k1[r, some], k2[r, some]
            a = product[r] + g_m * k3[r, some] + a_e2 * e2 + a_1 * x1
            low1[r, some] = a.astype(jnp.bfloat16)
            k4[r, some] = last * (a_m * k4[r, some] + k_m * a + beta * (e2 + g_1 * x1))
    for some in halves:
        product = dot(low1[...], low2[:, some])
        for r in chunks:
            g[r, some] = (k4[r, some] + last * product[r]).astype(jnp.bfloat16)
    q_m = q_m * last
    for some in halves:
        product = dot(image[...], g[:, some])
        mixed[:, some] = (product + q_m * image[:, some].astype(jnp.float32)).astype(jnp.bfloat16)
    stores = []
    for k, some in enumerate(blocks):
        moved = dot(mixed[...], x[:, some])
        for one in (0, 1):
            here = place(member, all_fars[2 * k + one], features)
            kept = p * tile[:, here].astype(jnp.float32)
            out[:, here] = (kept + moved[:, one * features : (one + 1) * features]).astype(jnp.bfloat16)
            store = pltpu.make_async_copy(out.at[:, here], out_hbm.at[:, here], sems.at[len(stores)])
            store.start()
            stores.append(store)
    for store in stores:
        store.wait()


def swap(value, far):
    return lax.ppermute(value, "grad", [(i, i ^ far) for i in range(lax.axis_size("grad"))])


def by_tokens(factor_inputs, tile):
    members, replicas = lax.axis_size("grad"), lax.axis_size("dp")
    rows, width = tile.shape
    features = factor_inputs.shape[2]
    tokens = factor_inputs.shape[0] * replicas
    params = pltpu.CompilerParams(vmem_limit_bytes=24 * 2**20)

    def shape(*sizes, kind=jnp.float32):
        return jax.ShapeDtypeStruct(sizes, kind)

    def scratch(*sizes, kind=jnp.bfloat16):
        return pltpu.VMEM(sizes, kind)

    *parts, tile = split_blocks(factor_inputs, tile)
    arrived = [
        lax.ppermute(parts[far], "dp", [(i, (i + far) % replicas) for i in range(replicas)])
        for far in range(1, replicas)
    ]
    fars = tuple(range(2, members, 2))
    own = jnp.concatenate([parts[0]] + arrived, axis=0)
    near = swap(own, 1)
    held = [swap(own, far) for far in fars]
    *state, zeros = pl.pallas_call(
        first_kernel,
        out_shape=[
            shape(2 * features, tokens, kind=jnp.bfloat16),
            shape(tokens, tokens),
            shape(rows, tokens),
            shape(1, 2 * features),
            shape(1, features, kind=jnp.bfloat16),
        ],
        in_specs=[WHOLE] * 3,
        out_specs=[WHOLE] * 5,
        compiler_params=params,
        cost_estimate=pl.CostEstimate(flops=4 * 10**8, bytes_accessed=0, transcendentals=0),
        name="first_pair",
    )(own, near, tile)
    pieces = [own, near]
    for k, piece in enumerate(held):
        pieces += [piece, swap(piece if k else piece + zeros, 1)]
    inputs = [*pieces, state[0], tile, *state[1:]]
    return pl.pallas_call(
        functools.partial(last_kernel, fars),
        out_shape=shape(rows, width, kind=jnp.bfloat16),
        in_specs=[WHOLE] * len(inputs),
        out_specs=ANYWHERE,
        scratch_shapes=[scratch(rows, width), scratch(tokens, width), scratch(width, tokens)]
        + [scratch(tokens, tokens, kind=jnp.float32)] * 4
        + [scratch(tokens, tokens)] * 5
        + [scratch(rows, tokens)] * 2
        + [pltpu.SemaphoreType.DMA((members,))],
        compiler_params=params,
        cost_estimate=pl.CostEstimate(flops=5 * 10**9, bytes_accessed=0, transcendentals=0),
        name="last_pairs",
    )(*inputs)


def local(factor_inputs, gradients):
    features, members = factor_inputs.shape[2], lax.axis_size("grad")
    tokens = factor_inputs.shape[0] * lax.axis_size("dp")
    tile = gradients[0]
    powers_of_two = all(size & (size - 1) == 0 for size in (members, lax.axis_size("dp")))
    if tokens < features * members and features % 128 == 0 and powers_of_two and members > 2:
        result = by_tokens(factor_inputs, tile)
    else:
        result = by_features(gather_block(factor_inputs), tile)
    return result.astype(jnp.bfloat16)[None]


def solution(mesh):
    placed = (P("dp", None, "grad"), P("dp", "grad", None))
    return jax.shard_map(
        local, mesh=mesh, in_specs=placed, out_specs=P("dp", "grad", None), check_vma=False
    )
```

```python
import functools

import jax
import jax.numpy as jnp
from jax import lax
from jax.experimental import pallas as pl
from jax.experimental.pallas import tpu as pltpu
from jax.sharding import PartitionSpec as P

ITERS = 4
DAMPING = 0.01
WHOLE = pl.BlockSpec(memory_space=pltpu.VMEM)
ANYWHERE = pl.BlockSpec(memory_space=pl.ANY)


def dot(a, b):
    return jnp.dot(a, b, preferred_element_type=jnp.float32)


def gather_block(factor_inputs):
    pieces = jnp.transpose(factor_inputs, (1, 0, 2))
    piece = lax.all_to_all(pieces, "dp", split_axis=0, concat_axis=1, tiled=True)[0]
    return lax.all_gather(piece, "grad", axis=1, tiled=True)


def by_features(columns, tile):
    tokens, width = columns.shape
    covariance = jnp.einsum("tr,tc->rc", columns, columns, preferred_element_type=jnp.float32) * (1.0 / tokens)
    damped = covariance + DAMPING * jnp.eye(width, dtype=jnp.float32)
    scale = 1.0 / jnp.max(jnp.sum(jnp.abs(damped), axis=1))
    image = scale * damped
    result = scale * tile.astype(jnp.float32)
    for step in range(ITERS):
        low = image.astype(jnp.bfloat16)
        result = 2.0 * result - dot(result.astype(jnp.bfloat16), low)
        if step < ITERS - 1:
            image = 2.0 * image - dot(low, low)
    return result


def split_kernel(x_ref, *out_refs):
    replicas, tokens = len(out_refs), out_refs[0].shape[0]
    here = lax.axis_index("dp")
    x = x_ref[...]
    rows = lax.broadcasted_iota(jnp.int32, (tokens, tokens * replicas), 0)
    cols = lax.broadcasted_iota(jnp.int32, (tokens, tokens * replicas), 1)
    offset = cols - rows * replicas
    for far, out_ref in enumerate(out_refs):
        choice = jnp.where(offset == lax.rem(here + far, replicas), 1.0, 0.0).astype(jnp.bfloat16)
        out_ref[...] = dot(choice, x).astype(jnp.bfloat16)


def split_blocks(factor_inputs):
    tokens, blocks, features = factor_inputs.shape
    return pl.pallas_call(
        split_kernel,
        out_shape=[jax.ShapeDtypeStruct((tokens, features), factor_inputs.dtype)] * blocks,
        in_specs=[WHOLE],
        out_specs=[WHOLE] * blocks,
        compiler_params=pltpu.CompilerParams(vmem_limit_bytes=16 * 2**20),
        name="split_blocks",
    )(factor_inputs.reshape(tokens * blocks, features))


def first_kernel(*refs):
    *pieces, turned, gram = refs
    features = pieces[0].shape[1]
    for k, piece in enumerate(pieces):
        turned[k * features : (k + 1) * features, :] = piece[...].T
    gram[...] = dot(jnp.concatenate([piece[...] for piece in pieces], axis=1), turned[...])


def last_kernel(fars, count, *refs):
    pieces, refs = refs[: len(fars)], refs[len(fars) :]
    turned, gram_in, tile_hbm, out_hbm, *refs = refs
    tile, out, x, xt, k1, k2, k3, k4, low1, low2, g, h, z, image, mixed, sems = refs
    load = pltpu.make_async_copy(tile_hbm, tile, sems.at[0])
    load.start()
    member = lax.axis_index("grad")
    tokens, features = pieces[0].shape
    half = 2 * features
    halves = [slice(at, at + half) for at in range(0, tokens, half)]
    blocks = [slice(at, at + half) for at in range(0, x.shape[1], half)]
    chunks = [slice(at, at + 32) for at in range(0, tokens, 32)]

    rest = []
    for k, (far, piece) in enumerate(zip(fars, pieces)):
        here = pl.ds(pl.multiple_of((member ^ far) * features, features), features)
        x[:, here] = piece[...]
        if k < count:
            xt[here, :] = turned[k * features : (k + 1) * features, :]
        else:
            rest.append(piece[...].T)
            xt[here, :] = rest[-1]
    late = jnp.concatenate([piece[...] for piece in pieces[count:]], axis=1)
    late_t = jnp.concatenate(rest, axis=0)
    for some in halves:
        gram = (gram_in[:, some] + dot(late, late_t[:, some])) * (1.0 / tokens)
        k1[:, some] = gram
        low1[:, some] = gram.astype(jnp.bfloat16)

    column_sums, row_sums = [0.0] * len(blocks), [0.0] * len(blocks)

    def add_sums(j):
        for i in range(j + 1):
            block = jnp.abs(dot(xt[blocks[i], :], x[:, blocks[j]]))
            column_sums[j] = column_sums[j] + jnp.sum(block, axis=0, keepdims=True)
            if i < j:
                row_sums[i] = row_sums[i] + block[:, :features] + block[:, features:]

    def move(some):
        image[:, some] = dot(tile[...], xt[:, some]).astype(jnp.bfloat16)

    for j in range(len(blocks) - 1):
        add_sums(j)
    for some in halves:
        k2[:, some] = dot(low1[...], low1[:, some])
    add_sums(len(blocks) - 1)
    load.wait()
    move(halves[0])

    largest = column_sums[-1]
    for column, row in zip(column_sums[:-1], row_sums):
        largest = jnp.maximum(largest, column + jnp.sum(row.T, axis=0, keepdims=True))
    c = 1.0 / (jnp.max(largest) * (1.0 / tokens) + DAMPING)
    eps = 1.0 - c * DAMPING
    eps2 = eps * eps
    zeta = eps2 * eps2
    eps8 = zeta * zeta
    e2_1, e2_2 = -2.0 * eps * c, c * c
    g_1 = -(1.0 + eps) * c
    g_m = eps2 + (1.0 + eps) * eps + eps
    h_m = zeta + (1.0 + eps2) * eps2 + eps2
    k_m = eps8 + (1.0 + zeta) * zeta + zeta + 1.0 + eps8
    k_z = 1.0 + 3.0 * zeta
    a_m = g_m * h_m
    a_e2 = g_m * (1.0 + eps2) + h_m
    a_1 = h_m * g_1
    beta = (1.0 + zeta) * (1.0 + eps8)
    q_m = a_m * k_m + beta * g_m + (1.0 + eps2) * beta
    last = -c * c * (1.0 / tokens)
    q_m = q_m * last
    p = c * (1.0 + eps) * (1.0 + eps2) * beta

    for some in halves:
        for r in chunks:
            x1 = k1[r, some]
            e2 = e2_1 * x1 + e2_2 * k2[r, some]
            k2[r, some] = e2
            low2[r, some] = e2.astype(jnp.bfloat16)
            g[r, some] = (e2 + g_1 * x1).astype(jnp.bfloat16)
    for some in halves:
        product = dot(low2[...], low2[:, some])
        for r in chunks:
            e2 = k2[r, some]
            fourth = 2.0 * eps2 * e2 + product[r]
            k3[r, some] = fourth
            z[r, some] = fourth.astype(jnp.bfloat16)
            h[r, some] = (fourth + (1.0 + eps2) * e2).astype(jnp.bfloat16)
    for some in halves[1:]:
        move(some)

    def add_a(some):
        product = dot(g[...], h[:, some])
        for r in chunks:
            x1, e2 = k1[r, some], k2[r, some]
            a = product[r] + g_m * k3[r, some] + a_e2 * e2 + a_1 * x1
            low1[r, some] = a.astype(jnp.bfloat16)
            k1[r, some] = last * (k_m * a + beta * (e2 + g_1 * x1))

    add_a(halves[0])
    for some in halves:
        product = dot(z[...], z[:, some])
        for r in chunks:
            k = product[r] + k_z * k3[r, some]
            k4[r, some] = k
            low2[r, some] = k.astype(jnp.bfloat16)
    for some in halves[1:]:
        add_a(some)
    for some in halves:
        product = dot(low2[...], low1[:, some])
        for r in chunks:
            g[r, some] = (k1[r, some] + last * (product[r] + a_m * k4[r, some])).astype(jnp.bfloat16)
    for some in halves:
        product = dot(image[...], g[:, some])
        mixed[:, some] = (product + q_m * image[:, some].astype(jnp.float32)).astype(jnp.bfloat16)
    stores = []
    for k, some in enumerate(blocks):
        moved = dot(mixed[...], x[:, some])
        out[:, some] = (p * tile[:, some].astype(jnp.float32) + moved).astype(jnp.bfloat16)
        store = pltpu.make_async_copy(out.at[:, some], out_hbm.at[:, some], sems.at[1 + k])
        store.start()
        stores.append(store)
    for store in stores:
        store.wait()


def swap(value, far):
    return lax.ppermute(value, "grad", [(i, i ^ far) for i in range(lax.axis_size("grad"))])


def by_tokens(factor_inputs, tile):
    members, replicas = lax.axis_size("grad"), lax.axis_size("dp")
    rows, width = tile.shape
    features = factor_inputs.shape[2]
    tokens = factor_inputs.shape[0] * replicas

    def shape(*sizes, kind=jnp.float32):
        return jax.ShapeDtypeStruct(sizes, kind)

    def scratch(*sizes, kind=jnp.bfloat16):
        return pltpu.VMEM(sizes, kind)

    parts = split_blocks(factor_inputs)
    arrived = [
        lax.ppermute(parts[far], "dp", [(i, (i + far) % replicas) for i in range(replicas)])
        for far in range(1, replicas)
    ]
    fars = tuple(range(2, members, 2))
    own = jnp.concatenate([parts[0]] + arrived, axis=0)
    near = swap(own, 1)
    held = [swap(own, far) for far in fars]
    far_near = [swap(piece, 1) for piece in held]
    here, there = [own, near, *held], far_near
    turned, gram = pl.pallas_call(
        first_kernel,
        out_shape=[shape(len(here) * features, tokens, kind=jnp.bfloat16), shape(tokens, tokens)],
        in_specs=[WHOLE] * len(here),
        out_specs=[WHOLE] * 2,
        compiler_params=pltpu.CompilerParams(vmem_limit_bytes=16 * 2**20),
        cost_estimate=pl.CostEstimate(flops=4 * 10**8, bytes_accessed=0, transcendentals=0),
        name="first_pieces",
    )(*here)
    return pl.pallas_call(
        functools.partial(last_kernel, (0, 1, *fars, *[far + 1 for far in fars]), len(here)),
        out_shape=shape(rows, width, kind=jnp.bfloat16),
        in_specs=[WHOLE] * (members + 2) + [ANYWHERE],
        out_specs=ANYWHERE,
        scratch_shapes=[scratch(rows, width)] * 2
        + [scratch(tokens, width), scratch(width, tokens)]
        + [scratch(tokens, tokens, kind=jnp.float32)] * 4
        + [scratch(tokens, tokens)] * 5
        + [scratch(rows, tokens)] * 2
        + [pltpu.SemaphoreType.DMA((1 + members // 2,))],
        compiler_params=pltpu.CompilerParams(vmem_limit_bytes=51 * 2**20),
        cost_estimate=pl.CostEstimate(flops=5 * 10**9, bytes_accessed=0, transcendentals=0),
        name="whole_block",
    )(*here, *there, turned, gram, tile)


def local(factor_inputs, gradients):
    features, members = factor_inputs.shape[2], lax.axis_size("grad")
    tokens = factor_inputs.shape[0] * lax.axis_size("dp")
    tile = gradients[0]
    powers_of_two = all(size & (size - 1) == 0 for size in (members, lax.axis_size("dp")))
    if tokens < features * members and features % 128 == 0 and powers_of_two and members > 2:
        result = by_tokens(factor_inputs, tile)
    else:
        result = by_features(gather_block(factor_inputs), tile)
    return result.astype(jnp.bfloat16)[None]


def solution(mesh):
    placed = (P("dp", None, "grad"), P("dp", "grad", None))
    return jax.shard_map(
        local, mesh=mesh, in_specs=placed, out_specs=P("dp", "grad", None), check_vma=False
    )
```

```python
import functools

import jax
import jax.numpy as jnp
from jax import lax
from jax.experimental import pallas as pl
from jax.experimental.pallas import tpu as pltpu
from jax.sharding import PartitionSpec as P

ITERS = 4
DAMPING = 0.01
WHOLE = pl.BlockSpec(memory_space=pltpu.VMEM)
ANYWHERE = pl.BlockSpec(memory_space=pl.ANY)


def dot(a, b):
    return jnp.dot(a, b, preferred_element_type=jnp.float32)


def gather_block(factor_inputs):
    pieces = jnp.transpose(factor_inputs, (1, 0, 2))
    piece = lax.all_to_all(pieces, "dp", split_axis=0, concat_axis=1, tiled=True)[0]
    return lax.all_gather(piece, "grad", axis=1, tiled=True)


def by_features(columns, tile):
    tokens, width = columns.shape
    covariance = jnp.einsum("tr,tc->rc", columns, columns, preferred_element_type=jnp.float32) * (1.0 / tokens)
    damped = covariance + DAMPING * jnp.eye(width, dtype=jnp.float32)
    scale = 1.0 / jnp.max(jnp.sum(jnp.abs(damped), axis=1))
    image = scale * damped
    result = scale * tile.astype(jnp.float32)
    for step in range(ITERS):
        low = image.astype(jnp.bfloat16)
        result = 2.0 * result - dot(result.astype(jnp.bfloat16), low)
        if step < ITERS - 1:
            image = 2.0 * image - dot(low, low)
    return result


def split_kernel(x_ref, *out_refs):
    replicas, tokens = len(out_refs), out_refs[0].shape[0]
    here = lax.axis_index("dp")
    x = x_ref[...]
    rows = lax.broadcasted_iota(jnp.int32, (tokens, tokens * replicas), 0)
    cols = lax.broadcasted_iota(jnp.int32, (tokens, tokens * replicas), 1)
    offset = cols - rows * replicas
    for far, out_ref in enumerate(out_refs):
        choice = jnp.where(offset == lax.rem(here + far, replicas), 1.0, 0.0).astype(jnp.bfloat16)
        out_ref[...] = dot(choice, x).astype(jnp.bfloat16)


def split_blocks(factor_inputs):
    tokens, blocks, features = factor_inputs.shape
    return pl.pallas_call(
        split_kernel,
        out_shape=[jax.ShapeDtypeStruct((tokens, features), factor_inputs.dtype)] * blocks,
        in_specs=[WHOLE],
        out_specs=[WHOLE] * blocks,
        compiler_params=pltpu.CompilerParams(vmem_limit_bytes=16 * 2**20),
        name="split_blocks",
    )(factor_inputs.reshape(tokens * blocks, features))


def first_kernel(*refs):
    *pieces, turned, gram = refs
    features = pieces[0].shape[1]
    for k, piece in enumerate(pieces):
        turned[k * features : (k + 1) * features, :] = piece[...].T
    gram[...] = dot(jnp.concatenate([piece[...] for piece in pieces], axis=1), turned[...])


def last_kernel(fars, count, *refs):
    pieces, refs = refs[: len(fars)], refs[len(fars) :]
    turned, gram_in, tile_hbm, out_hbm, *refs = refs
    tile, out, x, xt, k1, k2, k3, k4, low1, low2, g, h, z, image, mixed, sems = refs
    load = pltpu.make_async_copy(tile_hbm, tile, sems.at[0])
    load.start()
    member = lax.axis_index("grad")
    tokens, features = pieces[0].shape
    half = 2 * features
    halves = [slice(at, at + half) for at in range(0, tokens, half)]
    blocks = [slice(at, at + half) for at in range(0, x.shape[1], half)]
    chunks = [slice(at, at + 32) for at in range(0, tokens, 32)]

    for k, (far, piece) in enumerate(zip(fars, pieces)):
        here = pl.ds(pl.multiple_of((member ^ far) * features, features), features)
        x[:, here] = piece[...]
        xt[here, :] = turned[k * features : (k + 1) * features, :] if k < count else piece[...].T
    late = jnp.concatenate([piece[...] for piece in pieces[count:]], axis=1)
    for some in halves:
        product = lax.dot_general(late, late[some], (((1,), (1,)), ((), ())), preferred_element_type=jnp.float32)
        gram = (gram_in[:, some] + product) * (1.0 / tokens)
        k1[:, some] = gram
        low1[:, some] = gram.astype(jnp.bfloat16)

    column_sums, row_sums = [0.0] * len(blocks), [0.0] * len(blocks)

    def add_sums(j):
        column = jnp.abs(dot(xt[: half * (j + 1), :], x[:, blocks[j]]))
        column_sums[j] = column_sums[j] + jnp.sum(column, axis=0, keepdims=True)
        for i in range(j):
            block = column[blocks[i]]
            row_sums[i] = row_sums[i] + block[:, :features] + block[:, features:]

    def move(some):
        image[:, some] = dot(tile[...], xt[:, some]).astype(jnp.bfloat16)

    for j in range(len(blocks) - 1):
        add_sums(j)
    for some in halves:
        k2[:, some] = dot(low1[...], low1[:, some])
    add_sums(len(blocks) - 1)
    load.wait()
    move(halves[0])

    largest = column_sums[-1]
    for column, row in zip(column_sums[:-1], row_sums):
        largest = jnp.maximum(largest, column + jnp.sum(row.T, axis=0, keepdims=True))
    c = 1.0 / (jnp.max(largest) * (1.0 / tokens) + DAMPING)
    eps = 1.0 - c * DAMPING
    eps2 = eps * eps
    zeta = eps2 * eps2
    eps8 = zeta * zeta
    e2_1, e2_2 = -2.0 * eps * c, c * c
    g_1 = -(1.0 + eps) * c
    g_m = eps2 + (1.0 + eps) * eps + eps
    h_m = zeta + (1.0 + eps2) * eps2 + eps2
    k_m = eps8 + (1.0 + zeta) * zeta + zeta + 1.0 + eps8
    k_z = 1.0 + 3.0 * zeta
    a_m = g_m * h_m
    a_e2 = g_m * (1.0 + eps2) + h_m
    a_1 = h_m * g_1
    beta = (1.0 + zeta) * (1.0 + eps8)
    q_m = a_m * k_m + beta * g_m + (1.0 + eps2) * beta
    last = -c * c * (1.0 / tokens)
    q_m = q_m * last
    p = c * (1.0 + eps) * (1.0 + eps2) * beta

    for some in halves:
        for r in chunks:
            x1 = k1[r, some]
            e2 = e2_1 * x1 + e2_2 * k2[r, some]
            k2[r, some] = e2
            low2[r, some] = e2.astype(jnp.bfloat16)
            g[r, some] = (e2 + g_1 * x1).astype(jnp.bfloat16)
    for some in halves:
        product = dot(low2[...], low2[:, some])
        for r in chunks:
            e2 = k2[r, some]
            fourth = 2.0 * eps2 * e2 + product[r]
            k3[r, some] = fourth
            z[r, some] = fourth.astype(jnp.bfloat16)
            h[r, some] = (fourth + (1.0 + eps2) * e2).astype(jnp.bfloat16)
    for some in halves[1:]:
        move(some)

    def add_a(some):
        product = dot(g[...], h[:, some])
        for r in chunks:
            x1, e2 = k1[r, some], k2[r, some]
            a = product[r] + g_m * k3[r, some] + a_e2 * e2 + a_1 * x1
            low1[r, some] = a.astype(jnp.bfloat16)
            k1[r, some] = last * (k_m * a + beta * (e2 + g_1 * x1))

    add_a(halves[0])
    for some in halves:
        product = dot(z[...], z[:, some])
        for r in chunks:
            k = product[r] + k_z * k3[r, some]
            k4[r, some] = k
            low2[r, some] = k.astype(jnp.bfloat16)
    for some in halves[1:]:
        add_a(some)
    for some in halves:
        product = dot(low2[...], low1[:, some])
        for r in chunks:
            g[r, some] = (k1[r, some] + last * (product[r] + a_m * k4[r, some])).astype(jnp.bfloat16)
    for some in halves:
        product = dot(image[...], g[:, some])
        mixed[:, some] = (product + q_m * image[:, some].astype(jnp.float32)).astype(jnp.bfloat16)
    stores = []
    for some in blocks:
        moved = dot(mixed[...], x[:, some])
        parts = 1 if some is not blocks[-1] else 3
        step = moved.shape[0] // parts
        for at in range(0, parts * step, step):
            r = slice(at, at + step)
            out[r, some] = (p * tile[r, some].astype(jnp.float32) + moved[r]).astype(jnp.bfloat16)
            store = pltpu.make_async_copy(out.at[r, some], out_hbm.at[r, some], sems.at[1 + len(stores)])
            store.start()
            stores.append(store)
    for store in stores:
        store.wait()


def swap(value, far):
    return lax.ppermute(value, "grad", [(i, i ^ far) for i in range(lax.axis_size("grad"))])


def by_tokens(factor_inputs, tile):
    members, replicas = lax.axis_size("grad"), lax.axis_size("dp")
    rows, width = tile.shape
    features = factor_inputs.shape[2]
    tokens = factor_inputs.shape[0] * replicas

    def shape(*sizes, kind=jnp.float32):
        return jax.ShapeDtypeStruct(sizes, kind)

    def scratch(*sizes, kind=jnp.bfloat16):
        return pltpu.VMEM(sizes, kind)

    parts = split_blocks(factor_inputs)
    arrived = {
        far: lax.ppermute(parts[far], "dp", [(i, (i + far) % replicas) for i in range(replicas)])
        for far in sorted(range(1, replicas), key=lambda far: abs(far - replicas // 2))
    }
    fars = tuple(range(2, members, 2))
    own = jnp.concatenate([parts[0]] + [arrived[far] for far in range(1, replicas)], axis=0)
    near = swap(own, 1)
    held = [swap(own, far) for far in fars]
    far_near = [swap(piece, 1) for piece in held]
    here, there = [own, near, *held], far_near
    turned, gram = pl.pallas_call(
        first_kernel,
        out_shape=[shape(len(here) * features, tokens, kind=jnp.bfloat16), shape(tokens, tokens)],
        in_specs=[WHOLE] * len(here),
        out_specs=[WHOLE] * 2,
        compiler_params=pltpu.CompilerParams(vmem_limit_bytes=16 * 2**20),
        cost_estimate=pl.CostEstimate(flops=4 * 10**8, bytes_accessed=0, transcendentals=0),
        name="first_pieces",
    )(*here)
    return pl.pallas_call(
        functools.partial(last_kernel, (0, 1, *fars, *[far + 1 for far in fars]), len(here)),
        out_shape=shape(rows, width, kind=jnp.bfloat16),
        in_specs=[WHOLE] * (members + 2) + [ANYWHERE],
        out_specs=ANYWHERE,
        scratch_shapes=[scratch(rows, width)] * 2
        + [scratch(tokens, width), scratch(width, tokens)]
        + [scratch(tokens, tokens, kind=jnp.float32)] * 4
        + [scratch(tokens, tokens)] * 5
        + [scratch(rows, tokens)] * 2
        + [pltpu.SemaphoreType.DMA((3 + members // 2,))],
        compiler_params=pltpu.CompilerParams(vmem_limit_bytes=51 * 2**20),
        cost_estimate=pl.CostEstimate(flops=5 * 10**9, bytes_accessed=0, transcendentals=0),
        name="whole_block",
    )(*here, *there, turned, gram, tile)


def local(factor_inputs, gradients):
    features, members = factor_inputs.shape[2], lax.axis_size("grad")
    tokens = factor_inputs.shape[0] * lax.axis_size("dp")
    tile = gradients[0]
    powers_of_two = all(size & (size - 1) == 0 for size in (members, lax.axis_size("dp")))
    if tokens < features * members and features % 128 == 0 and powers_of_two and members > 2:
        result = by_tokens(factor_inputs, tile)
    else:
        result = by_features(gather_block(factor_inputs), tile)
    return result.astype(jnp.bfloat16)[None]


def solution(mesh):
    placed = (P("dp", None, "grad"), P("dp", "grad", None))
    return jax.shard_map(
        local, mesh=mesh, in_specs=placed, out_specs=P("dp", "grad", None), check_vma=False
    )
```

```python
import functools

import jax
import jax.numpy as jnp
from jax import lax
from jax.experimental import pallas as pl
from jax.experimental.pallas import tpu as pltpu
from jax.sharding import PartitionSpec as P

ITERS = 4
DAMPING = 0.01
WHOLE = pl.BlockSpec(memory_space=pltpu.VMEM)
ANYWHERE = pl.BlockSpec(memory_space=pl.ANY)


def dot(a, b):
    return jnp.dot(a, b, preferred_element_type=jnp.float32)


def gather_block(factor_inputs):
    pieces = jnp.transpose(factor_inputs, (1, 0, 2))
    piece = lax.all_to_all(pieces, "dp", split_axis=0, concat_axis=1, tiled=True)[0]
    return lax.all_gather(piece, "grad", axis=1, tiled=True)


def by_features(columns, tile):
    tokens, width = columns.shape
    covariance = jnp.einsum("tr,tc->rc", columns, columns, preferred_element_type=jnp.float32) * (1.0 / tokens)
    damped = covariance + DAMPING * jnp.eye(width, dtype=jnp.float32)
    scale = 1.0 / jnp.max(jnp.sum(jnp.abs(damped), axis=1))
    image = scale * damped
    result = scale * tile.astype(jnp.float32)
    for step in range(ITERS):
        low = image.astype(jnp.bfloat16)
        result = 2.0 * result - dot(result.astype(jnp.bfloat16), low)
        if step < ITERS - 1:
            image = 2.0 * image - dot(low, low)
    return result


def split_kernel(x_ref, *out_refs):
    replicas, tokens = len(out_refs), out_refs[0].shape[0]
    here = lax.axis_index("dp")
    x = x_ref[...]
    rows = lax.broadcasted_iota(jnp.int32, (tokens, tokens * replicas), 0)
    cols = lax.broadcasted_iota(jnp.int32, (tokens, tokens * replicas), 1)
    offset = cols - rows * replicas
    for far, out_ref in enumerate(out_refs):
        choice = jnp.where(offset == lax.rem(here + far, replicas), 1.0, 0.0).astype(jnp.bfloat16)
        out_ref[...] = dot(choice, x).astype(jnp.bfloat16)


def split_blocks(factor_inputs):
    tokens, blocks, features = factor_inputs.shape
    return pl.pallas_call(
        split_kernel,
        out_shape=[jax.ShapeDtypeStruct((tokens, features), factor_inputs.dtype)] * blocks,
        in_specs=[WHOLE],
        out_specs=[WHOLE] * blocks,
        compiler_params=pltpu.CompilerParams(vmem_limit_bytes=16 * 2**20),
        name="split_blocks",
    )(factor_inputs.reshape(tokens * blocks, features))


def first_kernel(*refs):
    *pieces, turned, gram = refs
    features = pieces[0].shape[1]
    for k, piece in enumerate(pieces):
        turned[k * features : (k + 1) * features, :] = piece[...].T
    gram[...] = dot(jnp.concatenate([piece[...] for piece in pieces], axis=1), turned[...])


def each(size, step, body, index=False, unroll=1):
    def run(i, carry):
        some = pl.ds(pl.multiple_of(i * step, step), step)
        body(some, i) if index else body(some)
        return carry

    lax.fori_loop(0, size // step, run, 0, unroll=unroll)


def last_kernel(fars, count, *refs):
    pieces, refs = refs[: len(fars)], refs[len(fars) :]
    turned, gram_in, tile_hbm, out_hbm, *refs = refs
    tile, out, x, xt, k1, k2, k3, k4, low1, low2, g, h, z, image, mixed, sems = refs
    load = pltpu.make_async_copy(tile_hbm, tile, sems.at[0])
    load.start()
    member = lax.axis_index("grad")
    tokens, features = pieces[0].shape
    half = 2 * features
    blocks = [slice(at, at + half) for at in range(0, x.shape[1], half)]
    chunks = [slice(at, at + 32) for at in range(0, tokens, 32)]

    for k, (far, piece) in enumerate(zip(fars, pieces)):
        here = pl.ds(pl.multiple_of((member ^ far) * features, features), features)
        x[:, here] = piece[...]
        xt[here, :] = turned[k * features : (k + 1) * features, :] if k < count else piece[...].T
    late = jnp.concatenate([piece[...] for piece in pieces[count:]], axis=1)
    def gram_half(some):
        other = jnp.concatenate([piece[some, :] for piece in pieces[count:]], axis=1)
        product = lax.dot_general(late, other, (((1,), (1,)), ((), ())), preferred_element_type=jnp.float32)
        gram = (gram_in[:, some] + product) * (1.0 / tokens)
        k1[:, some] = gram
        low1[:, some] = gram.astype(jnp.bfloat16)

    each(tokens, half, gram_half)

    column_sums, row_sums = [0.0] * len(blocks), [0.0] * len(blocks)

    def add_sums(j):
        column = jnp.abs(dot(xt[: half * (j + 1), :], x[:, blocks[j]]))
        column_sums[j] = column_sums[j] + jnp.sum(column, axis=0, keepdims=True)
        for i in range(j):
            block = column[blocks[i]]
            row_sums[i] = row_sums[i] + block[:, :features] + block[:, features:]

    def move(some):
        image[:, some] = dot(tile[...], xt[:, some]).astype(jnp.bfloat16)

    for j in range(len(blocks) - 1):
        add_sums(j)
    def second(some):
        k2[:, some] = dot(low1[...], low1[:, some])

    each(tokens, half, second)
    add_sums(len(blocks) - 1)
    load.wait()
    each(tokens, half, move)

    largest = column_sums[-1]
    for column, row in zip(column_sums[:-1], row_sums):
        largest = jnp.maximum(largest, column + jnp.sum(row.T, axis=0, keepdims=True))
    c = 1.0 / (jnp.max(largest) * (1.0 / tokens) + DAMPING)
    eps = 1.0 - c * DAMPING
    eps2 = eps * eps
    zeta = eps2 * eps2
    eps8 = zeta * zeta
    e2_1, e2_2 = -2.0 * eps * c, c * c
    g_1 = -(1.0 + eps) * c
    g_m = eps2 + (1.0 + eps) * eps + eps
    h_m = zeta + (1.0 + eps2) * eps2 + eps2
    k_m = eps8 + (1.0 + zeta) * zeta + zeta + 1.0 + eps8
    k_z = 1.0 + 3.0 * zeta
    a_m = g_m * h_m
    a_e2 = g_m * (1.0 + eps2) + h_m
    a_1 = h_m * g_1
    beta = (1.0 + zeta) * (1.0 + eps8)
    q_m = a_m * k_m + beta * g_m + (1.0 + eps2) * beta
    last = -c * c * (1.0 / tokens)
    q_m = q_m * last
    p = c * (1.0 + eps) * (1.0 + eps2) * beta

    def squares(r):
        x1 = k1[r, :]
        e2 = e2_1 * x1 + e2_2 * k2[r, :]
        k2[r, :] = e2
        low2[r, :] = e2.astype(jnp.bfloat16)
        g[r, :] = (e2 + g_1 * x1).astype(jnp.bfloat16)

    each(tokens, 32, squares, unroll=2)

    def fourths(some):
        product = dot(low2[...], low2[:, some])
        for r in chunks:
            e2 = k2[r, some]
            fourth = 2.0 * eps2 * e2 + product[r]
            k3[r, some] = fourth
            z[r, some] = fourth.astype(jnp.bfloat16)
            h[r, some] = (fourth + (1.0 + eps2) * e2).astype(jnp.bfloat16)

    each(tokens, half, fourths)

    def add_a(some):
        product = dot(g[...], h[:, some])
        for r in chunks:
            x1, e2 = k1[r, some], k2[r, some]
            a = product[r] + g_m * k3[r, some] + a_e2 * e2 + a_1 * x1
            low1[r, some] = a.astype(jnp.bfloat16)
            k1[r, some] = last * (k_m * a + beta * (e2 + g_1 * x1))

    each(tokens, half, add_a)

    def add_k(some):
        product = dot(z[...], z[:, some])
        for r in chunks:
            k = product[r] + k_z * k3[r, some]
            k4[r, some] = k
            low2[r, some] = k.astype(jnp.bfloat16)

    each(tokens, half, add_k)

    def add_q(some):
        product = dot(low2[...], low1[:, some])
        for r in chunks:
            g[r, some] = (k1[r, some] + last * (product[r] + a_m * k4[r, some])).astype(jnp.bfloat16)

    each(tokens, half, add_q)

    def mix(some):
        product = dot(image[...], g[:, some])
        mixed[:, some] = (product + q_m * image[:, some].astype(jnp.float32)).astype(jnp.bfloat16)

    each(tokens, half, mix)

    def store(some, i):
        return pltpu.make_async_copy(out.at[:, some], out_hbm.at[:, some], sems.at[1 + i])

    def result(some, i):
        moved = dot(mixed[...], x[:, some])
        out[:, some] = (p * tile[:, some].astype(jnp.float32) + moved).astype(jnp.bfloat16)
        store(some, i).start()

    each(x.shape[1], half, result, index=True)
    each(x.shape[1], half, lambda some, i: store(some, i).wait(), index=True)


def swap(value, far):
    return lax.ppermute(value, "grad", [(i, i ^ far) for i in range(lax.axis_size("grad"))])


def by_tokens(factor_inputs, tile):
    members, replicas = lax.axis_size("grad"), lax.axis_size("dp")
    rows, width = tile.shape
    features = factor_inputs.shape[2]
    tokens = factor_inputs.shape[0] * replicas

    def shape(*sizes, kind=jnp.float32):
        return jax.ShapeDtypeStruct(sizes, kind)

    def scratch(*sizes, kind=jnp.bfloat16):
        return pltpu.VMEM(sizes, kind)

    parts = split_blocks(factor_inputs)
    arrived = {
        far: lax.ppermute(parts[far], "dp", [(i, (i + far) % replicas) for i in range(replicas)])
        for far in sorted(range(1, replicas), key=lambda far: abs(far - replicas // 2))
    }
    fars = tuple(range(2, members, 2))
    own = jnp.concatenate([parts[0]] + [arrived[far] for far in range(1, replicas)], axis=0)
    near = swap(own, 1)
    held = [swap(own, far) for far in fars]
    far_near = [swap(piece, 1) for piece in held]
    here, there = [own, near, *held], far_near
    turned, gram = pl.pallas_call(
        first_kernel,
        out_shape=[shape(len(here) * features, tokens, kind=jnp.bfloat16), shape(tokens, tokens)],
        in_specs=[WHOLE] * len(here),
        out_specs=[WHOLE] * 2,
        compiler_params=pltpu.CompilerParams(vmem_limit_bytes=16 * 2**20),
        cost_estimate=pl.CostEstimate(flops=4 * 10**8, bytes_accessed=0, transcendentals=0),
        name="first_pieces",
    )(*here)
    return pl.pallas_call(
        functools.partial(last_kernel, (0, 1, *fars, *[far + 1 for far in fars]), len(here)),
        out_shape=shape(rows, width, kind=jnp.bfloat16),
        in_specs=[WHOLE] * (members + 2) + [ANYWHERE],
        out_specs=ANYWHERE,
        scratch_shapes=[scratch(rows, width)] * 2
        + [scratch(tokens, width), scratch(width, tokens)]
        + [scratch(tokens, tokens, kind=jnp.float32)] * 4
        + [scratch(tokens, tokens)] * 5
        + [scratch(rows, tokens)] * 2
        + [pltpu.SemaphoreType.DMA((1 + members // 2,))],
        compiler_params=pltpu.CompilerParams(vmem_limit_bytes=51 * 2**20),
        cost_estimate=pl.CostEstimate(flops=5 * 10**9, bytes_accessed=0, transcendentals=0),
        name="whole_block",
    )(*here, *there, turned, gram, tile)


def local(factor_inputs, gradients):
    features, members = factor_inputs.shape[2], lax.axis_size("grad")
    tokens = factor_inputs.shape[0] * lax.axis_size("dp")
    tile = gradients[0]
    powers_of_two = all(size & (size - 1) == 0 for size in (members, lax.axis_size("dp")))
    if tokens < features * members and features % 128 == 0 and powers_of_two and members > 2:
        result = by_tokens(factor_inputs, tile)
    else:
        result = by_features(gather_block(factor_inputs), tile)
    return result.astype(jnp.bfloat16)[None]


def solution(mesh):
    placed = (P("dp", None, "grad"), P("dp", "grad", None))
    return jax.shard_map(
        local, mesh=mesh, in_specs=placed, out_specs=P("dp", "grad", None), check_vma=False
    )
```

```python
import functools

import jax
import jax.numpy as jnp
from jax import lax
from jax.experimental import pallas as pl
from jax.experimental.pallas import tpu as pltpu
from jax.sharding import PartitionSpec as P

ITERS = 4
DAMPING = 0.01
WHOLE = pl.BlockSpec(memory_space=pltpu.VMEM)
ANYWHERE = pl.BlockSpec(memory_space=pl.ANY)


def dot(a, b):
    return jnp.dot(a, b, preferred_element_type=jnp.float32)


def gather_block(factor_inputs):
    pieces = jnp.transpose(factor_inputs, (1, 0, 2))
    piece = lax.all_to_all(pieces, "dp", split_axis=0, concat_axis=1, tiled=True)[0]
    return lax.all_gather(piece, "grad", axis=1, tiled=True)


def by_features(columns, tile):
    tokens, width = columns.shape
    covariance = jnp.einsum("tr,tc->rc", columns, columns, preferred_element_type=jnp.float32) * (1.0 / tokens)
    damped = covariance + DAMPING * jnp.eye(width, dtype=jnp.float32)
    scale = 1.0 / jnp.max(jnp.sum(jnp.abs(damped), axis=1))
    image = scale * damped
    result = scale * tile.astype(jnp.float32)
    for step in range(ITERS):
        low = image.astype(jnp.bfloat16)
        result = 2.0 * result - dot(result.astype(jnp.bfloat16), low)
        if step < ITERS - 1:
            image = 2.0 * image - dot(low, low)
    return result


def split_kernel(x_ref, *out_refs):
    replicas, tokens = len(out_refs), out_refs[0].shape[0]
    here = lax.axis_index("dp")
    x = x_ref[...]
    rows = lax.broadcasted_iota(jnp.int32, (tokens, tokens * replicas), 0)
    cols = lax.broadcasted_iota(jnp.int32, (tokens, tokens * replicas), 1)
    offset = cols - rows * replicas
    for far, out_ref in enumerate(out_refs):
        choice = jnp.where(offset == lax.rem(here + far, replicas), 1.0, 0.0).astype(jnp.bfloat16)
        out_ref[...] = dot(choice, x).astype(jnp.bfloat16)


def split_blocks(factor_inputs):
    tokens, blocks, features = factor_inputs.shape
    return pl.pallas_call(
        split_kernel,
        out_shape=[jax.ShapeDtypeStruct((tokens, features), factor_inputs.dtype)] * blocks,
        in_specs=[WHOLE],
        out_specs=[WHOLE] * blocks,
        compiler_params=pltpu.CompilerParams(vmem_limit_bytes=16 * 2**20),
        name="split_blocks",
    )(factor_inputs.reshape(tokens * blocks, features))


def first_kernel(*refs):
    *pieces, turned, gram = refs
    features = pieces[0].shape[1]
    for k, piece in enumerate(pieces):
        turned[k * features : (k + 1) * features, :] = piece[...].T
    gram[...] = dot(jnp.concatenate([piece[...] for piece in pieces], axis=1), turned[...])


def last_kernel(fars, count, *refs):
    pieces, refs = refs[: len(fars)], refs[len(fars) :]
    turned, gram_in, tile_hbm, out_hbm, *refs = refs
    tile, out, x, xt, k1, k2, e2, g, z, h, a, k, q, image, mixed, sems = refs
    load = pltpu.make_async_copy(tile_hbm, tile, sems.at[0])
    load.start()
    member = lax.axis_index("grad")
    tokens, features = pieces[0].shape
    half = 2 * features
    halves = [slice(at, at + half) for at in range(0, tokens, half)]
    blocks = [slice(at, at + half) for at in range(0, x.shape[1], half)]
    chunks = [slice(at, at + 32) for at in range(0, tokens, 32)]

    for n, (far, piece) in enumerate(zip(fars, pieces)):
        here = pl.ds(pl.multiple_of((member ^ far) * features, features), features)
        x[:, here] = piece[...]
        xt[here, :] = turned[n * features : (n + 1) * features, :] if n < count else piece[...].T
    late = jnp.concatenate([piece[...] for piece in pieces[count:]], axis=1)
    for some in halves:
        product = lax.dot_general(late, late[some], (((1,), (1,)), ((), ())), preferred_element_type=jnp.float32)
        k1[:, some] = ((gram_in[:, some] + product) * (1.0 / tokens)).astype(jnp.bfloat16)

    column_sums, row_sums = [0.0] * len(blocks), [0.0] * len(blocks)

    def add_sums(j):
        column = jnp.abs(dot(xt[: half * (j + 1), :], x[:, blocks[j]]))
        column_sums[j] = column_sums[j] + jnp.sum(column, axis=0, keepdims=True)
        for i in range(j):
            block = column[blocks[i]]
            row_sums[i] = row_sums[i] + block[:, :features] + block[:, features:]

    def move(some):
        image[:, some] = dot(tile[...], xt[:, some]).astype(jnp.bfloat16)

    for j in range(len(blocks) - 1):
        add_sums(j)
    for some in halves:
        k2[:, some] = dot(k1[...], k1[:, some]).astype(jnp.bfloat16)
    add_sums(len(blocks) - 1)
    load.wait()
    move(halves[0])

    largest = column_sums[-1]
    for column, row in zip(column_sums[:-1], row_sums):
        largest = jnp.maximum(largest, column + jnp.sum(row.T, axis=0, keepdims=True))
    c = 1.0 / (jnp.max(largest) * (1.0 / tokens) + DAMPING)
    eps = 1.0 - c * DAMPING
    eps2 = eps * eps
    zeta = eps2 * eps2
    eps8 = zeta * zeta
    e2_1, e2_2 = -2.0 * eps * c, c * c
    g_1 = -(1.0 + eps) * c
    g_m = eps2 + (1.0 + eps) * eps + eps
    h_m = zeta + (1.0 + eps2) * eps2 + eps2
    k_m = eps8 + (1.0 + zeta) * zeta + zeta + 1.0 + eps8
    k_z = 1.0 + 3.0 * zeta
    a_m = g_m * h_m
    beta = (1.0 + zeta) * (1.0 + eps8)
    q_m = a_m * k_m + beta * g_m + (1.0 + eps2) * beta
    last = -c * c * (1.0 / tokens)
    q_m = q_m * last
    p = c * (1.0 + eps) * (1.0 + eps2) * beta

    def wide(ref, r, some):
        return ref[r, some].astype(jnp.float32)

    for some in halves:
        for r in chunks:
            first = wide(k1, r, some)
            square = e2_1 * first + e2_2 * wide(k2, r, some)
            e2[r, some] = square.astype(jnp.bfloat16)
            g[r, some] = (square + g_1 * first).astype(jnp.bfloat16)
    for some in halves:
        product = dot(e2[...], e2[:, some])
        for r in chunks:
            square = wide(e2, r, some)
            fourth = 2.0 * eps2 * square + product[r]
            z[r, some] = fourth.astype(jnp.bfloat16)
            h[r, some] = (fourth + (1.0 + eps2) * square).astype(jnp.bfloat16)
    for some in halves[1:]:
        move(some)

    def add_a(some):
        product = dot(g[...], h[:, some])
        for r in chunks:
            a[r, some] = (product[r] + g_m * wide(h, r, some) + h_m * wide(g, r, some)).astype(jnp.bfloat16)

    add_a(halves[0])
    for some in halves:
        product = dot(z[...], z[:, some])
        for r in chunks:
            k[r, some] = (product[r] + k_z * wide(z, r, some)).astype(jnp.bfloat16)
    for some in halves[1:]:
        add_a(some)
    q_k, q_a, q_g = last * a_m, last * k_m, last * beta
    for some in halves:
        product = dot(k[...], a[:, some])
        for r in chunks:
            rest = q_k * wide(k, r, some) + q_a * wide(a, r, some) + q_g * wide(g, r, some)
            q[r, some] = (last * product[r] + rest).astype(jnp.bfloat16)
    for some in halves:
        product = dot(image[...], q[:, some])
        mixed[:, some] = (product + q_m * image[:, some].astype(jnp.float32)).astype(jnp.bfloat16)
    stores = []
    for some in blocks:
        moved = dot(mixed[...], x[:, some])
        parts = 1 if some is not blocks[-1] else 3
        step = moved.shape[0] // parts
        for at in range(0, parts * step, step):
            r = slice(at, at + step)
            out[r, some] = (p * tile[r, some].astype(jnp.float32) + moved[r]).astype(jnp.bfloat16)
            store = pltpu.make_async_copy(out.at[r, some], out_hbm.at[r, some], sems.at[1 + len(stores)])
            store.start()
            stores.append(store)
    for store in stores:
        store.wait()


def swap(value, far):
    return lax.ppermute(value, "grad", [(i, i ^ far) for i in range(lax.axis_size("grad"))])


def by_tokens(factor_inputs, tile):
    members, replicas = lax.axis_size("grad"), lax.axis_size("dp")
    rows, width = tile.shape
    features = factor_inputs.shape[2]
    tokens = factor_inputs.shape[0] * replicas

    def shape(*sizes, kind=jnp.float32):
        return jax.ShapeDtypeStruct(sizes, kind)

    def scratch(*sizes, kind=jnp.bfloat16):
        return pltpu.VMEM(sizes, kind)

    parts = split_blocks(factor_inputs)
    arrived = {
        far: lax.ppermute(parts[far], "dp", [(i, (i + far) % replicas) for i in range(replicas)])
        for far in sorted(range(1, replicas), key=lambda far: abs(far - replicas // 2))
    }
    fars = tuple(range(2, members, 2))
    own = jnp.concatenate([parts[0]] + [arrived[far] for far in range(1, replicas)], axis=0)
    near = swap(own, 1)
    held = [swap(own, far) for far in fars]
    far_near = [swap(piece, 1) for piece in held]
    here, there = [own, near, *held], far_near
    turned, gram = pl.pallas_call(
        first_kernel,
        out_shape=[shape(len(here) * features, tokens, kind=jnp.bfloat16), shape(tokens, tokens)],
        in_specs=[WHOLE] * len(here),
        out_specs=[WHOLE] * 2,
        compiler_params=pltpu.CompilerParams(vmem_limit_bytes=16 * 2**20),
        cost_estimate=pl.CostEstimate(flops=4 * 10**8, bytes_accessed=0, transcendentals=0),
        name="first_pieces",
    )(*here)
    return pl.pallas_call(
        functools.partial(last_kernel, (0, 1, *fars, *[far + 1 for far in fars]), len(here)),
        out_shape=shape(rows, width, kind=jnp.bfloat16),
        in_specs=[WHOLE] * (members + 2) + [ANYWHERE],
        out_specs=ANYWHERE,
        scratch_shapes=[scratch(rows, width)] * 2
        + [scratch(tokens, width), scratch(width, tokens)]
        + [scratch(tokens, tokens)] * 9
        + [scratch(rows, tokens)] * 2
        + [pltpu.SemaphoreType.DMA((3 + members // 2,))],
        compiler_params=pltpu.CompilerParams(vmem_limit_bytes=51 * 2**20),
        cost_estimate=pl.CostEstimate(flops=5 * 10**9, bytes_accessed=0, transcendentals=0),
        name="whole_block",
    )(*here, *there, turned, gram, tile)


def local(factor_inputs, gradients):
    features, members = factor_inputs.shape[2], lax.axis_size("grad")
    tokens = factor_inputs.shape[0] * lax.axis_size("dp")
    tile = gradients[0]
    powers_of_two = all(size & (size - 1) == 0 for size in (members, lax.axis_size("dp")))
    if tokens < features * members and features % 128 == 0 and powers_of_two and members > 2:
        result = by_tokens(factor_inputs, tile)
    else:
        result = by_features(gather_block(factor_inputs), tile)
    return result.astype(jnp.bfloat16)[None]


def solution(mesh):
    placed = (P("dp", None, "grad"), P("dp", "grad", None))
    return jax.shard_map(
        local, mesh=mesh, in_specs=placed, out_specs=P("dp", "grad", None), check_vma=False
    )
```

```python
import functools

import jax
import jax.numpy as jnp
from jax import lax
from jax.experimental import pallas as pl
from jax.experimental.pallas import tpu as pltpu
from jax.sharding import PartitionSpec as P

ITERS = 4
DAMPING = 0.01
WHOLE = pl.BlockSpec(memory_space=pltpu.VMEM)
ANYWHERE = pl.BlockSpec(memory_space=pl.ANY)


def dot(a, b):
    return jnp.dot(a, b, preferred_element_type=jnp.float32)


def gather_block(factor_inputs):
    pieces = jnp.transpose(factor_inputs, (1, 0, 2))
    piece = lax.all_to_all(pieces, "dp", split_axis=0, concat_axis=1, tiled=True)[0]
    return lax.all_gather(piece, "grad", axis=1, tiled=True)


def by_features(columns, tile):
    tokens, width = columns.shape
    covariance = jnp.einsum("tr,tc->rc", columns, columns, preferred_element_type=jnp.float32) * (1.0 / tokens)
    damped = covariance + DAMPING * jnp.eye(width, dtype=jnp.float32)
    scale = 1.0 / jnp.max(jnp.sum(jnp.abs(damped), axis=1))
    image = scale * damped
    result = scale * tile.astype(jnp.float32)
    for step in range(ITERS):
        low = image.astype(jnp.bfloat16)
        result = 2.0 * result - dot(result.astype(jnp.bfloat16), low)
        if step < ITERS - 1:
            image = 2.0 * image - dot(low, low)
    return result


def split_kernel(x_ref, *out_refs):
    replicas, tokens = len(out_refs), out_refs[0].shape[0]
    here = lax.axis_index("dp")
    x = x_ref[...]
    rows = lax.broadcasted_iota(jnp.int32, (tokens, tokens * replicas), 0)
    cols = lax.broadcasted_iota(jnp.int32, (tokens, tokens * replicas), 1)
    offset = cols - rows * replicas
    for far, out_ref in enumerate(out_refs):
        choice = jnp.where(offset == lax.rem(here + far, replicas), 1.0, 0.0).astype(jnp.bfloat16)
        out_ref[...] = dot(choice, x).astype(jnp.bfloat16)


def split_blocks(factor_inputs):
    tokens, blocks, features = factor_inputs.shape
    return pl.pallas_call(
        split_kernel,
        out_shape=[jax.ShapeDtypeStruct((tokens, features), factor_inputs.dtype)] * blocks,
        in_specs=[WHOLE],
        out_specs=[WHOLE] * blocks,
        compiler_params=pltpu.CompilerParams(vmem_limit_bytes=16 * 2**20),
        name="split_blocks",
    )(factor_inputs.reshape(tokens * blocks, features))


def first_kernel(*refs):
    *pieces, turned, gram = refs
    features = pieces[0].shape[1]
    for k, piece in enumerate(pieces):
        turned[k * features : (k + 1) * features, :] = piece[...].T
    gram[...] = dot(jnp.concatenate([piece[...] for piece in pieces], axis=1), turned[...])


def last_kernel(fars, count, *refs):
    pieces, refs = refs[: len(fars)], refs[len(fars) :]
    turned, gram_in, tile_hbm, out_hbm, *refs = refs
    tile, out, x, xt, k1, k2, e2, g, z, h, a, k, q, image, mixed, sems = refs
    load = pltpu.make_async_copy(tile_hbm, tile, sems.at[0])
    load.start()
    member = lax.axis_index("grad")
    tokens, features = pieces[0].shape
    half = 2 * features
    halves = [slice(at, at + half) for at in range(0, tokens, half)]
    blocks = [slice(at, at + half) for at in range(0, x.shape[1], half)]
    chunks = [slice(at, at + 32) for at in range(0, tokens, 32)]

    for n, (far, piece) in enumerate(zip(fars, pieces)):
        here = pl.ds(pl.multiple_of((member ^ far) * features, features), features)
        x[:, here] = piece[...]
        xt[here, :] = turned[n * features : (n + 1) * features, :] if n < count else piece[...].T
    late = jnp.concatenate([piece[...] for piece in pieces[count:]], axis=1)

    def symmetric(left, right, finish, *refs):
        for n, some in enumerate(halves):
            rows = slice(some.start, tokens)
            product = left(rows, some) if right is None else dot(left[rows, :], right[:, some])
            for r in chunks[some.start // 32 :]:
                values = finish(product[r.start - some.start : r.stop - some.start], r, some)
                for ref, value in zip(refs, values):
                    ref[r, some] = value.astype(jnp.bfloat16)
            for other in halves[n + 1 :]:
                for ref in refs:
                    ref[some, other] = ref[other, some].T

    def gram(rows, some):
        return lax.dot_general(late[rows], late[some], (((1,), (1,)), ((), ())), preferred_element_type=jnp.float32)

    symmetric(gram, None, lambda product, r, some: [(gram_in[r, some] + product) * (1.0 / tokens)], k1)

    column_sums, row_sums = [0.0] * len(blocks), [0.0] * len(blocks)

    def add_sums(j):
        column = jnp.abs(dot(xt[: half * (j + 1), :], x[:, blocks[j]]))
        column_sums[j] = column_sums[j] + jnp.sum(column, axis=0, keepdims=True)
        for i in range(j):
            block = column[blocks[i]]
            row_sums[i] = row_sums[i] + block[:, :features] + block[:, features:]

    def move(some):
        image[:, some] = dot(tile[...], xt[:, some]).astype(jnp.bfloat16)

    for j in range(len(blocks) - 1):
        add_sums(j)
    symmetric(k1, k1, lambda product, r, some: [product], k2)
    add_sums(len(blocks) - 1)
    load.wait()
    move(halves[0])

    largest = column_sums[-1]
    for column, row in zip(column_sums[:-1], row_sums):
        largest = jnp.maximum(largest, column + jnp.sum(row.T, axis=0, keepdims=True))
    c = 1.0 / (jnp.max(largest) * (1.0 / tokens) + DAMPING)
    eps = 1.0 - c * DAMPING
    eps2 = eps * eps
    zeta = eps2 * eps2
    eps8 = zeta * zeta
    e2_1, e2_2 = -2.0 * eps * c, c * c
    g_1 = -(1.0 + eps) * c
    g_m = eps2 + (1.0 + eps) * eps + eps
    h_m = zeta + (1.0 + eps2) * eps2 + eps2
    k_m = eps8 + (1.0 + zeta) * zeta + zeta + 1.0 + eps8
    k_z = 1.0 + 3.0 * zeta
    a_m = g_m * h_m
    beta = (1.0 + zeta) * (1.0 + eps8)
    q_m = a_m * k_m + beta * g_m + (1.0 + eps2) * beta
    last = -c * c * (1.0 / tokens)
    q_m = q_m * last
    p = c * (1.0 + eps) * (1.0 + eps2) * beta

    def wide(ref, r, some):
        return ref[r, some].astype(jnp.float32)

    for some in halves:
        for r in chunks:
            first = wide(k1, r, some)
            square = e2_1 * first + e2_2 * wide(k2, r, some)
            e2[r, some] = square.astype(jnp.bfloat16)
            g[r, some] = (square + g_1 * first).astype(jnp.bfloat16)

    def fourth(product, r, some):
        square = wide(e2, r, some)
        value = 2.0 * eps2 * square + product
        return value, value + (1.0 + eps2) * square

    symmetric(e2, e2, fourth, z, h)
    for some in halves[1:]:
        move(some)
    symmetric(z, z, lambda product, r, some: [product + k_z * wide(z, r, some)], k)
    symmetric(g, h, lambda product, r, some: [product + g_m * wide(h, r, some) + h_m * wide(g, r, some)], a)
    q_k, q_a, q_g = last * a_m, last * k_m, last * beta

    def whole(product, r, some):
        return [last * product + q_k * wide(k, r, some) + q_a * wide(a, r, some) + q_g * wide(g, r, some)]

    symmetric(k, a, whole, q)
    for some in halves:
        product = dot(image[...], q[:, some])
        mixed[:, some] = (product + q_m * image[:, some].astype(jnp.float32)).astype(jnp.bfloat16)
    stores = []
    for some in blocks:
        moved = dot(mixed[...], x[:, some])
        parts = 1 if some is not blocks[-1] else 3
        step = moved.shape[0] // parts
        for at in range(0, parts * step, step):
            r = slice(at, at + step)
            out[r, some] = (p * tile[r, some].astype(jnp.float32) + moved[r]).astype(jnp.bfloat16)
            store = pltpu.make_async_copy(out.at[r, some], out_hbm.at[r, some], sems.at[1 + len(stores)])
            store.start()
            stores.append(store)
    for store in stores:
        store.wait()


def swap(value, far):
    return lax.ppermute(value, "grad", [(i, i ^ far) for i in range(lax.axis_size("grad"))])


def by_tokens(factor_inputs, tile):
    members, replicas = lax.axis_size("grad"), lax.axis_size("dp")
    rows, width = tile.shape
    features = factor_inputs.shape[2]
    tokens = factor_inputs.shape[0] * replicas

    def shape(*sizes, kind=jnp.float32):
        return jax.ShapeDtypeStruct(sizes, kind)

    def scratch(*sizes, kind=jnp.bfloat16):
        return pltpu.VMEM(sizes, kind)

    parts = split_blocks(factor_inputs)
    arrived = {
        far: lax.ppermute(parts[far], "dp", [(i, (i + far) % replicas) for i in range(replicas)])
        for far in sorted(range(1, replicas), key=lambda far: abs(far - replicas // 2))
    }
    fars = tuple(range(2, members, 2))
    rest = jnp.concatenate([arrived[far] for far in range(1, replicas)], axis=0)
    early = swap(parts[0], fars[-1])
    own = jnp.concatenate([parts[0] + 0.0 * early, rest], axis=0)
    near = swap(own, 1)
    held = [swap(own, far) for far in fars[:-1]]
    held.append(jnp.concatenate([early, swap(own[parts[0].shape[0] :], fars[-1])], axis=0))
    held_near = [swap(piece, 1) for piece in held]
    here, there = [own, near, *held, held_near[-1]], held_near[:-1]
    turned, gram = pl.pallas_call(
        first_kernel,
        out_shape=[shape(len(here) * features, tokens, kind=jnp.bfloat16), shape(tokens, tokens)],
        in_specs=[WHOLE] * len(here),
        out_specs=[WHOLE] * 2,
        compiler_params=pltpu.CompilerParams(vmem_limit_bytes=16 * 2**20),
        cost_estimate=pl.CostEstimate(flops=4 * 10**8, bytes_accessed=0, transcendentals=0),
        name="first_pieces",
    )(*here)
    return pl.pallas_call(
        functools.partial(last_kernel, (0, 1, *fars, fars[-1] + 1, *[far + 1 for far in fars[:-1]]), len(here)),
        out_shape=shape(rows, width, kind=jnp.bfloat16),
        in_specs=[WHOLE] * (members + 2) + [ANYWHERE],
        out_specs=ANYWHERE,
        scratch_shapes=[scratch(rows, width)] * 2
        + [scratch(tokens, width), scratch(width, tokens)]
        + [scratch(tokens, tokens)] * 9
        + [scratch(rows, tokens)] * 2
        + [pltpu.SemaphoreType.DMA((3 + members // 2,))],
        compiler_params=pltpu.CompilerParams(vmem_limit_bytes=51 * 2**20),
        cost_estimate=pl.CostEstimate(flops=5 * 10**9, bytes_accessed=0, transcendentals=0),
        name="whole_block",
    )(*here, *there, turned, gram, tile)


def local(factor_inputs, gradients):
    features, members = factor_inputs.shape[2], lax.axis_size("grad")
    tokens = factor_inputs.shape[0] * lax.axis_size("dp")
    tile = gradients[0]
    powers_of_two = all(size & (size - 1) == 0 for size in (members, lax.axis_size("dp")))
    if tokens < features * members and features % 128 == 0 and powers_of_two and members > 2:
        result = by_tokens(factor_inputs, tile)
    else:
        result = by_features(gather_block(factor_inputs), tile)
    return result.astype(jnp.bfloat16)[None]


def solution(mesh):
    placed = (P("dp", None, "grad"), P("dp", "grad", None))
    return jax.shard_map(
        local, mesh=mesh, in_specs=placed, out_specs=P("dp", "grad", None), check_vma=False
    )
```

```python
import functools

import jax
import jax.numpy as jnp
from jax import lax
from jax.experimental import pallas as pl
from jax.experimental.pallas import tpu as pltpu
from jax.sharding import PartitionSpec as P

ITERS = 4
DAMPING = 0.01
WHOLE = pl.BlockSpec(memory_space=pltpu.VMEM)
ANYWHERE = pl.BlockSpec(memory_space=pl.ANY)


def dot(a, b):
    return jnp.dot(a, b, preferred_element_type=jnp.float32)


def gather_block(factor_inputs):
    pieces = jnp.transpose(factor_inputs, (1, 0, 2))
    piece = lax.all_to_all(pieces, "dp", split_axis=0, concat_axis=1, tiled=True)[0]
    return lax.all_gather(piece, "grad", axis=1, tiled=True)


def by_features(columns, tile):
    tokens, width = columns.shape
    covariance = jnp.einsum("tr,tc->rc", columns, columns, preferred_element_type=jnp.float32) * (1.0 / tokens)
    damped = covariance + DAMPING * jnp.eye(width, dtype=jnp.float32)
    scale = 1.0 / jnp.max(jnp.sum(jnp.abs(damped), axis=1))
    image = scale * damped
    result = scale * tile.astype(jnp.float32)
    for step in range(ITERS):
        low = image.astype(jnp.bfloat16)
        result = 2.0 * result - dot(result.astype(jnp.bfloat16), low)
        if step < ITERS - 1:
            image = 2.0 * image - dot(low, low)
    return result


def split_kernel(x_ref, *out_refs):
    replicas, tokens = len(out_refs), out_refs[0].shape[0]
    here = lax.axis_index("dp")
    core = lax.rem(lax.axis_index("grad"), 2)
    fars = (0, 2, 1 + 2 * core, 3 - 2 * core)
    x = x_ref[...]
    rows = lax.broadcasted_iota(jnp.int32, (tokens, tokens * replicas), 0)
    cols = lax.broadcasted_iota(jnp.int32, (tokens, tokens * replicas), 1)
    offset = cols - rows * replicas
    for far, out_ref in zip(fars, out_refs):
        choice = jnp.where(offset == lax.rem(here + far, replicas), 1.0, 0.0).astype(jnp.bfloat16)
        out_ref[...] = dot(choice, x).astype(jnp.bfloat16)


def split_blocks(factor_inputs):
    tokens, blocks, features = factor_inputs.shape
    return pl.pallas_call(
        split_kernel,
        out_shape=[jax.ShapeDtypeStruct((tokens, features), factor_inputs.dtype)] * blocks,
        in_specs=[WHOLE],
        out_specs=[WHOLE] * blocks,
        compiler_params=pltpu.CompilerParams(vmem_limit_bytes=16 * 2**20),
        name="split_blocks",
    )(factor_inputs.reshape(tokens * blocks, features))


def columns_of(same, other):
    tokens = same.shape[0]
    q0, q1, q2, q3 = [slice(at, at + tokens // 4) for at in range(0, tokens, tokens // 4)]
    mine = jnp.concatenate([same[q0, :], same[q1, :], same[q2, :], other[q3, :]], axis=0)
    its = jnp.concatenate([other[q0, :], other[q1, :], same[q3, :], other[q2, :]], axis=0)
    return jnp.concatenate([mine, its], axis=1)


def first_kernel(own, near, across, across_near, got, columns, turned, gram):
    tokens = own.shape[0]
    pairs = [(own, near), (across, across_near), (got.at[:tokens], got.at[tokens:])]
    wide = 2 * own.shape[1]
    for n, (same, other) in enumerate(pairs):
        some = slice(n * wide, (n + 1) * wide)
        value = columns_of(same, other)
        columns[:, some] = value
        turned[some, :] = value.T
    gram[...] = dot(columns[...], turned[...])


def last_kernel(late_ref, x, xt, gram_in, tile_hbm, out_hbm, *refs):
    tile, out, late, late_t, k1, k2, e2, g, z, h, a, k, q, image, mixed, sems = refs
    load = pltpu.make_async_copy(tile_hbm, tile, sems.at[0])
    load.start()
    member = lax.axis_index("grad")
    core = lax.rem(member, 2)
    tokens = x.shape[0]
    half = late.shape[1]
    features = half // 2
    halves = [slice(at, at + half) for at in range(0, tokens, half)]
    blocks = [slice(at, at + half) for at in range(0, x.shape[1], half)]
    chunks = [slice(at, at + 32) for at in range(0, tokens, 32)]
    fars = [0, 6, 2 + 2 * core, 4 - 2 * core]

    def place(far):
        return pl.ds(pl.multiple_of((member ^ far) * features, features), features)

    def chosen(some):
        return jnp.concatenate([tile[:, place(far ^ one)] for far in some for one in (0, 1)], axis=1)

    late[...] = columns_of(late_ref.at[tokens:], late_ref.at[:tokens])
    late_t[...] = late[...].T

    def symmetric(left, right, finish, *refs):
        for n, some in enumerate(halves):
            rows = slice(some.start, tokens)
            product = left(rows, some) if right is None else dot(left[rows, :], right[:, some])
            for r in chunks[some.start // 32 :]:
                values = finish(product[r.start - some.start : r.stop - some.start], r, some)
                for ref, value in zip(refs, values):
                    ref[r, some] = value.astype(jnp.bfloat16)
            for other in halves[n + 1 :]:
                for ref in refs:
                    ref[some, other] = ref[other, some].T

    def gram(rows, some):
        return lax.dot_general(late[rows, :], late[some, :], (((1,), (1,)), ((), ())), preferred_element_type=jnp.float32)

    symmetric(gram, None, lambda product, r, some: [(gram_in[r, some] + product) * (1.0 / tokens)], k1)

    column_sums, row_sums = [0.0] * (len(blocks) + 1), [0.0] * len(blocks)

    def add_sums(n, left, right):
        column = jnp.abs(dot(left, right))
        column_sums[n] = column_sums[n] + jnp.sum(column, axis=0, keepdims=True)
        for i, some in enumerate(blocks[: min(n, column.shape[0] // half)]):
            row_sums[i] = row_sums[i] + column[some, :features] + column[some, features:]

    def move(some):
        moved = dot(chosen(fars[:-1]), xt[:, some]) + dot(chosen(fars[-1:]), late_t[:, some])
        image[:, some] = moved.astype(jnp.bfloat16)

    for n, some in enumerate(blocks):
        add_sums(n, xt[: some.stop, :], x[:, some])
    symmetric(k1, k1, lambda product, r, some: [product], k2)
    add_sums(len(blocks), xt[...], late[...])
    column_sums[-1] = column_sums[-1] + jnp.sum(jnp.abs(dot(late_t[...], late[...])), axis=0, keepdims=True)
    load.wait()
    move(halves[0])

    largest = column_sums[-1]
    for column, row in zip(column_sums[:-1], row_sums):
        largest = jnp.maximum(largest, column + jnp.sum(row.T, axis=0, keepdims=True))
    c = 1.0 / (jnp.max(largest) * (1.0 / tokens) + DAMPING)
    eps = 1.0 - c * DAMPING
    eps2 = eps * eps
    zeta = eps2 * eps2
    eps8 = zeta * zeta
    e2_1, e2_2 = -2.0 * eps * c, c * c
    g_1 = -(1.0 + eps) * c
    g_m = eps2 + (1.0 + eps) * eps + eps
    h_m = zeta + (1.0 + eps2) * eps2 + eps2
    k_m = eps8 + (1.0 + zeta) * zeta + zeta + 1.0 + eps8
    k_z = 1.0 + 3.0 * zeta
    a_m = g_m * h_m
    beta = (1.0 + zeta) * (1.0 + eps8)
    q_m = a_m * k_m + beta * g_m + (1.0 + eps2) * beta
    last = -c * c * (1.0 / tokens)
    q_m = q_m * last
    p = c * (1.0 + eps) * (1.0 + eps2) * beta

    def wide(ref, r, some):
        return ref[r, some].astype(jnp.float32)

    for some in halves:
        for r in chunks:
            first = wide(k1, r, some)
            square = e2_1 * first + e2_2 * wide(k2, r, some)
            e2[r, some] = square.astype(jnp.bfloat16)
            g[r, some] = (square + g_1 * first).astype(jnp.bfloat16)

    def fourth(product, r, some):
        square = wide(e2, r, some)
        value = 2.0 * eps2 * square + product
        return value, value + (1.0 + eps2) * square

    symmetric(e2, e2, fourth, z, h)
    for some in halves[1:]:
        move(some)
    symmetric(z, z, lambda product, r, some: [product + k_z * wide(z, r, some)], k)
    for some in halves:
        product = dot(g[...], h[:, some])
        for r in chunks:
            a[r, some] = (product[r] + g_m * wide(h, r, some) + h_m * wide(g, r, some)).astype(jnp.bfloat16)
    q_k, q_a, q_g = last * a_m, last * k_m, last * beta
    for some in halves:
        product = dot(k[...], a[:, some])
        for r in chunks:
            rest = q_k * wide(k, r, some) + q_a * wide(a, r, some) + q_g * wide(g, r, some)
            q[r, some] = (last * product[r] + rest).astype(jnp.bfloat16)
    for some in halves:
        product = dot(image[...], q[:, some])
        mixed[:, some] = (product + q_m * image[:, some].astype(jnp.float32)).astype(jnp.bfloat16)
    stores = []
    for n, far in enumerate(fars):
        moved = dot(mixed[...], late[...] if n == len(blocks) else x[:, blocks[n]])
        for one in (0, 1):
            here = place(far ^ one)
            kept = p * tile[:, here].astype(jnp.float32)
            out[:, here] = (kept + moved[:, one * features : (one + 1) * features]).astype(jnp.bfloat16)
            store = pltpu.make_async_copy(out.at[:, here], out_hbm.at[:, here], sems.at[1 + len(stores)])
            store.start()
            stores.append(store)
    for store in stores:
        store.wait()


def by_tokens(factor_inputs, tile):
    members, replicas = lax.axis_size("grad"), lax.axis_size("dp")
    rows, width = tile.shape
    features = factor_inputs.shape[2]
    tokens = factor_inputs.shape[0] * replicas

    def shape(*sizes, kind=jnp.bfloat16):
        return jax.ShapeDtypeStruct(sizes, kind)

    def scratch(*sizes):
        return pltpu.VMEM(sizes, jnp.bfloat16)

    def swap(value, *fars):
        return lax.ppermute(value, "grad", [(i, i ^ fars[i % len(fars)]) for i in range(members)])

    part, part_across, mine, given = split_blocks(factor_inputs)
    both = jnp.concatenate([mine, swap(given, 1)], axis=0)
    across = lax.ppermute(part_across, "dp", [(i, (i + 2) % replicas) for i in range(replicas)])
    along = lax.ppermute(
        both,
        ("dp", "grad"),
        [
            (i * members + j, (i + (3 if j % 2 else 1)) % replicas * members + j)
            for i in range(replicas)
            for j in range(members)
        ],
    )
    own = jnp.concatenate([part, across, along], axis=0)
    near = swap(own, 1)
    diagonal = swap(own, 6)
    got = swap(jnp.concatenate([own, near], axis=0), 2, 4)
    diagonal_near = swap(diagonal, 1)
    late = swap(got, 1)
    early = width - 2 * features
    columns, turned, gram = pl.pallas_call(
        first_kernel,
        out_shape=[shape(tokens, early), shape(early, tokens), shape(tokens, tokens, kind=jnp.float32)],
        in_specs=[WHOLE] * 5,
        out_specs=[WHOLE] * 3,
        compiler_params=pltpu.CompilerParams(vmem_limit_bytes=16 * 2**20),
        cost_estimate=pl.CostEstimate(flops=4 * 10**8, bytes_accessed=0, transcendentals=0),
        name="first_chips",
    )(own, near, diagonal, diagonal_near, got)
    return pl.pallas_call(
        last_kernel,
        out_shape=shape(rows, width),
        in_specs=[WHOLE] * 4 + [ANYWHERE],
        out_specs=ANYWHERE,
        scratch_shapes=[scratch(rows, width)] * 2
        + [scratch(tokens, 2 * features), scratch(2 * features, tokens)]
        + [scratch(tokens, tokens)] * 9
        + [scratch(rows, tokens)] * 2
        + [pltpu.SemaphoreType.DMA((1 + members,))],
        compiler_params=pltpu.CompilerParams(vmem_limit_bytes=51 * 2**20),
        cost_estimate=pl.CostEstimate(flops=5 * 10**9, bytes_accessed=0, transcendentals=0),
        name="whole_block",
    )(late, columns, turned, gram, tile)


def local(factor_inputs, gradients):
    features, members = factor_inputs.shape[2], lax.axis_size("grad")
    tokens = factor_inputs.shape[0] * lax.axis_size("dp")
    tile = gradients[0]
    if tokens < features * members and features % 128 == 0 and (members, lax.axis_size("dp")) == (8, 4):
        result = by_tokens(factor_inputs, tile)
    else:
        result = by_features(gather_block(factor_inputs), tile)
    return result.astype(jnp.bfloat16)[None]


def solution(mesh):
    placed = (P("dp", None, "grad"), P("dp", "grad", None))
    return jax.shard_map(
        local, mesh=mesh, in_specs=placed, out_specs=P("dp", "grad", None), check_vma=False
    )
```

```python
import functools

import jax
import jax.numpy as jnp
from jax import lax
from jax.experimental import pallas as pl
from jax.experimental.pallas import tpu as pltpu
from jax.sharding import PartitionSpec as P

ITERS = 4
DAMPING = 0.01
WHOLE = pl.BlockSpec(memory_space=pltpu.VMEM)
ANYWHERE = pl.BlockSpec(memory_space=pl.ANY)


def dot(a, b):
    return jnp.dot(a, b, preferred_element_type=jnp.float32)


def gather_block(factor_inputs):
    pieces = jnp.transpose(factor_inputs, (1, 0, 2))
    piece = lax.all_to_all(pieces, "dp", split_axis=0, concat_axis=1, tiled=True)[0]
    return lax.all_gather(piece, "grad", axis=1, tiled=True)


def by_features(columns, tile):
    tokens, width = columns.shape
    covariance = jnp.einsum("tr,tc->rc", columns, columns, preferred_element_type=jnp.float32) * (1.0 / tokens)
    damped = covariance + DAMPING * jnp.eye(width, dtype=jnp.float32)
    scale = 1.0 / jnp.max(jnp.sum(jnp.abs(damped), axis=1))
    image = scale * damped
    result = scale * tile.astype(jnp.float32)
    for step in range(ITERS):
        low = image.astype(jnp.bfloat16)
        result = 2.0 * result - dot(result.astype(jnp.bfloat16), low)
        if step < ITERS - 1:
            image = 2.0 * image - dot(low, low)
    return result


def split_kernel(fars, x_ref, *out_refs):
    replicas, tokens = len(out_refs), out_refs[0].shape[0]
    here = lax.axis_index("dp")
    x = x_ref[...]
    rows = lax.broadcasted_iota(jnp.int32, (tokens, tokens * replicas), 0)
    cols = lax.broadcasted_iota(jnp.int32, (tokens, tokens * replicas), 1)
    offset = cols - rows * replicas
    for far, out_ref in zip(fars, out_refs):
        choice = jnp.where(offset == lax.rem(here + far, replicas), 1.0, 0.0).astype(jnp.bfloat16)
        out_ref[...] = dot(choice, x).astype(jnp.bfloat16)


def split_blocks(factor_inputs, fars):
    tokens, blocks, features = factor_inputs.shape
    return pl.pallas_call(
        functools.partial(split_kernel, fars),
        out_shape=[jax.ShapeDtypeStruct((tokens, features), factor_inputs.dtype)] * blocks,
        in_specs=[WHOLE],
        out_specs=[WHOLE] * blocks,
        compiler_params=pltpu.CompilerParams(vmem_limit_bytes=16 * 2**20),
        name="split_blocks",
    )(factor_inputs.reshape(tokens * blocks, features))


def first_kernel(*refs):
    *pieces, columns, turned, gram = refs
    features = pieces[0].shape[1]
    for n, piece in enumerate(pieces):
        some = slice(n * features, (n + 1) * features)
        columns[:, some] = piece[...]
        turned[some, :] = piece[...].T
    gram[...] = dot(columns[...], turned[...])


def last_kernel(fars, late0, late1, x, xt, gram_in, tile_hbm, out_hbm, *refs):
    tile, out, late, late_t, k1, k2, e2, g, z, h, a, k, q, image, mixed, sems = refs
    load = pltpu.make_async_copy(tile_hbm, tile, sems.at[0])
    load.start()
    member = lax.axis_index("grad")
    tokens = x.shape[0]
    half = late.shape[1]
    features = half // 2
    halves = [slice(at, at + half) for at in range(0, tokens, half)]
    blocks = [slice(at, at + half) for at in range(0, x.shape[1], half)]
    chunks = [slice(at, at + 32) for at in range(0, tokens, 32)]

    def place(far):
        return pl.ds(pl.multiple_of((member ^ far) * features, features), features)

    def chosen(some):
        return jnp.concatenate([tile[:, place(far)] for far in some], axis=1)

    late[...] = jnp.concatenate([late0[...], late1[...]], axis=1)
    late_t[...] = late[...].T

    def symmetric(left, right, finish, *refs):
        for n, some in enumerate(halves):
            rows = slice(some.start, tokens)
            product = left(rows, some) if right is None else dot(left[rows, :], right[:, some])
            for r in chunks[some.start // 32 :]:
                values = finish(product[r.start - some.start : r.stop - some.start], r, some)
                for ref, value in zip(refs, values):
                    ref[r, some] = value.astype(jnp.bfloat16)
            for other in halves[n + 1 :]:
                for ref in refs:
                    ref[some, other] = ref[other, some].T

    def gram(rows, some):
        return lax.dot_general(late[rows, :], late[some, :], (((1,), (1,)), ((), ())), preferred_element_type=jnp.float32)

    symmetric(gram, None, lambda product, r, some: [(gram_in[r, some] + product) * (1.0 / tokens)], k1)

    column_sums, row_sums = [0.0] * (len(blocks) + 1), [0.0] * len(blocks)

    def add_sums(n, left, right):
        column = jnp.abs(dot(left, right))
        column_sums[n] = column_sums[n] + jnp.sum(column, axis=0, keepdims=True)
        for i, some in enumerate(blocks[: min(n, column.shape[0] // half)]):
            row_sums[i] = row_sums[i] + column[some, :features] + column[some, features:]

    def move(some):
        moved = dot(chosen(fars[:-2]), xt[:, some]) + dot(chosen(fars[-2:]), late_t[:, some])
        image[:, some] = moved.astype(jnp.bfloat16)

    for n, some in enumerate(blocks):
        add_sums(n, xt[: some.stop, :], x[:, some])
    symmetric(k1, k1, lambda product, r, some: [product], k2)
    add_sums(len(blocks), xt[...], late[...])
    column_sums[-1] = column_sums[-1] + jnp.sum(jnp.abs(dot(late_t[...], late[...])), axis=0, keepdims=True)
    load.wait()
    move(halves[0])

    largest = column_sums[-1]
    for column, row in zip(column_sums[:-1], row_sums):
        largest = jnp.maximum(largest, column + jnp.sum(row.T, axis=0, keepdims=True))
    c = 1.0 / (jnp.max(largest) * (1.0 / tokens) + DAMPING)
    eps = 1.0 - c * DAMPING
    eps2 = eps * eps
    zeta = eps2 * eps2
    eps8 = zeta * zeta
    e2_1, e2_2 = -2.0 * eps * c, c * c
    g_1 = -(1.0 + eps) * c
    g_m = eps2 + (1.0 + eps) * eps + eps
    h_m = zeta + (1.0 + eps2) * eps2 + eps2
    k_m = eps8 + (1.0 + zeta) * zeta + zeta + 1.0 + eps8
    k_z = 1.0 + 3.0 * zeta
    a_m = g_m * h_m
    beta = (1.0 + zeta) * (1.0 + eps8)
    q_m = a_m * k_m + beta * g_m + (1.0 + eps2) * beta
    last = -c * c * (1.0 / tokens)
    q_m = q_m * last
    p = c * (1.0 + eps) * (1.0 + eps2) * beta

    def wide(ref, r, some):
        return ref[r, some].astype(jnp.float32)

    for some in halves:
        for r in chunks:
            first = wide(k1, r, some)
            square = e2_1 * first + e2_2 * wide(k2, r, some)
            e2[r, some] = square.astype(jnp.bfloat16)
            g[r, some] = (square + g_1 * first).astype(jnp.bfloat16)

    def fourth(product, r, some):
        square = wide(e2, r, some)
        value = 2.0 * eps2 * square + product
        return value, value + (1.0 + eps2) * square

    symmetric(e2, e2, fourth, z, h)
    for some in halves[1:]:
        move(some)
    symmetric(z, z, lambda product, r, some: [product + k_z * wide(z, r, some)], k)
    for some in halves:
        product = dot(g[...], h[:, some])
        for r in chunks:
            a[r, some] = (product[r] + g_m * wide(h, r, some) + h_m * wide(g, r, some)).astype(jnp.bfloat16)
    q_k, q_a, q_g = last * a_m, last * k_m, last * beta
    for some in halves:
        product = dot(k[...], a[:, some])
        for r in chunks:
            rest = q_k * wide(k, r, some) + q_a * wide(a, r, some) + q_g * wide(g, r, some)
            q[r, some] = (last * product[r] + rest).astype(jnp.bfloat16)
    for some in halves:
        product = dot(image[...], q[:, some])
        mixed[:, some] = (product + q_m * image[:, some].astype(jnp.float32)).astype(jnp.bfloat16)
    stores = []
    for n in range(len(blocks) + 1):
        moved = dot(mixed[...], late[...] if n == len(blocks) else x[:, blocks[n]])
        for one in (0, 1):
            here = place(fars[2 * n + one])
            kept = p * tile[:, here].astype(jnp.float32)
            out[:, here] = (kept + moved[:, one * features : (one + 1) * features]).astype(jnp.bfloat16)
            store = pltpu.make_async_copy(out.at[:, here], out_hbm.at[:, here], sems.at[1 + len(stores)])
            store.start()
            stores.append(store)
    for store in stores:
        store.wait()


def by_tokens(factor_inputs, tile):
    members, replicas = lax.axis_size("grad"), lax.axis_size("dp")
    rows, width = tile.shape
    features = factor_inputs.shape[2]
    tokens = factor_inputs.shape[0] * replicas

    def shape(*sizes, kind=jnp.bfloat16):
        return jax.ShapeDtypeStruct(sizes, kind)

    def scratch(*sizes):
        return pltpu.VMEM(sizes, jnp.bfloat16)

    def swap(value, far):
        return lax.ppermute(value, "grad", [(i, i ^ far) for i in range(members)])

    order = (0, 2, 1, 3)
    parts = dict(zip(order, split_blocks(factor_inputs, order)))
    for far in order[1:]:
        parts[far] = lax.ppermute(parts[far], "dp", [(i, (i + far) % replicas) for i in range(replicas)])
    own = jnp.concatenate([parts[far] for far in order], axis=0)
    fars = (0, 1, 6, 7, 4, 2, 5, 3)
    pieces = {0: own}
    for far in (2, 4, 6):
        pieces[far] = swap(own, far)
    for far in (0, 2, 4, 6):
        pieces[far + 1] = swap(pieces[far], 1)
    pieces = [pieces[far] for far in fars]
    early = width - 2 * features
    columns, turned, gram = pl.pallas_call(
        first_kernel,
        out_shape=[shape(tokens, early), shape(early, tokens), shape(tokens, tokens, kind=jnp.float32)],
        in_specs=[WHOLE] * 6,
        out_specs=[WHOLE] * 3,
        compiler_params=pltpu.CompilerParams(vmem_limit_bytes=16 * 2**20),
        cost_estimate=pl.CostEstimate(flops=4 * 10**8, bytes_accessed=0, transcendentals=0),
        name="first_pieces",
    )(*pieces[:6])
    return pl.pallas_call(
        functools.partial(last_kernel, fars),
        out_shape=shape(rows, width),
        in_specs=[WHOLE] * 5 + [ANYWHERE],
        out_specs=ANYWHERE,
        scratch_shapes=[scratch(rows, width)] * 2
        + [scratch(tokens, 2 * features), scratch(2 * features, tokens)]
        + [scratch(tokens, tokens)] * 9
        + [scratch(rows, tokens)] * 2
        + [pltpu.SemaphoreType.DMA((1 + members,))],
        compiler_params=pltpu.CompilerParams(vmem_limit_bytes=51 * 2**20),
        cost_estimate=pl.CostEstimate(flops=5 * 10**9, bytes_accessed=0, transcendentals=0),
        name="whole_block",
    )(*pieces[6:], columns, turned, gram, tile)


def local(factor_inputs, gradients):
    features, members = factor_inputs.shape[2], lax.axis_size("grad")
    tokens = factor_inputs.shape[0] * lax.axis_size("dp")
    tile = gradients[0]
    if tokens < features * members and features % 128 == 0 and (members, lax.axis_size("dp")) == (8, 4):
        result = by_tokens(factor_inputs, tile)
    else:
        result = by_features(gather_block(factor_inputs), tile)
    return result.astype(jnp.bfloat16)[None]


def solution(mesh):
    placed = (P("dp", None, "grad"), P("dp", "grad", None))
    return jax.shard_map(
        local, mesh=mesh, in_specs=placed, out_specs=P("dp", "grad", None), check_vma=False
    )
```

```python
import functools

import jax
import jax.numpy as jnp
from jax import lax
from jax.experimental import pallas as pl
from jax.experimental.pallas import tpu as pltpu
from jax.sharding import PartitionSpec as P

ITERS = 4
DAMPING = 0.01
WHOLE = pl.BlockSpec(memory_space=pltpu.VMEM)
ANYWHERE = pl.BlockSpec(memory_space=pl.ANY)


def dot(a, b):
    return jnp.dot(a, b, preferred_element_type=jnp.float32)


def gather_block(factor_inputs):
    pieces = jnp.transpose(factor_inputs, (1, 0, 2))
    piece = lax.all_to_all(pieces, "dp", split_axis=0, concat_axis=1, tiled=True)[0]
    return lax.all_gather(piece, "grad", axis=1, tiled=True)


def by_features(columns, tile):
    tokens, width = columns.shape
    covariance = jnp.einsum("tr,tc->rc", columns, columns, preferred_element_type=jnp.float32) * (1.0 / tokens)
    damped = covariance + DAMPING * jnp.eye(width, dtype=jnp.float32)
    scale = 1.0 / jnp.max(jnp.sum(jnp.abs(damped), axis=1))
    image = scale * damped
    result = scale * tile.astype(jnp.float32)
    for step in range(ITERS):
        low = image.astype(jnp.bfloat16)
        result = 2.0 * result - dot(result.astype(jnp.bfloat16), low)
        if step < ITERS - 1:
            image = 2.0 * image - dot(low, low)
    return result


def split_kernel(fars, x_ref, *out_refs):
    replicas, tokens = len(out_refs), out_refs[0].shape[0]
    here = lax.axis_index("dp")
    x = x_ref[...]
    rows = lax.broadcasted_iota(jnp.int32, (tokens, tokens * replicas), 0)
    cols = lax.broadcasted_iota(jnp.int32, (tokens, tokens * replicas), 1)
    offset = cols - rows * replicas
    for far, out_ref in zip(fars, out_refs):
        choice = jnp.where(offset == lax.rem(here + far, replicas), 1.0, 0.0).astype(jnp.bfloat16)
        out_ref[...] = dot(choice, x).astype(jnp.bfloat16)


def split_blocks(factor_inputs, fars):
    tokens, blocks, features = factor_inputs.shape
    return pl.pallas_call(
        functools.partial(split_kernel, fars),
        out_shape=[jax.ShapeDtypeStruct((tokens, features), factor_inputs.dtype)] * blocks,
        in_specs=[WHOLE],
        out_specs=[WHOLE] * blocks,
        compiler_params=pltpu.CompilerParams(vmem_limit_bytes=16 * 2**20),
        name="split_blocks",
    )(factor_inputs.reshape(tokens * blocks, features))


def add_sums(sums, earlier_t, columns, columns_t):
    half = columns.shape[1]
    mine = jnp.sum(jnp.abs(dot(columns_t, columns)), axis=0, keepdims=True)
    sums = list(sums)
    at = 0
    for before in earlier_t:
        block = jnp.abs(dot(before, columns))
        mine = mine + jnp.sum(block, axis=0, keepdims=True)
        for top in range(0, block.shape[0], half):
            part = block[top : top + half]
            part = functools.reduce(jnp.add, [part[:, side : side + 128] for side in range(0, half, 128)])
            sums[at] = sums[at] + jnp.sum(part.T, axis=0, keepdims=True)
            at += 1
    return sums + [mine]


def add_kernel(*refs):
    *refs, columns, turned, gram, sums_out, zeros = refs
    count = columns.shape[1] // refs[0].shape[1]
    pieces, before = refs[:count], refs[count:]
    features = pieces[0].shape[1]
    for n, piece in enumerate(pieces):
        some = slice(n * features, (n + 1) * features)
        columns[:, some] = piece[...]
        turned[some, :] = piece[...].T
    product = dot(columns[...], turned[...])
    sums, earlier = [], []
    if before:
        turned_in, gram_in, sums_in = before
        product = product + gram_in[...]
        sums, earlier = [sums_in[n : n + 1, :] for n in range(sums_in.shape[0])], [turned_in]
    gram[...] = product
    for at in range(0, columns.shape[1], 2 * features):
        some = slice(at, at + 2 * features)
        lefts = [ref[...] for ref in earlier] + ([turned[:at, :]] if at else [])
        sums = add_sums(sums, lefts, columns[:, some], turned[some, :])
    for n, value in enumerate(sums):
        sums_out[n : n + 1, :] = value
    zeros[...] = jnp.zeros_like(zeros)


def last_kernel(fars, late0, late1, x0, x1, xt0, xt1, gram_in, sums_in, tile_hbm, out_hbm, *refs):
    tile, out, late, late_t, k1, k2, e2, g, z, h, a, k, q, image, mixed, sems = refs
    load = pltpu.make_async_copy(tile_hbm, tile, sems.at[0])
    load.start()
    member = lax.axis_index("grad")
    tokens = x0.shape[0]
    half = late.shape[1]
    features = half // 2
    halves = [slice(at, at + half) for at in range(0, tokens, half)]
    chunks = [slice(at, at + 32) for at in range(0, tokens, 32)]

    def place(far):
        return pl.ds(pl.multiple_of((member ^ far) * features, features), features)

    def chosen(some):
        return jnp.concatenate([tile[:, place(far)] for far in some], axis=1)

    late[...] = jnp.concatenate([late0[...], late1[...]], axis=1)
    late_t[...] = late[...].T

    def symmetric(left, right, finish, *refs):
        for n, some in enumerate(halves):
            rows = slice(some.start, tokens)
            product = left(rows, some) if right is None else dot(left[rows, :], right[:, some])
            for r in chunks[some.start // 32 :]:
                values = finish(product[r.start - some.start : r.stop - some.start], r, some)
                for ref, value in zip(refs, values):
                    ref[r, some] = value.astype(jnp.bfloat16)
            for other in halves[n + 1 :]:
                for ref in refs:
                    ref[some, other] = ref[other, some].T

    def gram(rows, some):
        return lax.dot_general(late[rows, :], late[some, :], (((1,), (1,)), ((), ())), preferred_element_type=jnp.float32)

    symmetric(gram, None, lambda product, r, some: [(gram_in[r, some] + product) * (1.0 / tokens)], k1)

    def move(some):
        moved, at = 0.0, 0
        for ref in (xt0, xt1, late_t):
            count = ref.shape[0] // features
            moved = moved + dot(chosen(fars[at : at + count]), ref[:, some])
            at += count
        image[:, some] = moved.astype(jnp.bfloat16)

    symmetric(k1, k1, lambda product, r, some: [product], k2)
    sums = [sums_in[n : n + 1, :] for n in range(sums_in.shape[0])]
    sums = add_sums(sums, [xt0[...], xt1[...]], late[...], late_t[...])
    load.wait()
    move(halves[0])

    largest = functools.reduce(jnp.maximum, sums)
    c = 1.0 / (jnp.max(largest) * (1.0 / tokens) + DAMPING)
    eps = 1.0 - c * DAMPING
    eps2 = eps * eps
    zeta = eps2 * eps2
    eps8 = zeta * zeta
    e2_1, e2_2 = -2.0 * eps * c, c * c
    g_1 = -(1.0 + eps) * c
    g_m = eps2 + (1.0 + eps) * eps + eps
    h_m = zeta + (1.0 + eps2) * eps2 + eps2
    k_m = eps8 + (1.0 + zeta) * zeta + zeta + 1.0 + eps8
    k_z = 1.0 + 3.0 * zeta
    a_m = g_m * h_m
    beta = (1.0 + zeta) * (1.0 + eps8)
    q_m = a_m * k_m + beta * g_m + (1.0 + eps2) * beta
    last = -c * c * (1.0 / tokens)
    q_m = q_m * last
    p = c * (1.0 + eps) * (1.0 + eps2) * beta

    def wide(ref, r, some):
        return ref[r, some].astype(jnp.float32)

    for some in halves:
        for r in chunks:
            first = wide(k1, r, some)
            square = e2_1 * first + e2_2 * wide(k2, r, some)
            e2[r, some] = square.astype(jnp.bfloat16)
            g[r, some] = (square + g_1 * first).astype(jnp.bfloat16)

    def fourth(product, r, some):
        square = wide(e2, r, some)
        value = 2.0 * eps2 * square + product
        return value, value + (1.0 + eps2) * square

    symmetric(e2, e2, fourth, z, h)
    for some in halves[1:]:
        move(some)
    symmetric(z, z, lambda product, r, some: [product + k_z * wide(z, r, some)], k)
    for some in halves:
        product = dot(g[...], h[:, some])
        for r in chunks:
            a[r, some] = (product[r] + g_m * wide(h, r, some) + h_m * wide(g, r, some)).astype(jnp.bfloat16)
    q_k, q_a, q_g = last * a_m, last * k_m, last * beta
    for some in halves:
        product = dot(k[...], a[:, some])
        for r in chunks:
            rest = q_k * wide(k, r, some) + q_a * wide(a, r, some) + q_g * wide(g, r, some)
            q[r, some] = (last * product[r] + rest).astype(jnp.bfloat16)
    for some in halves:
        product = dot(image[...], q[:, some])
        mixed[:, some] = (product + q_m * image[:, some].astype(jnp.float32)).astype(jnp.bfloat16)
    stores = []
    blocks = [ref[:, at : at + half] for ref in (x0, x1, late) for at in range(0, ref.shape[1], half)]
    for n, block in enumerate(blocks):
        moved = dot(mixed[...], block)
        for one in (0, 1):
            here = place(fars[2 * n + one])
            kept = p * tile[:, here].astype(jnp.float32)
            out[:, here] = (kept + moved[:, one * features : (one + 1) * features]).astype(jnp.bfloat16)
            store = pltpu.make_async_copy(out.at[:, here], out_hbm.at[:, here], sems.at[1 + len(stores)])
            store.start()
            stores.append(store)
    for store in stores:
        store.wait()


def by_tokens(factor_inputs, tile):
    members, replicas = lax.axis_size("grad"), lax.axis_size("dp")
    rows, width = tile.shape
    features = factor_inputs.shape[2]
    tokens = factor_inputs.shape[0] * replicas

    def shape(*sizes, kind=jnp.bfloat16):
        return jax.ShapeDtypeStruct(sizes, kind)

    def scratch(*sizes):
        return pltpu.VMEM(sizes, jnp.bfloat16)

    def swap(value, far):
        return lax.ppermute(value, "grad", [(i, i ^ far) for i in range(members)])

    parts = list(split_blocks(factor_inputs, range(replicas)))
    for far in range(1, replicas):
        parts[far] = lax.ppermute(parts[far], "dp", [(i, (i + far) % replicas) for i in range(replicas)])
    own = jnp.concatenate(parts, axis=0)
    here = {0: own, 1: swap(own, 1)}
    for far in (6, 2, 4):
        here[far] = swap(own, far)
    for far in (6, 2):
        here[far + 1] = swap(here[far], 1)

    def add(name, pieces, *before):
        wide = len(pieces) * features
        blocks = wide // (2 * features) + (before[-1].shape[0] if before else 0)
        return pl.pallas_call(
            add_kernel,
            out_shape=[
                shape(tokens, wide),
                shape(wide, tokens),
                shape(tokens, tokens, kind=jnp.float32),
                shape(blocks, 2 * features, kind=jnp.float32),
                shape(1, features),
            ],
            in_specs=[WHOLE] * (len(pieces) + len(before)),
            out_specs=[WHOLE] * 5,
            compiler_params=pltpu.CompilerParams(vmem_limit_bytes=16 * 2**20),
            cost_estimate=pl.CostEstimate(flops=6 * 10**8, bytes_accessed=0, transcendentals=0),
            name=name,
        )(*pieces, *before)

    fars = (0, 1, 6, 2, 7, 4, 3, 5)
    x0, xt0, gram, sums, zeros = add("first_pieces", [here[far] for far in fars[:4]])
    here[5] = swap(here[4] + zeros, 1)
    x1, xt1, gram, sums, _ = add("next_pieces", [here[far] for far in fars[4:6]], xt0, gram, sums)
    return pl.pallas_call(
        functools.partial(last_kernel, fars),
        out_shape=shape(rows, width),
        in_specs=[WHOLE] * 8 + [ANYWHERE],
        out_specs=ANYWHERE,
        scratch_shapes=[scratch(rows, width)] * 2
        + [scratch(tokens, 2 * features), scratch(2 * features, tokens)]
        + [scratch(tokens, tokens)] * 9
        + [scratch(rows, tokens)] * 2
        + [pltpu.SemaphoreType.DMA((1 + members,))],
        compiler_params=pltpu.CompilerParams(vmem_limit_bytes=51 * 2**20),
        cost_estimate=pl.CostEstimate(flops=5 * 10**9, bytes_accessed=0, transcendentals=0),
        name="whole_block",
    )(here[3], here[5], x0, x1, xt0, xt1, gram, sums, tile)


def local(factor_inputs, gradients):
    features, members = factor_inputs.shape[2], lax.axis_size("grad")
    tokens = factor_inputs.shape[0] * lax.axis_size("dp")
    tile = gradients[0]
    if tokens < features * members and features % 128 == 0 and (members, lax.axis_size("dp")) == (8, 4):
        result = by_tokens(factor_inputs, tile)
    else:
        result = by_features(gather_block(factor_inputs), tile)
    return result.astype(jnp.bfloat16)[None]


def solution(mesh):
    placed = (P("dp", None, "grad"), P("dp", "grad", None))
    return jax.shard_map(
        local, mesh=mesh, in_specs=placed, out_specs=P("dp", "grad", None), check_vma=False
    )
```

```python
import functools

import jax
import jax.numpy as jnp
from jax import lax
from jax.experimental import pallas as pl
from jax.experimental.pallas import tpu as pltpu
from jax.sharding import PartitionSpec as P

ITERS = 4
DAMPING = 0.01
LOADS = 8
WHOLE = pl.BlockSpec(memory_space=pltpu.VMEM)
ANYWHERE = pl.BlockSpec(memory_space=pl.ANY)


def dot(a, b):
    return jnp.dot(a, b, preferred_element_type=jnp.float32)


def gather_block(factor_inputs):
    pieces = jnp.transpose(factor_inputs, (1, 0, 2))
    piece = lax.all_to_all(pieces, "dp", split_axis=0, concat_axis=1, tiled=True)[0]
    return lax.all_gather(piece, "grad", axis=1, tiled=True)


def by_features(columns, tile):
    tokens, width = columns.shape
    covariance = jnp.einsum("tr,tc->rc", columns, columns, preferred_element_type=jnp.float32) * (1.0 / tokens)
    damped = covariance + DAMPING * jnp.eye(width, dtype=jnp.float32)
    scale = 1.0 / jnp.max(jnp.sum(jnp.abs(damped), axis=1))
    image = scale * damped
    result = scale * tile.astype(jnp.float32)
    for step in range(ITERS):
        low = image.astype(jnp.bfloat16)
        result = 2.0 * result - dot(result.astype(jnp.bfloat16), low)
        if step < ITERS - 1:
            image = 2.0 * image - dot(low, low)
    return result


def split_kernel(fars, x_ref, *out_refs):
    replicas, tokens = len(out_refs), out_refs[0].shape[0]
    here = lax.axis_index("dp")
    x = x_ref[...]
    rows = lax.broadcasted_iota(jnp.int32, (tokens, tokens * replicas), 0)
    cols = lax.broadcasted_iota(jnp.int32, (tokens, tokens * replicas), 1)
    offset = cols - rows * replicas
    for far, out_ref in zip(fars, out_refs):
        choice = jnp.where(offset == lax.rem(here + far, replicas), 1.0, 0.0).astype(jnp.bfloat16)
        out_ref[...] = dot(choice, x).astype(jnp.bfloat16)


def split_blocks(factor_inputs, fars):
    tokens, blocks, features = factor_inputs.shape
    return pl.pallas_call(
        functools.partial(split_kernel, fars),
        out_shape=[jax.ShapeDtypeStruct((tokens, features), factor_inputs.dtype)] * blocks,
        in_specs=[WHOLE],
        out_specs=[WHOLE] * blocks,
        compiler_params=pltpu.CompilerParams(vmem_limit_bytes=16 * 2**20),
        name="split_blocks",
    )(factor_inputs.reshape(tokens * blocks, features))


def add_sums(sums, before_t, columns, columns_t):
    half = columns.shape[1]
    mine = jnp.sum(jnp.abs(dot(columns_t, columns)), axis=0, keepdims=True)
    sums = list(sums)
    if before_t is not None:
        block = jnp.abs(dot(before_t, columns))
        mine = mine + jnp.sum(block, axis=0, keepdims=True)
        for n in range(len(sums)):
            part = block[n * half : (n + 1) * half]
            part = functools.reduce(jnp.add, [part[:, side : side + 128] for side in range(0, half, 128)])
            sums[n] = sums[n] + jnp.sum(part.T, axis=0, keepdims=True)
    return sums + [mine]


def add_kernel(*refs):
    *pieces, columns, turned, gram, sums_out = refs
    features = pieces[0].shape[1]
    for n, piece in enumerate(pieces):
        some = slice(n * features, (n + 1) * features)
        columns[:, some] = piece[...]
        turned[some, :] = piece[...].T
    gram[...] = dot(columns[...], turned[...])
    sums = []
    for at in range(0, columns.shape[1], 2 * features):
        some = slice(at, at + 2 * features)
        sums = add_sums(sums, turned[:at, :] if at else None, columns[:, some], turned[some, :])
    for n, value in enumerate(sums):
        sums_out[n : n + 1, :] = value


def last_kernel(fars, late0, late1, x, xt, gram_in, sums_in, tile_hbm, out_hbm, *refs):
    tile, out, late, late_t, k1, k2, e2, g, z, h, a, k, q, image, mixed, sems = refs
    loads = []
    step = tile.shape[0] // LOADS
    for n in range(LOADS):
        some = pl.ds(n * step, step)
        loads.append(pltpu.make_async_copy(tile_hbm.at[some, :], tile.at[some, :], sems.at[n]))
        loads[-1].start()
    member = lax.axis_index("grad")
    tokens = x.shape[0]
    half = late.shape[1]
    features = half // 2
    halves = [slice(at, at + half) for at in range(0, tokens, half)]
    chunks = [slice(at, at + 32) for at in range(0, tokens, 32)]

    def place(far):
        return pl.ds(pl.multiple_of((member ^ far) * features, features), features)

    def chosen(some):
        return jnp.concatenate([tile[:, place(far)] for far in some], axis=1)

    late[...] = jnp.concatenate([late0[...], late1[...]], axis=1)
    late_t[...] = late[...].T

    def symmetric(left, right, finish, *refs):
        for n, some in enumerate(halves):
            rows = slice(some.start, tokens)
            product = left(rows, some) if right is None else dot(left[rows, :], right[:, some])
            for r in chunks[some.start // 32 :]:
                values = finish(product[r.start - some.start : r.stop - some.start], r, some)
                for ref, value in zip(refs, values):
                    ref[r, some] = value.astype(jnp.bfloat16)
            for other in halves[n + 1 :]:
                for ref in refs:
                    ref[some, other] = ref[other, some].T

    def gram(rows, some):
        return lax.dot_general(late[rows, :], late[some, :], (((1,), (1,)), ((), ())), preferred_element_type=jnp.float32)

    symmetric(gram, None, lambda product, r, some: [(gram_in[r, some] + product) * (1.0 / tokens)], k1)

    def move(some):
        moved = dot(chosen(fars[:-2]), xt[:, some]) + dot(chosen(fars[-2:]), late_t[:, some])
        image[:, some] = moved.astype(jnp.bfloat16)

    symmetric(k1, k1, lambda product, r, some: [product], k2)
    sums = [sums_in[n : n + 1, :] for n in range(sums_in.shape[0])]
    sums = add_sums(sums, xt[...], late[...], late_t[...])
    for load in loads:
        load.wait()
    move(halves[0])

    largest = functools.reduce(jnp.maximum, sums)
    c = 1.0 / (jnp.max(largest) * (1.0 / tokens) + DAMPING)
    eps = 1.0 - c * DAMPING
    eps2 = eps * eps
    zeta = eps2 * eps2
    eps8 = zeta * zeta
    e2_1, e2_2 = -2.0 * eps * c, c * c
    g_1 = -(1.0 + eps) * c
    g_m = eps2 + (1.0 + eps) * eps + eps
    h_m = zeta + (1.0 + eps2) * eps2 + eps2
    k_m = eps8 + (1.0 + zeta) * zeta + zeta + 1.0 + eps8
    k_z = 1.0 + 3.0 * zeta
    a_m = g_m * h_m
    beta = (1.0 + zeta) * (1.0 + eps8)
    q_m = a_m * k_m + beta * g_m + (1.0 + eps2) * beta
    last = -c * c * (1.0 / tokens)
    q_m = q_m * last
    p = c * (1.0 + eps) * (1.0 + eps2) * beta

    def wide(ref, r, some):
        return ref[r, some].astype(jnp.float32)

    for some in halves:
        for r in chunks:
            first = wide(k1, r, some)
            square = e2_1 * first + e2_2 * wide(k2, r, some)
            e2[r, some] = square.astype(jnp.bfloat16)
            g[r, some] = (square + g_1 * first).astype(jnp.bfloat16)

    def fourth(product, r, some):
        square = wide(e2, r, some)
        value = 2.0 * eps2 * square + product
        return value, value + (1.0 + eps2) * square

    symmetric(e2, e2, fourth, z, h)
    for some in halves[1:]:
        move(some)
    symmetric(z, z, lambda product, r, some: [product + k_z * wide(z, r, some)], k)
    for some in halves:
        product = dot(g[...], h[:, some])
        for r in chunks:
            a[r, some] = (product[r] + g_m * wide(h, r, some) + h_m * wide(g, r, some)).astype(jnp.bfloat16)
    q_k, q_a, q_g = last * a_m, last * k_m, last * beta
    for some in halves:
        product = dot(k[...], a[:, some])
        for r in chunks:
            rest = q_k * wide(k, r, some) + q_a * wide(a, r, some) + q_g * wide(g, r, some)
            q[r, some] = (last * product[r] + rest).astype(jnp.bfloat16)
    for some in halves:
        product = dot(image[...], q[:, some])
        mixed[:, some] = (product + q_m * image[:, some].astype(jnp.float32)).astype(jnp.bfloat16)
    stores = []
    blocks = [x[:, at : at + half] for at in range(0, x.shape[1], half)] + [late[...]]
    for n, block in enumerate(blocks):
        moved = dot(mixed[...], block)
        parts = 3 if n == len(blocks) - 1 else 1
        step = moved.shape[0] // parts
        for at in range(0, parts * step, step):
            r = slice(at, at + step)
            for one in (0, 1):
                here = place(fars[2 * n + one])
                kept = p * tile[r, here].astype(jnp.float32)
                out[r, here] = (kept + moved[r, one * features : (one + 1) * features]).astype(jnp.bfloat16)
                store = pltpu.make_async_copy(out.at[r, here], out_hbm.at[r, here], sems.at[LOADS + len(stores)])
                store.start()
                stores.append(store)
    for store in stores:
        store.wait()


def by_tokens(factor_inputs, tile):
    members, replicas = lax.axis_size("grad"), lax.axis_size("dp")
    rows, width = tile.shape
    features = factor_inputs.shape[2]
    tokens = factor_inputs.shape[0] * replicas

    def shape(*sizes, kind=jnp.bfloat16):
        return jax.ShapeDtypeStruct(sizes, kind)

    def scratch(*sizes):
        return pltpu.VMEM(sizes, jnp.bfloat16)

    def swap(value, far):
        return lax.ppermute(value, "grad", [(i, i ^ far) for i in range(members)])

    parts = list(split_blocks(factor_inputs, range(replicas)))
    for far in range(1, replicas):
        parts[far] = lax.ppermute(parts[far], "dp", [(i, (i + far) % replicas) for i in range(replicas)])
    own = jnp.concatenate(parts, axis=0)
    fars = (0, 1, 6, 7, 2, 4, 3, 5)
    pieces = {0: own}
    for far in (2, 4, 6):
        pieces[far] = swap(own, far)
    for far in (0, 2, 4, 6):
        pieces[far + 1] = swap(pieces[far], 1)
    pieces = [pieces[far] for far in fars]
    early = width - 2 * features
    first = pl.pallas_call(
        add_kernel,
        out_shape=[
            shape(tokens, early),
            shape(early, tokens),
            shape(tokens, tokens, kind=jnp.float32),
            shape(early // (2 * features), 2 * features, kind=jnp.float32),
        ],
        in_specs=[WHOLE] * 6,
        out_specs=[WHOLE] * 4,
        compiler_params=pltpu.CompilerParams(vmem_limit_bytes=16 * 2**20),
        cost_estimate=pl.CostEstimate(flops=8 * 10**8, bytes_accessed=0, transcendentals=0),
        name="first_pieces",
    )(*pieces[:6])
    return pl.pallas_call(
        functools.partial(last_kernel, fars),
        out_shape=shape(rows, width),
        in_specs=[WHOLE] * 6 + [ANYWHERE],
        out_specs=ANYWHERE,
        scratch_shapes=[scratch(rows, width)] * 2
        + [scratch(tokens, 2 * features), scratch(2 * features, tokens)]
        + [scratch(tokens, tokens)] * 9
        + [scratch(rows, tokens)] * 2
        + [pltpu.SemaphoreType.DMA((LOADS + members + 4,))],
        compiler_params=pltpu.CompilerParams(vmem_limit_bytes=51 * 2**20),
        cost_estimate=pl.CostEstimate(flops=5 * 10**9, bytes_accessed=0, transcendentals=0),
        name="whole_block",
    )(*pieces[6:], *first, tile)


def local(factor_inputs, gradients):
    features, members = factor_inputs.shape[2], lax.axis_size("grad")
    tokens = factor_inputs.shape[0] * lax.axis_size("dp")
    tile = gradients[0]
    if tokens < features * members and features % 128 == 0 and (members, lax.axis_size("dp")) == (8, 4):
        result = by_tokens(factor_inputs, tile)
    else:
        result = by_features(gather_block(factor_inputs), tile)
    return result.astype(jnp.bfloat16)[None]


def solution(mesh):
    placed = (P("dp", None, "grad"), P("dp", "grad", None))
    return jax.shard_map(
        local, mesh=mesh, in_specs=placed, out_specs=P("dp", "grad", None), check_vma=False
    )
```

```python
import functools

import jax
import jax.numpy as jnp
from jax import lax
from jax.experimental import pallas as pl
from jax.experimental.pallas import tpu as pltpu
from jax.sharding import PartitionSpec as P

ITERS = 4
DAMPING = 0.01
WHOLE = pl.BlockSpec(memory_space=pltpu.VMEM)
ANYWHERE = pl.BlockSpec(memory_space=pl.ANY)


def dot(a, b):
    return jnp.dot(a, b, preferred_element_type=jnp.float32)


def gather_block(factor_inputs):
    pieces = jnp.transpose(factor_inputs, (1, 0, 2))
    piece = lax.all_to_all(pieces, "dp", split_axis=0, concat_axis=1, tiled=True)[0]
    return lax.all_gather(piece, "grad", axis=1, tiled=True)


def by_features(columns, tile):
    tokens, width = columns.shape
    covariance = jnp.einsum("tr,tc->rc", columns, columns, preferred_element_type=jnp.float32) * (1.0 / tokens)
    damped = covariance + DAMPING * jnp.eye(width, dtype=jnp.float32)
    scale = 1.0 / jnp.max(jnp.sum(jnp.abs(damped), axis=1))
    image = scale * damped
    result = scale * tile.astype(jnp.float32)
    for step in range(ITERS):
        low = image.astype(jnp.bfloat16)
        result = 2.0 * result - dot(result.astype(jnp.bfloat16), low)
        if step < ITERS - 1:
            image = 2.0 * image - dot(low, low)
    return result


def split_kernel(fars, x_ref, *out_refs):
    replicas, tokens = len(out_refs), out_refs[0].shape[0]
    here = lax.axis_index("dp")
    x = x_ref[...]
    rows = lax.broadcasted_iota(jnp.int32, (tokens, tokens * replicas), 0)
    cols = lax.broadcasted_iota(jnp.int32, (tokens, tokens * replicas), 1)
    offset = cols - rows * replicas
    for far, out_ref in zip(fars, out_refs):
        choice = jnp.where(offset == lax.rem(here + far, replicas), 1.0, 0.0).astype(jnp.bfloat16)
        out_ref[...] = dot(choice, x).astype(jnp.bfloat16)


def split_blocks(factor_inputs, fars):
    tokens, blocks, features = factor_inputs.shape
    return pl.pallas_call(
        functools.partial(split_kernel, fars),
        out_shape=[jax.ShapeDtypeStruct((tokens, features), factor_inputs.dtype)] * blocks,
        in_specs=[WHOLE],
        out_specs=[WHOLE] * blocks,
        compiler_params=pltpu.CompilerParams(vmem_limit_bytes=16 * 2**20),
        name="split_blocks",
    )(factor_inputs.reshape(tokens * blocks, features))


def add_sums(sums, before_t, columns, columns_t):
    half = columns.shape[1]
    mine = jnp.sum(jnp.abs(dot(columns_t, columns)), axis=0, keepdims=True)
    sums = list(sums)
    if before_t is not None:
        block = jnp.abs(dot(before_t, columns))
        mine = mine + jnp.sum(block, axis=0, keepdims=True)
        for n in range(len(sums)):
            part = block[n * half : (n + 1) * half]
            part = functools.reduce(jnp.add, [part[:, side : side + 128] for side in range(0, half, 128)])
            sums[n] = sums[n] + jnp.sum(part.T, axis=0, keepdims=True)
    return sums + [mine]


def add_kernel(*refs):
    *pieces, columns, turned, gram, sums_out = refs
    features = pieces[0].shape[1]
    for n, piece in enumerate(pieces):
        some = slice(n * features, (n + 1) * features)
        columns[:, some] = piece[...]
        turned[some, :] = piece[...].T
    gram[...] = dot(columns[...], turned[...])
    sums = []
    for at in range(0, columns.shape[1], 2 * features):
        some = slice(at, at + 2 * features)
        sums = add_sums(sums, turned[:at, :] if at else None, columns[:, some], turned[some, :])
    for n, value in enumerate(sums):
        sums_out[n : n + 1, :] = value


def last_kernel(fars, late0, late1, x, xt, gram_in, sums_in, tile_hbm, out_hbm, *refs):
    tile, out, late, late_t, k1, k2, e2, g, z, h, a, k, q, image, mixed, sems = refs
    load = pltpu.make_async_copy(tile_hbm, tile, sems.at[0])
    load.start()
    member = lax.axis_index("grad")
    tokens = x.shape[0]
    half = late.shape[1]
    features = half // 2
    halves = [slice(at, at + half) for at in range(0, tokens, half)]
    chunks = [slice(at, at + 32) for at in range(0, tokens, 32)]

    def place(far):
        return pl.ds(pl.multiple_of((member ^ far) * features, features), features)

    def chosen(some):
        return jnp.concatenate([tile[:, place(far)] for far in some], axis=1)

    late[...] = jnp.concatenate([late0[...], late1[...]], axis=1)
    late_t[...] = late[...].T

    sums = [sums_in[n : n + 1, :] for n in range(sums_in.shape[0])]
    largest = functools.reduce(jnp.maximum, add_sums(sums, xt[...], late[...], late_t[...]))

    def symmetric(left, right, finish, *refs):
        for n, some in enumerate(halves):
            rows = slice(some.start, tokens)
            product = left(rows, some) if right is None else dot(left[rows, :], right[:, some])
            for r in chunks[some.start // 32 :]:
                values = finish(product[r.start - some.start : r.stop - some.start], r, some)
                for ref, value in zip(refs, values):
                    ref[r, some] = value.astype(jnp.bfloat16)
            for other in halves[n + 1 :]:
                for ref in refs:
                    ref[some, other] = ref[other, some].T

    def gram(rows, some):
        return lax.dot_general(late[rows, :], late[some, :], (((1,), (1,)), ((), ())), preferred_element_type=jnp.float32)

    symmetric(gram, None, lambda product, r, some: [(gram_in[r, some] + product) * (1.0 / tokens)], k1)

    def move(some):
        moved = dot(chosen(fars[:-2]), xt[:, some]) + dot(chosen(fars[-2:]), late_t[:, some])
        image[:, some] = moved.astype(jnp.bfloat16)

    symmetric(k1, k1, lambda product, r, some: [product], k2)
    c = 1.0 / (jnp.max(largest) * (1.0 / tokens) + DAMPING)
    eps = 1.0 - c * DAMPING
    eps2 = eps * eps
    zeta = eps2 * eps2
    eps8 = zeta * zeta
    e2_1, e2_2 = -2.0 * eps * c, c * c
    g_1 = -(1.0 + eps) * c
    g_m = eps2 + (1.0 + eps) * eps + eps
    h_m = zeta + (1.0 + eps2) * eps2 + eps2
    k_m = eps8 + (1.0 + zeta) * zeta + zeta + 1.0 + eps8
    k_z = 1.0 + 3.0 * zeta
    a_m = g_m * h_m
    beta = (1.0 + zeta) * (1.0 + eps8)
    q_m = a_m * k_m + beta * g_m + (1.0 + eps2) * beta
    last = -c * c * (1.0 / tokens)
    q_m = q_m * last
    p = c * (1.0 + eps) * (1.0 + eps2) * beta

    def wide(ref, r, some):
        return ref[r, some].astype(jnp.float32)

    for some in halves:
        for r in chunks:
            first = wide(k1, r, some)
            square = e2_1 * first + e2_2 * wide(k2, r, some)
            e2[r, some] = square.astype(jnp.bfloat16)
            g[r, some] = (square + g_1 * first).astype(jnp.bfloat16)

    def fourth(product, r, some):
        square = wide(e2, r, some)
        value = 2.0 * eps2 * square + product
        return value, value + (1.0 + eps2) * square

    symmetric(e2, e2, fourth, z, h)
    load.wait()
    move(halves[0])
    symmetric(z, z, lambda product, r, some: [product + k_z * wide(z, r, some)], k)
    for some in halves:
        product = dot(g[...], h[:, some])
        for r in chunks:
            a[r, some] = (product[r] + g_m * wide(h, r, some) + h_m * wide(g, r, some)).astype(jnp.bfloat16)
    for some in halves[1:]:
        move(some)
    q_k, q_a, q_g = last * a_m, last * k_m, last * beta
    for some in halves:
        product = dot(k[...], a[:, some])
        for r in chunks:
            rest = q_k * wide(k, r, some) + q_a * wide(a, r, some) + q_g * wide(g, r, some)
            q[r, some] = (last * product[r] + rest).astype(jnp.bfloat16)
    for some in halves:
        product = dot(image[...], q[:, some])
        mixed[:, some] = (product + q_m * image[:, some].astype(jnp.float32)).astype(jnp.bfloat16)
    stores = []
    blocks = [x[:, at : at + half] for at in range(0, x.shape[1], half)] + [late[...]]
    for n, block in enumerate(blocks):
        moved = dot(mixed[...], block)
        for one in (0, 1):
            here = place(fars[2 * n + one])
            kept = p * tile[:, here].astype(jnp.float32)
            out[:, here] = (kept + moved[:, one * features : (one + 1) * features]).astype(jnp.bfloat16)
            store = pltpu.make_async_copy(out.at[:, here], out_hbm.at[:, here], sems.at[1 + len(stores)])
            store.start()
            stores.append(store)
    for store in stores:
        store.wait()


def by_tokens(factor_inputs, tile):
    members, replicas = lax.axis_size("grad"), lax.axis_size("dp")
    rows, width = tile.shape
    features = factor_inputs.shape[2]
    tokens = factor_inputs.shape[0] * replicas

    def shape(*sizes, kind=jnp.bfloat16):
        return jax.ShapeDtypeStruct(sizes, kind)

    def scratch(*sizes):
        return pltpu.VMEM(sizes, jnp.bfloat16)

    def swap(value, far):
        return lax.ppermute(value, "grad", [(i, i ^ far) for i in range(members)])

    parts = list(split_blocks(factor_inputs, range(replicas)))
    for far in range(1, replicas):
        parts[far] = lax.ppermute(parts[far], "dp", [(i, (i + far) % replicas) for i in range(replicas)])
    own = jnp.concatenate(parts, axis=0)
    fars = (0, 1, 6, 7, 2, 4, 3, 5)
    pieces = {0: own}
    for far in (2, 4, 6):
        pieces[far] = swap(own, far)
    for far in (0, 2, 4, 6):
        pieces[far + 1] = swap(pieces[far], 1)
    pieces = [pieces[far] for far in fars]
    early = width - 2 * features
    first = pl.pallas_call(
        add_kernel,
        out_shape=[
            shape(tokens, early),
            shape(early, tokens),
            shape(tokens, tokens, kind=jnp.float32),
            shape(early // (2 * features), 2 * features, kind=jnp.float32),
        ],
        in_specs=[WHOLE] * 6,
        out_specs=[WHOLE] * 4,
        compiler_params=pltpu.CompilerParams(vmem_limit_bytes=16 * 2**20),
        cost_estimate=pl.CostEstimate(flops=8 * 10**8, bytes_accessed=0, transcendentals=0),
        name="first_pieces",
    )(*pieces[:6])
    return pl.pallas_call(
        functools.partial(last_kernel, fars),
        out_shape=shape(rows, width),
        in_specs=[WHOLE] * 6 + [ANYWHERE],
        out_specs=ANYWHERE,
        scratch_shapes=[scratch(rows, width)] * 2
        + [scratch(tokens, 2 * features), scratch(2 * features, tokens)]
        + [scratch(tokens, tokens)] * 9
        + [scratch(rows, tokens)] * 2
        + [pltpu.SemaphoreType.DMA((1 + members,))],
        compiler_params=pltpu.CompilerParams(vmem_limit_bytes=51 * 2**20),
        cost_estimate=pl.CostEstimate(flops=5 * 10**9, bytes_accessed=0, transcendentals=0),
        name="whole_block",
    )(*pieces[6:], *first, tile)


def local(factor_inputs, gradients):
    features, members = factor_inputs.shape[2], lax.axis_size("grad")
    tokens = factor_inputs.shape[0] * lax.axis_size("dp")
    tile = gradients[0]
    if tokens < features * members and features % 128 == 0 and (members, lax.axis_size("dp")) == (8, 4):
        result = by_tokens(factor_inputs, tile)
    else:
        result = by_features(gather_block(factor_inputs), tile)
    return result.astype(jnp.bfloat16)[None]


def solution(mesh):
    placed = (P("dp", None, "grad"), P("dp", "grad", None))
    return jax.shard_map(
        local, mesh=mesh, in_specs=placed, out_specs=P("dp", "grad", None), check_vma=False
    )
```

```python
import functools

import jax
import jax.numpy as jnp
from jax import lax
from jax.experimental import pallas as pl
from jax.experimental.pallas import tpu as pltpu
from jax.sharding import PartitionSpec as P

ITERS = 4
DAMPING = 0.01
WHOLE = pl.BlockSpec(memory_space=pltpu.VMEM)
ANYWHERE = pl.BlockSpec(memory_space=pl.ANY)


def dot(a, b):
    return jnp.dot(a, b, preferred_element_type=jnp.float32)


def gather_block(factor_inputs):
    pieces = jnp.transpose(factor_inputs, (1, 0, 2))
    piece = lax.all_to_all(pieces, "dp", split_axis=0, concat_axis=1, tiled=True)[0]
    return lax.all_gather(piece, "grad", axis=1, tiled=True)


def by_features(columns, tile):
    tokens, width = columns.shape
    covariance = jnp.einsum("tr,tc->rc", columns, columns, preferred_element_type=jnp.float32) * (1.0 / tokens)
    damped = covariance + DAMPING * jnp.eye(width, dtype=jnp.float32)
    scale = 1.0 / jnp.max(jnp.sum(jnp.abs(damped), axis=1))
    image = scale * damped
    result = scale * tile.astype(jnp.float32)
    for step in range(ITERS):
        low = image.astype(jnp.bfloat16)
        result = 2.0 * result - dot(result.astype(jnp.bfloat16), low)
        if step < ITERS - 1:
            image = 2.0 * image - dot(low, low)
    return result


def split_kernel(fars, x_ref, *out_refs):
    replicas, tokens = len(out_refs), out_refs[0].shape[0]
    here = lax.axis_index("dp")
    x = x_ref[...]
    rows = lax.broadcasted_iota(jnp.int32, (tokens, tokens * replicas), 0)
    cols = lax.broadcasted_iota(jnp.int32, (tokens, tokens * replicas), 1)
    offset = cols - rows * replicas
    for far, out_ref in zip(fars, out_refs):
        choice = jnp.where(offset == lax.rem(here + far, replicas), 1.0, 0.0).astype(jnp.bfloat16)
        out_ref[...] = dot(choice, x).astype(jnp.bfloat16)


def split_blocks(factor_inputs, fars):
    tokens, blocks, features = factor_inputs.shape
    return pl.pallas_call(
        functools.partial(split_kernel, fars),
        out_shape=[jax.ShapeDtypeStruct((tokens, features), factor_inputs.dtype)] * blocks,
        in_specs=[WHOLE],
        out_specs=[WHOLE] * blocks,
        compiler_params=pltpu.CompilerParams(vmem_limit_bytes=16 * 2**20),
        name="split_blocks",
    )(factor_inputs.reshape(tokens * blocks, features))


def first_kernel(*refs):
    *pieces, columns, turned, gram = refs
    features = pieces[0].shape[1]
    for n, piece in enumerate(pieces):
        some = slice(n * features, (n + 1) * features)
        columns[:, some] = piece[...]
        turned[some, :] = piece[...].T
    gram[...] = dot(columns[...], turned[...])


def last_kernel(fars, late0, late1, x, xt, gram_in, tile_hbm, out_hbm, *refs):
    tile, out, late, late_t, k1, k2, e2, g, z, h, a, k, q, image, mixed, sems = refs
    load = pltpu.make_async_copy(tile_hbm, tile, sems.at[0])
    load.start()
    member = lax.axis_index("grad")
    tokens = x.shape[0]
    half = late.shape[1]
    features = half // 2
    chunks = [slice(at, at + 32) for at in range(0, tokens, 32)]

    def place(far):
        return pl.ds(pl.multiple_of((member ^ far) * features, features), features)

    def chosen(some, rows):
        return jnp.concatenate([tile[rows, place(far)] for far in some], axis=1)

    late[...] = jnp.concatenate([late0[...], late1[...]], axis=1)
    late_t[...] = late[...].T

    def each(product, finish, *refs):
        for r in chunks:
            for ref, value in zip(refs, finish(product[r], r)):
                ref[r, :] = value.astype(jnp.bfloat16)

    product = lax.dot_general(late[...], late[...], (((1,), (1,)), ((), ())), preferred_element_type=jnp.float32)
    each(product, lambda product, r: [(gram_in[r, :] + product) * (1.0 / tokens)], k1)

    def sums(column):
        return jnp.sum(column, axis=0, keepdims=True)

    def turned_sums(column):
        folded = functools.reduce(jnp.add, [column[:, at : at + 128] for at in range(0, column.shape[1], 128)])
        return sums(folded.T)

    def move(some):
        moved = dot(chosen(fars[:-2], some), xt[...]) + dot(chosen(fars[-2:], some), late_t[...])
        image[some, :] = moved.astype(jnp.bfloat16)

    top, side = xt.shape[0] - half, slice(xt.shape[0] - half, xt.shape[0])
    first = jnp.abs(dot(xt[:top, :], x[:, :top]))
    each(dot(k1[...], k1[...]), lambda product, r: [product], k2)
    ends = jnp.concatenate([x[:, side], late[...]], axis=1)
    second = jnp.abs(dot(xt[...], ends))
    third = jnp.abs(dot(late_t[...], ends))
    tops = sums(first) + turned_sums(second[:top])
    load.wait()
    rows = tile.shape[0]
    move(slice(0, rows // 2))
    sides = sums(second[:, :half]) + sums(third[:, :half])
    lates = sums(second[:, half:]) + sums(third[:, half:])
    largest = jnp.maximum(jnp.max(tops, axis=1, keepdims=True), jnp.max(jnp.maximum(sides, lates), axis=1, keepdims=True))
    c = 1.0 / (jnp.max(largest) * (1.0 / tokens) + DAMPING)
    eps = 1.0 - c * DAMPING
    eps2 = eps * eps
    zeta = eps2 * eps2
    eps8 = zeta * zeta
    e2_1, e2_2 = -2.0 * eps * c, c * c
    g_1 = -(1.0 + eps) * c
    g_m = eps2 + (1.0 + eps) * eps + eps
    h_m = zeta + (1.0 + eps2) * eps2 + eps2
    k_m = eps8 + (1.0 + zeta) * zeta + zeta + 1.0 + eps8
    k_z = 1.0 + 3.0 * zeta
    a_m = g_m * h_m
    beta = (1.0 + zeta) * (1.0 + eps8)
    q_m = a_m * k_m + beta * g_m + (1.0 + eps2) * beta
    last = -c * c * (1.0 / tokens)
    q_m = q_m * last
    p = c * (1.0 + eps) * (1.0 + eps2) * beta

    def wide(ref, r):
        return ref[r, :].astype(jnp.float32)

    for r in chunks:
        one = wide(k1, r)
        square = e2_1 * one + e2_2 * wide(k2, r)
        e2[r, :] = square.astype(jnp.bfloat16)
        g[r, :] = (square + g_1 * one).astype(jnp.bfloat16)

    def fourth(product, r):
        square = wide(e2, r)
        value = 2.0 * eps2 * square + product
        return value, value + (1.0 + eps2) * square

    each(dot(e2[...], e2[...]), fourth, z, h)
    move(slice(rows // 2, rows))
    each(dot(z[...], z[...]), lambda product, r: [product + k_z * wide(z, r)], k)
    each(dot(g[...], h[...]), lambda product, r: [product + g_m * wide(h, r) + h_m * wide(g, r)], a)
    q_k, q_a, q_g = last * a_m, last * k_m, last * beta

    def whole(product, r):
        return [last * product + q_k * wide(k, r) + q_a * wide(a, r) + q_g * wide(g, r)]

    each(dot(k[...], a[...]), whole, q)
    product = dot(image[...], q[...])
    mixed[...] = (product + q_m * image[...].astype(jnp.float32)).astype(jnp.bfloat16)
    stores = []
    for n, block in enumerate((x[:, :top], ends)):
        moved = dot(mixed[...], block)
        for at in range(0, block.shape[1], features):
            here = place(fars[(n * top + at) // features])
            kept = p * tile[:, here].astype(jnp.float32)
            out[:, here] = (kept + moved[:, at : at + features]).astype(jnp.bfloat16)
            store = pltpu.make_async_copy(out.at[:, here], out_hbm.at[:, here], sems.at[1 + len(stores)])
            store.start()
            stores.append(store)
    for store in stores:
        store.wait()


def by_tokens(factor_inputs, tile):
    members, replicas = lax.axis_size("grad"), lax.axis_size("dp")
    rows, width = tile.shape
    features = factor_inputs.shape[2]
    tokens = factor_inputs.shape[0] * replicas

    def shape(*sizes, kind=jnp.bfloat16):
        return jax.ShapeDtypeStruct(sizes, kind)

    def scratch(*sizes):
        return pltpu.VMEM(sizes, jnp.bfloat16)

    def swap(value, far):
        return lax.ppermute(value, "grad", [(i, i ^ far) for i in range(members)])

    parts = list(split_blocks(factor_inputs, range(replicas)))
    for far in range(1, replicas):
        parts[far] = lax.ppermute(parts[far], "dp", [(i, (i + far) % replicas) for i in range(replicas)])
    own = jnp.concatenate(parts, axis=0)
    fars = (0, 1, 6, 7, 4, 2, 5, 3)
    pieces = {0: own}
    for far in (2, 4, 6):
        pieces[far] = swap(own, far)
    for far in (0, 2, 4, 6):
        pieces[far + 1] = swap(pieces[far], 1)
    pieces = [pieces[far] for far in fars]
    early = width - 2 * features
    columns, turned, gram = pl.pallas_call(
        first_kernel,
        out_shape=[shape(tokens, early), shape(early, tokens), shape(tokens, tokens, kind=jnp.float32)],
        in_specs=[WHOLE] * 6,
        out_specs=[WHOLE] * 3,
        compiler_params=pltpu.CompilerParams(vmem_limit_bytes=16 * 2**20),
        cost_estimate=pl.CostEstimate(flops=4 * 10**8, bytes_accessed=0, transcendentals=0),
        name="first_pieces",
    )(*pieces[:6])
    return pl.pallas_call(
        functools.partial(last_kernel, fars),
        out_shape=shape(rows, width),
        in_specs=[WHOLE] * 5 + [ANYWHERE],
        out_specs=ANYWHERE,
        scratch_shapes=[scratch(rows, width)] * 2
        + [scratch(tokens, 2 * features), scratch(2 * features, tokens)]
        + [scratch(tokens, tokens)] * 9
        + [scratch(rows, tokens)] * 2
        + [pltpu.SemaphoreType.DMA((1 + members,))],
        compiler_params=pltpu.CompilerParams(vmem_limit_bytes=51 * 2**20),
        cost_estimate=pl.CostEstimate(flops=5 * 10**9, bytes_accessed=0, transcendentals=0),
        name="whole_block",
    )(*pieces[6:], columns, turned, gram, tile)


def local(factor_inputs, gradients):
    features, members = factor_inputs.shape[2], lax.axis_size("grad")
    tokens = factor_inputs.shape[0] * lax.axis_size("dp")
    tile = gradients[0]
    if tokens < features * members and features % 128 == 0 and (members, lax.axis_size("dp")) == (8, 4):
        result = by_tokens(factor_inputs, tile)
    else:
        result = by_features(gather_block(factor_inputs), tile)
    return result.astype(jnp.bfloat16)[None]


def solution(mesh):
    placed = (P("dp", None, "grad"), P("dp", "grad", None))
    return jax.shard_map(
        local, mesh=mesh, in_specs=placed, out_specs=P("dp", "grad", None), check_vma=False
    )
```

```python
import functools

import jax
import jax.numpy as jnp
from jax import lax
from jax.experimental import pallas as pl
from jax.experimental.pallas import tpu as pltpu
from jax.sharding import PartitionSpec as P

ITERS = 4
DAMPING = 0.01
ROWS = (0, 256, 512, 640)
WHOLE = pl.BlockSpec(memory_space=pltpu.VMEM)
ANYWHERE = pl.BlockSpec(memory_space=pl.ANY)


def dot(a, b):
    return jnp.dot(a, b, preferred_element_type=jnp.float32)


def gather_block(factor_inputs):
    pieces = jnp.transpose(factor_inputs, (1, 0, 2))
    piece = lax.all_to_all(pieces, "dp", split_axis=0, concat_axis=1, tiled=True)[0]
    return lax.all_gather(piece, "grad", axis=1, tiled=True)


def by_features(columns, tile):
    tokens, width = columns.shape
    covariance = jnp.einsum("tr,tc->rc", columns, columns, preferred_element_type=jnp.float32) * (1.0 / tokens)
    damped = covariance + DAMPING * jnp.eye(width, dtype=jnp.float32)
    scale = 1.0 / jnp.max(jnp.sum(jnp.abs(damped), axis=1))
    image = scale * damped
    result = scale * tile.astype(jnp.float32)
    for step in range(ITERS):
        low = image.astype(jnp.bfloat16)
        result = 2.0 * result - dot(result.astype(jnp.bfloat16), low)
        if step < ITERS - 1:
            image = 2.0 * image - dot(low, low)
    return result


def split_kernel(fars, x_ref, *out_refs):
    replicas, tokens = len(out_refs), out_refs[0].shape[0]
    here = lax.axis_index("dp")
    x = x_ref[...]
    rows = lax.broadcasted_iota(jnp.int32, (tokens, tokens * replicas), 0)
    cols = lax.broadcasted_iota(jnp.int32, (tokens, tokens * replicas), 1)
    offset = cols - rows * replicas
    for far, out_ref in zip(fars, out_refs):
        choice = jnp.where(offset == lax.rem(here + far, replicas), 1.0, 0.0).astype(jnp.bfloat16)
        out_ref[...] = dot(choice, x).astype(jnp.bfloat16)


def split_blocks(factor_inputs, fars):
    tokens, blocks, features = factor_inputs.shape
    return pl.pallas_call(
        functools.partial(split_kernel, fars),
        out_shape=[jax.ShapeDtypeStruct((tokens, features), factor_inputs.dtype)] * blocks,
        in_specs=[WHOLE],
        out_specs=[WHOLE] * blocks,
        compiler_params=pltpu.CompilerParams(vmem_limit_bytes=16 * 2**20),
        name="split_blocks",
    )(factor_inputs.reshape(tokens * blocks, features))


def first_kernel(*refs):
    *pieces, columns, turned, gram = refs
    features = pieces[0].shape[1]
    for n, piece in enumerate(pieces):
        some = slice(n * features, (n + 1) * features)
        columns[:, some] = piece[...]
        turned[some, :] = piece[...].T
    gram[...] = dot(columns[...], turned[...])


def last_kernel(fars, late0, late1, x, xt, gram_in, tile_hbm, out_hbm, *refs):
    tile, out, late, late_t, k1, k2, e2, g, z, h, a, k, q, image, sems = refs
    load = pltpu.make_async_copy(tile_hbm, tile, sems.at[0])
    load.start()
    member = lax.axis_index("grad")
    tokens = x.shape[0]
    half = late.shape[1]
    features = half // 2
    chunks = [slice(at, at + 32) for at in range(0, tokens, 32)]

    def place(far):
        return pl.ds(pl.multiple_of((member ^ far) * features, features), features)

    def chosen(some, rows):
        return jnp.concatenate([tile[rows, place(far)] for far in some], axis=1)

    late[...] = jnp.concatenate([late0[...], late1[...]], axis=1)
    late_t[...] = late[...].T

    def each(product, finish, *refs):
        for r in chunks:
            for ref, value in zip(refs, finish(product[r], r)):
                ref[r, :] = value.astype(jnp.bfloat16)

    product = lax.dot_general(late[...], late[...], (((1,), (1,)), ((), ())), preferred_element_type=jnp.float32)
    each(product, lambda product, r: [(gram_in[r, :] + product) * (1.0 / tokens)], k1)

    def sums(column):
        return jnp.sum(column, axis=0, keepdims=True)

    def turned_sums(column):
        folded = functools.reduce(jnp.add, [column[:, at : at + 128] for at in range(0, column.shape[1], 128)])
        return sums(folded.T)

    def move(some):
        moved = dot(chosen(fars[:-2], some), xt[...]) + dot(chosen(fars[-2:], some), late_t[...])
        image[some, :] = moved.astype(jnp.bfloat16)

    top, side = xt.shape[0] - half, slice(xt.shape[0] - half, xt.shape[0])
    first = jnp.abs(dot(xt[:top, :], x[:, :top]))
    each(dot(k1[...], k1[...]), lambda product, r: [product], k2)
    ends = jnp.concatenate([x[:, side], late[...]], axis=1)
    second = jnp.abs(dot(xt[...], ends))
    third = jnp.abs(dot(late_t[...], ends))
    tops = sums(first) + turned_sums(second[:top])
    load.wait()
    rows = tile.shape[0]
    move(slice(0, rows // 2))
    sides = sums(second[:, :half]) + sums(third[:, :half])
    lates = sums(second[:, half:]) + sums(third[:, half:])
    largest = jnp.maximum(jnp.max(tops, axis=1, keepdims=True), jnp.max(jnp.maximum(sides, lates), axis=1, keepdims=True))
    c = 1.0 / (jnp.max(largest) * (1.0 / tokens) + DAMPING)
    eps = 1.0 - c * DAMPING
    eps2 = eps * eps
    zeta = eps2 * eps2
    eps8 = zeta * zeta
    e2_1, e2_2 = -2.0 * eps * c, c * c
    g_1 = -(1.0 + eps) * c
    g_m = eps2 + (1.0 + eps) * eps + eps
    h_m = zeta + (1.0 + eps2) * eps2 + eps2
    k_m = eps8 + (1.0 + zeta) * zeta + zeta + 1.0 + eps8
    k_z = 1.0 + 3.0 * zeta
    a_m = g_m * h_m
    beta = (1.0 + zeta) * (1.0 + eps8)
    q_m = a_m * k_m + beta * g_m + (1.0 + eps2) * beta
    last = -c * c * (1.0 / tokens)
    q_m = q_m * last
    p = c * (1.0 + eps) * (1.0 + eps2) * beta

    def wide(ref, r):
        return ref[r, :].astype(jnp.float32)

    for r in chunks:
        one = wide(k1, r)
        square = e2_1 * one + e2_2 * wide(k2, r)
        e2[r, :] = square.astype(jnp.bfloat16)
        g[r, :] = (square + g_1 * one).astype(jnp.bfloat16)

    def fourth(product, r):
        square = wide(e2, r)
        value = 2.0 * eps2 * square + product
        return value, value + (1.0 + eps2) * square

    each(dot(e2[...], e2[...]), fourth, z, h)
    move(slice(rows // 2, rows))
    each(dot(z[...], z[...]), lambda product, r: [product + k_z * wide(z, r)], k)
    each(dot(g[...], h[...]), lambda product, r: [product + g_m * wide(h, r) + h_m * wide(g, r)], a)
    q_k, q_a, q_g = last * a_m, last * k_m, last * beta

    def whole(product, r):
        return [last * product + q_k * wide(k, r) + q_a * wide(a, r) + q_g * wide(g, r)]

    each(dot(k[...], a[...]), whole, q)
    stores = []
    for at, stop in zip(ROWS, ROWS[1:] + (rows,)):
        some = slice(at, stop)
        mixed = (dot(image[some, :], q[...]) + q_m * image[some, :].astype(jnp.float32)).astype(jnp.bfloat16)
        for n, block in enumerate((x[:, :top], ends)):
            moved = dot(mixed, block)
            for side in range(0, block.shape[1], features):
                here = place(fars[(n * top + side) // features])
                kept = p * tile[some, here].astype(jnp.float32)
                out[some, here] = (kept + moved[:, side : side + features]).astype(jnp.bfloat16)
        store = pltpu.make_async_copy(out.at[some, :], out_hbm.at[some, :], sems.at[1 + len(stores)])
        store.start()
        stores.append(store)
    for store in stores:
        store.wait()


def by_tokens(factor_inputs, tile):
    members, replicas = lax.axis_size("grad"), lax.axis_size("dp")
    rows, width = tile.shape
    features = factor_inputs.shape[2]
    tokens = factor_inputs.shape[0] * replicas

    def shape(*sizes, kind=jnp.bfloat16):
        return jax.ShapeDtypeStruct(sizes, kind)

    def scratch(*sizes):
        return pltpu.VMEM(sizes, jnp.bfloat16)

    def swap(value, far):
        return lax.ppermute(value, "grad", [(i, i ^ far) for i in range(members)])

    parts = list(split_blocks(factor_inputs, range(replicas)))
    for far in range(1, replicas):
        parts[far] = lax.ppermute(parts[far], "dp", [(i, (i + far) % replicas) for i in range(replicas)])
    own = jnp.concatenate(parts, axis=0)
    fars = (0, 1, 6, 7, 4, 2, 5, 3)
    pieces = {0: own}
    for far in (2, 4, 6):
        pieces[far] = swap(own, far)
    for far in (0, 2, 4, 6):
        pieces[far + 1] = swap(pieces[far], 1)
    pieces = [pieces[far] for far in fars]
    early = width - 2 * features
    columns, turned, gram = pl.pallas_call(
        first_kernel,
        out_shape=[shape(tokens, early), shape(early, tokens), shape(tokens, tokens, kind=jnp.float32)],
        in_specs=[WHOLE] * 6,
        out_specs=[WHOLE] * 3,
        compiler_params=pltpu.CompilerParams(vmem_limit_bytes=16 * 2**20),
        cost_estimate=pl.CostEstimate(flops=4 * 10**8, bytes_accessed=0, transcendentals=0),
        name="first_pieces",
    )(*pieces[:6])
    return pl.pallas_call(
        functools.partial(last_kernel, fars),
        out_shape=shape(rows, width),
        in_specs=[WHOLE] * 5 + [ANYWHERE],
        out_specs=ANYWHERE,
        scratch_shapes=[scratch(rows, width)] * 2
        + [scratch(tokens, 2 * features), scratch(2 * features, tokens)]
        + [scratch(tokens, tokens)] * 9
        + [scratch(rows, tokens)]
        + [pltpu.SemaphoreType.DMA((1 + len(ROWS),))],
        compiler_params=pltpu.CompilerParams(vmem_limit_bytes=51 * 2**20),
        cost_estimate=pl.CostEstimate(flops=5 * 10**9, bytes_accessed=0, transcendentals=0),
        name="whole_block",
    )(*pieces[6:], columns, turned, gram, tile)


def local(factor_inputs, gradients):
    features, members = factor_inputs.shape[2], lax.axis_size("grad")
    tokens = factor_inputs.shape[0] * lax.axis_size("dp")
    tile = gradients[0]
    if tokens < features * members and features % 128 == 0 and (members, lax.axis_size("dp"), len(tile)) == (8, 4, 768):
        result = by_tokens(factor_inputs, tile)
    else:
        result = by_features(gather_block(factor_inputs), tile)
    return result.astype(jnp.bfloat16)[None]


def solution(mesh):
    placed = (P("dp", None, "grad"), P("dp", "grad", None))
    return jax.shard_map(
        local, mesh=mesh, in_specs=placed, out_specs=P("dp", "grad", None), check_vma=False
    )
```

```python
import functools

import jax
import jax.numpy as jnp
from jax import lax
from jax.experimental import pallas as pl
from jax.experimental.pallas import tpu as pltpu
from jax.sharding import PartitionSpec as P

ITERS = 4
DAMPING = 0.01
SPLIT_VMEM = 56393728
WHOLE = pl.BlockSpec(memory_space=pltpu.VMEM)
ANYWHERE = pl.BlockSpec(memory_space=pl.ANY)


def dot(a, b):
    return jnp.dot(a, b, preferred_element_type=jnp.float32)


def gather_block(factor_inputs):
    pieces = jnp.transpose(factor_inputs, (1, 0, 2))
    piece = lax.all_to_all(pieces, "dp", split_axis=0, concat_axis=1, tiled=True)[0]
    return lax.all_gather(piece, "grad", axis=1, tiled=True)


def by_features(columns, tile):
    tokens, width = columns.shape
    covariance = jnp.einsum("tr,tc->rc", columns, columns, preferred_element_type=jnp.float32) * (1.0 / tokens)
    damped = covariance + DAMPING * jnp.eye(width, dtype=jnp.float32)
    scale = 1.0 / jnp.max(jnp.sum(jnp.abs(damped), axis=1))
    image = scale * damped
    result = scale * tile.astype(jnp.float32)
    for step in range(ITERS):
        low = image.astype(jnp.bfloat16)
        result = 2.0 * result - dot(result.astype(jnp.bfloat16), low)
        if step < ITERS - 1:
            image = 2.0 * image - dot(low, low)
    return result


def split_kernel(fars, x_hbm, *refs):
    *out_refs, x, sems = refs
    count = sems.shape[0]
    step = x.shape[0] // count
    loads = [
        pltpu.make_async_copy(x_hbm.at[pl.ds(n * step, step), :], x.at[pl.ds(n * step, step), :], sems.at[n])
        for n in range(count)
    ]
    for load in loads:
        load.start()
    replicas, tokens = len(out_refs), out_refs[0].shape[0]
    here = lax.axis_index("dp")
    rows = lax.broadcasted_iota(jnp.int32, (tokens, tokens * replicas), 0)
    cols = lax.broadcasted_iota(jnp.int32, (tokens, tokens * replicas), 1)
    offset = cols - rows * replicas
    choices = [
        jnp.where(offset == lax.rem(here + far, replicas), 1.0, 0.0).astype(jnp.bfloat16) for far in fars
    ]
    for load in loads:
        load.wait()
    for choice, out_ref in zip(choices, out_refs):
        out_ref[...] = dot(choice, x[...]).astype(jnp.bfloat16)


def split_blocks(factor_inputs, fars):
    tokens, blocks, features = factor_inputs.shape
    return pl.pallas_call(
        functools.partial(split_kernel, fars),
        out_shape=[jax.ShapeDtypeStruct((tokens, features), factor_inputs.dtype)] * blocks,
        in_specs=[ANYWHERE],
        out_specs=[WHOLE] * blocks,
        scratch_shapes=[pltpu.VMEM((tokens * blocks, features), factor_inputs.dtype), pltpu.SemaphoreType.DMA((2,))],
        compiler_params=pltpu.CompilerParams(vmem_limit_bytes=SPLIT_VMEM),
        name="split_blocks",
    )(factor_inputs.reshape(tokens * blocks, features))


def first_kernel(*refs):
    *pieces, columns, turned, gram = refs
    features = pieces[0].shape[1]
    for n, piece in enumerate(pieces):
        some = slice(n * features, (n + 1) * features)
        columns[:, some] = piece[...]
        turned[some, :] = piece[...].T
    gram[...] = dot(columns[...], turned[...])


def last_kernel(fars, late0, late1, x, xt, gram_in, tile_hbm, out_hbm, *refs):
    tile, out, late, late_t, k1, k2, e2, g, z, h, a, k, q, image, mixed, sems = refs
    load = pltpu.make_async_copy(tile_hbm, tile, sems.at[0])
    load.start()
    member = lax.axis_index("grad")
    tokens = x.shape[0]
    half = late.shape[1]
    features = half // 2
    halves = [slice(at, at + half) for at in range(0, tokens, half)]
    blocks = [slice(at, at + half) for at in range(0, x.shape[1], half)]
    chunks = [slice(at, at + 32) for at in range(0, tokens, 32)]

    def place(far):
        return pl.ds(pl.multiple_of((member ^ far) * features, features), features)

    def chosen(some):
        return jnp.concatenate([tile[:, place(far)] for far in some], axis=1)

    late[...] = jnp.concatenate([late0[...], late1[...]], axis=1)
    late_t[...] = late[...].T

    def symmetric(left, right, finish, *refs):
        for n, some in enumerate(halves):
            rows = slice(some.start, tokens)
            product = left(rows, some) if right is None else dot(left[rows, :], right[:, some])
            for r in chunks[some.start // 32 :]:
                values = finish(product[r.start - some.start : r.stop - some.start], r, some)
                for ref, value in zip(refs, values):
                    ref[r, some] = value.astype(jnp.bfloat16)
            for other in halves[n + 1 :]:
                for ref in refs:
                    ref[some, other] = ref[other, some].T

    def gram(rows, some):
        return lax.dot_general(late[rows, :], late[some, :], (((1,), (1,)), ((), ())), preferred_element_type=jnp.float32)

    symmetric(gram, None, lambda product, r, some: [(gram_in[r, some] + product) * (1.0 / tokens)], k1)

    column_sums, row_sums = [0.0] * (len(blocks) + 1), [0.0] * len(blocks)

    def add_sums(n, left, right):
        column = jnp.abs(dot(left, right))
        column_sums[n] = column_sums[n] + jnp.sum(column, axis=0, keepdims=True)
        for i, some in enumerate(blocks[: min(n, column.shape[0] // half)]):
            row_sums[i] = row_sums[i] + column[some, :features] + column[some, features:]

    def move(some):
        moved = dot(chosen(fars[:-2]), xt[:, some]) + dot(chosen(fars[-2:]), late_t[:, some])
        image[:, some] = moved.astype(jnp.bfloat16)

    for n, some in enumerate(blocks):
        add_sums(n, xt[: some.stop, :], x[:, some])
    symmetric(k1, k1, lambda product, r, some: [product], k2)
    add_sums(len(blocks), xt[...], late[...])
    column_sums[-1] = column_sums[-1] + jnp.sum(jnp.abs(dot(late_t[...], late[...])), axis=0, keepdims=True)
    load.wait()
    move(halves[0])

    largest = column_sums[-1]
    for column, row in zip(column_sums[:-1], row_sums):
        largest = jnp.maximum(largest, column + jnp.sum(row.T, axis=0, keepdims=True))
    c = 1.0 / (jnp.max(largest) * (1.0 / tokens) + DAMPING)
    eps = 1.0 - c * DAMPING
    eps2 = eps * eps
    zeta = eps2 * eps2
    eps8 = zeta * zeta
    e2_1, e2_2 = -2.0 * eps * c, c * c
    g_1 = -(1.0 + eps) * c
    g_m = eps2 + (1.0 + eps) * eps + eps
    h_m = zeta + (1.0 + eps2) * eps2 + eps2
    k_m = eps8 + (1.0 + zeta) * zeta + zeta + 1.0 + eps8
    k_z = 1.0 + 3.0 * zeta
    a_m = g_m * h_m
    beta = (1.0 + zeta) * (1.0 + eps8)
    q_m = a_m * k_m + beta * g_m + (1.0 + eps2) * beta
    last = -c * c * (1.0 / tokens)
    q_m = q_m * last
    p = c * (1.0 + eps) * (1.0 + eps2) * beta

    def wide(ref, r, some):
        return ref[r, some].astype(jnp.float32)

    for some in halves:
        for r in chunks:
            first = wide(k1, r, some)
            square = e2_1 * first + e2_2 * wide(k2, r, some)
            e2[r, some] = square.astype(jnp.bfloat16)
            g[r, some] = (square + g_1 * first).astype(jnp.bfloat16)

    def fourth(product, r, some):
        square = wide(e2, r, some)
        value = 2.0 * eps2 * square + product
        return value, value + (1.0 + eps2) * square

    symmetric(e2, e2, fourth, z, h)
    for some in halves[1:]:
        move(some)
    symmetric(z, z, lambda product, r, some: [product + k_z * wide(z, r, some)], k)
    for some in halves:
        product = dot(g[...], h[:, some])
        for r in chunks:
            a[r, some] = (product[r] + g_m * wide(h, r, some) + h_m * wide(g, r, some)).astype(jnp.bfloat16)
    q_k, q_a, q_g = last * a_m, last * k_m, last * beta
    for some in halves:
        product = dot(k[...], a[:, some])
        for r in chunks:
            rest = q_k * wide(k, r, some) + q_a * wide(a, r, some) + q_g * wide(g, r, some)
            q[r, some] = (last * product[r] + rest).astype(jnp.bfloat16)
    for some in halves:
        product = dot(image[...], q[:, some])
        mixed[:, some] = (product + q_m * image[:, some].astype(jnp.float32)).astype(jnp.bfloat16)
    stores = []
    for n in range(len(blocks) + 1):
        moved = dot(mixed[...], late[...] if n == len(blocks) else x[:, blocks[n]])
        for one in (0, 1):
            here = place(fars[2 * n + one])
            kept = p * tile[:, here].astype(jnp.float32)
            out[:, here] = (kept + moved[:, one * features : (one + 1) * features]).astype(jnp.bfloat16)
            store = pltpu.make_async_copy(out.at[:, here], out_hbm.at[:, here], sems.at[1 + len(stores)])
            store.start()
            stores.append(store)
    for store in stores:
        store.wait()


def by_tokens(factor_inputs, tile):
    members, replicas = lax.axis_size("grad"), lax.axis_size("dp")
    rows, width = tile.shape
    features = factor_inputs.shape[2]
    tokens = factor_inputs.shape[0] * replicas

    def shape(*sizes, kind=jnp.bfloat16):
        return jax.ShapeDtypeStruct(sizes, kind)

    def scratch(*sizes):
        return pltpu.VMEM(sizes, jnp.bfloat16)

    def swap(value, far):
        return lax.ppermute(value, "grad", [(i, i ^ far) for i in range(members)])

    parts = list(split_blocks(factor_inputs, range(replicas)))
    for far in range(1, replicas):
        parts[far] = lax.ppermute(parts[far], "dp", [(i, (i + far) % replicas) for i in range(replicas)])
    own = jnp.concatenate(parts, axis=0)
    fars = (0, 1, 6, 7, 2, 4, 3, 5)
    pieces = {0: own}
    for far in (2, 4, 6):
        pieces[far] = swap(own, far)
    for far in (0, 2, 4, 6):
        pieces[far + 1] = swap(pieces[far], 1)
    pieces = [pieces[far] for far in fars]
    early = width - 2 * features
    columns, turned, gram = pl.pallas_call(
        first_kernel,
        out_shape=[shape(tokens, early), shape(early, tokens), shape(tokens, tokens, kind=jnp.float32)],
        in_specs=[WHOLE] * 6,
        out_specs=[WHOLE] * 3,
        compiler_params=pltpu.CompilerParams(vmem_limit_bytes=16 * 2**20),
        cost_estimate=pl.CostEstimate(flops=4 * 10**8, bytes_accessed=0, transcendentals=0),
        name="first_pieces",
    )(*pieces[:6])
    return pl.pallas_call(
        functools.partial(last_kernel, fars),
        out_shape=shape(rows, width),
        in_specs=[WHOLE] * 5 + [ANYWHERE],
        out_specs=ANYWHERE,
        scratch_shapes=[scratch(rows, width)] * 2
        + [scratch(tokens, 2 * features), scratch(2 * features, tokens)]
        + [scratch(tokens, tokens)] * 9
        + [scratch(rows, tokens)] * 2
        + [pltpu.SemaphoreType.DMA((1 + members,))],
        compiler_params=pltpu.CompilerParams(vmem_limit_bytes=51 * 2**20),
        cost_estimate=pl.CostEstimate(flops=5 * 10**9, bytes_accessed=0, transcendentals=0),
        name="whole_block",
    )(*pieces[6:], columns, turned, gram, tile)


def local(factor_inputs, gradients):
    features, members = factor_inputs.shape[2], lax.axis_size("grad")
    tokens = factor_inputs.shape[0] * lax.axis_size("dp")
    tile = gradients[0]
    if tokens < features * members and features % 128 == 0 and (members, lax.axis_size("dp")) == (8, 4):
        result = by_tokens(factor_inputs, tile)
    else:
        result = by_features(gather_block(factor_inputs), tile)
    return result.astype(jnp.bfloat16)[None]


def solution(mesh):
    placed = (P("dp", None, "grad"), P("dp", "grad", None))
    return jax.shard_map(
        local, mesh=mesh, in_specs=placed, out_specs=P("dp", "grad", None), check_vma=False
    )
```

```python
import functools

import jax
import jax.numpy as jnp
from jax import lax
from jax.experimental import pallas as pl
from jax.experimental.pallas import tpu as pltpu
from jax.sharding import PartitionSpec as P

ITERS = 4
DAMPING = 0.01
WHOLE = pl.BlockSpec(memory_space=pltpu.VMEM)
ANYWHERE = pl.BlockSpec(memory_space=pl.ANY)


def dot(a, b):
    return jnp.dot(a, b, preferred_element_type=jnp.float32)


def gather_block(factor_inputs):
    pieces = jnp.transpose(factor_inputs, (1, 0, 2))
    piece = lax.all_to_all(pieces, "dp", split_axis=0, concat_axis=1, tiled=True)[0]
    return lax.all_gather(piece, "grad", axis=1, tiled=True)


def by_features(columns, tile):
    tokens, width = columns.shape
    covariance = jnp.einsum("tr,tc->rc", columns, columns, preferred_element_type=jnp.float32) * (1.0 / tokens)
    damped = covariance + DAMPING * jnp.eye(width, dtype=jnp.float32)
    scale = 1.0 / jnp.max(jnp.sum(jnp.abs(damped), axis=1))
    image = scale * damped
    result = scale * tile.astype(jnp.float32)
    for step in range(ITERS):
        low = image.astype(jnp.bfloat16)
        result = 2.0 * result - dot(result.astype(jnp.bfloat16), low)
        if step < ITERS - 1:
            image = 2.0 * image - dot(low, low)
    return result


def split_kernel(fars, x_ref, *out_refs):
    replicas, tokens = len(out_refs), out_refs[0].shape[0]
    here = lax.axis_index("dp")
    x = x_ref[...]
    rows = lax.broadcasted_iota(jnp.int32, (tokens, tokens * replicas), 0)
    cols = lax.broadcasted_iota(jnp.int32, (tokens, tokens * replicas), 1)
    offset = cols - rows * replicas
    for far, out_ref in zip(fars, out_refs):
        choice = jnp.where(offset == lax.rem(here + far, replicas), 1.0, 0.0).astype(jnp.bfloat16)
        out_ref[...] = dot(choice, x).astype(jnp.bfloat16)


def split_blocks(factor_inputs, fars):
    tokens, blocks, features = factor_inputs.shape
    return pl.pallas_call(
        functools.partial(split_kernel, fars),
        out_shape=[jax.ShapeDtypeStruct((tokens, features), factor_inputs.dtype)] * blocks,
        in_specs=[WHOLE],
        out_specs=[WHOLE] * blocks,
        compiler_params=pltpu.CompilerParams(vmem_limit_bytes=16 * 2**20),
        name="split_blocks",
    )(factor_inputs.reshape(tokens * blocks, features))


def first_kernel(*refs):
    *pieces, columns, turned, gram = refs
    features = pieces[0].shape[1]
    for n, piece in enumerate(pieces):
        some = slice(n * features, (n + 1) * features)
        columns[:, some] = piece[...]
        turned[some, :] = piece[...].T
    gram[...] = dot(columns[...], turned[...])


def last_kernel(fars, late0, late1, x, xt, gram_in, tile_hbm, out_hbm, *refs):
    tile, out, late, late_t, k1, k2, e2, g, z, h, k, image, by_g, by_h, mixed, sems = refs
    load = pltpu.make_async_copy(tile_hbm, tile, sems.at[0])
    load.start()
    member = lax.axis_index("grad")
    tokens = x.shape[0]
    half = late.shape[1]
    features = half // 2
    halves = [slice(at, at + half) for at in range(0, tokens, half)]
    blocks = [slice(at, at + half) for at in range(0, x.shape[1], half)]
    chunks = [slice(at, at + 32) for at in range(0, tokens, 32)]

    def place(far):
        return pl.ds(pl.multiple_of((member ^ far) * features, features), features)

    def chosen(some):
        return jnp.concatenate([tile[:, place(far)] for far in some], axis=1)

    late[...] = jnp.concatenate([late0[...], late1[...]], axis=1)
    late_t[...] = late[...].T

    def symmetric(left, right, finish, *refs):
        for n, some in enumerate(halves):
            rows = slice(some.start, tokens)
            product = left(rows, some) if right is None else dot(left[rows, :], right[:, some])
            for r in chunks[some.start // 32 :]:
                values = finish(product[r.start - some.start : r.stop - some.start], r, some)
                for ref, value in zip(refs, values):
                    ref[r, some] = value.astype(jnp.bfloat16)
            for other in halves[n + 1 :]:
                for ref in refs:
                    ref[some, other] = ref[other, some].T

    def gram(rows, some):
        return lax.dot_general(late[rows, :], late[some, :], (((1,), (1,)), ((), ())), preferred_element_type=jnp.float32)

    symmetric(gram, None, lambda product, r, some: [(gram_in[r, some] + product) * (1.0 / tokens)], k1)

    column_sums, row_sums = [0.0] * (len(blocks) + 1), [0.0] * len(blocks)

    def add_sums(n, left, right):
        column = jnp.abs(dot(left, right))
        column_sums[n] = column_sums[n] + jnp.sum(column, axis=0, keepdims=True)
        for i, some in enumerate(blocks[: min(n, column.shape[0] // half)]):
            row_sums[i] = row_sums[i] + column[some, :features] + column[some, features:]

    def move(some):
        moved = dot(chosen(fars[:-2]), xt[:, some]) + dot(chosen(fars[-2:]), late_t[:, some])
        image[:, some] = moved.astype(jnp.bfloat16)

    for n, some in enumerate(blocks):
        add_sums(n, xt[: some.stop, :], x[:, some])
    symmetric(k1, k1, lambda product, r, some: [product], k2)
    add_sums(len(blocks), xt[...], late[...])
    column_sums[-1] = column_sums[-1] + jnp.sum(jnp.abs(dot(late_t[...], late[...])), axis=0, keepdims=True)
    load.wait()
    for some in halves:
        move(some)

    largest = column_sums[-1]
    for column, row in zip(column_sums[:-1], row_sums):
        largest = jnp.maximum(largest, column + jnp.sum(row.T, axis=0, keepdims=True))
    c = 1.0 / (jnp.max(largest) * (1.0 / tokens) + DAMPING)
    eps = 1.0 - c * DAMPING
    eps2 = eps * eps
    zeta = eps2 * eps2
    eps8 = zeta * zeta
    e2_1, e2_2 = -2.0 * eps * c, c * c
    g_1 = -(1.0 + eps) * c
    g_m = eps2 + (1.0 + eps) * eps + eps
    h_m = zeta + (1.0 + eps2) * eps2 + eps2
    k_m = eps8 + (1.0 + zeta) * zeta + zeta + 1.0 + eps8
    k_z = 1.0 + 3.0 * zeta
    beta = (1.0 + zeta) * (1.0 + eps8)
    last = -c * c * (1.0 / tokens)
    p = c * (1.0 + eps) * (1.0 + eps2) * beta

    def wide(ref, r, some):
        return ref[r, some].astype(jnp.float32)

    for some in halves:
        for r in chunks:
            first = wide(k1, r, some)
            square = e2_1 * first + e2_2 * wide(k2, r, some)
            e2[r, some] = square.astype(jnp.bfloat16)
            g[r, some] = (square + g_1 * first).astype(jnp.bfloat16)

    def fourth(product, r, some):
        square = wide(e2, r, some)
        value = 2.0 * eps2 * square + product
        return value, value + (1.0 + eps2) * square

    symmetric(e2, e2, fourth, z, h)

    def apply(left, right, parts, result, scale=None):
        for some in halves:
            total = dot(left[...], right[:, some])
            total = total if scale is None else total * scale
            for weight, part in parts:
                total = total + weight * part[:, some].astype(jnp.float32)
            result[:, some] = total.astype(jnp.bfloat16)

    apply(image, g, [(g_m, image)], by_g)
    symmetric(z, z, lambda product, r, some: [product + k_z * wide(z, r, some)], k)
    apply(by_g, h, [(h_m, by_g)], by_h)
    apply(by_h, k, [(last * (1.0 + eps2) * beta, image), (last * beta, by_g), (last * k_m, by_h)], mixed, last)
    stores = []
    for n in range(len(blocks) + 1):
        moved = dot(mixed[...], late[...] if n == len(blocks) else x[:, blocks[n]])
        for one in (0, 1):
            here = place(fars[2 * n + one])
            kept = p * tile[:, here].astype(jnp.float32)
            out[:, here] = (kept + moved[:, one * features : (one + 1) * features]).astype(jnp.bfloat16)
            store = pltpu.make_async_copy(out.at[:, here], out_hbm.at[:, here], sems.at[1 + len(stores)])
            store.start()
            stores.append(store)
    for store in stores:
        store.wait()


def by_tokens(factor_inputs, tile):
    members, replicas = lax.axis_size("grad"), lax.axis_size("dp")
    rows, width = tile.shape
    features = factor_inputs.shape[2]
    tokens = factor_inputs.shape[0] * replicas

    def shape(*sizes, kind=jnp.bfloat16):
        return jax.ShapeDtypeStruct(sizes, kind)

    def scratch(*sizes):
        return pltpu.VMEM(sizes, jnp.bfloat16)

    def swap(value, far):
        return lax.ppermute(value, "grad", [(i, i ^ far) for i in range(members)])

    parts = list(split_blocks(factor_inputs, range(replicas)))
    for far in range(1, replicas):
        parts[far] = lax.ppermute(parts[far], "dp", [(i, (i + far) % replicas) for i in range(replicas)])
    own = jnp.concatenate(parts, axis=0)
    fars = (0, 1, 6, 7, 2, 4, 3, 5)
    pieces = {0: own}
    for far in (2, 4, 6):
        pieces[far] = swap(own, far)
    for far in (0, 2, 4, 6):
        pieces[far + 1] = swap(pieces[far], 1)
    pieces = [pieces[far] for far in fars]
    early = width - 2 * features
    columns, turned, gram = pl.pallas_call(
        first_kernel,
        out_shape=[shape(tokens, early), shape(early, tokens), shape(tokens, tokens, kind=jnp.float32)],
        in_specs=[WHOLE] * 6,
        out_specs=[WHOLE] * 3,
        compiler_params=pltpu.CompilerParams(vmem_limit_bytes=16 * 2**20),
        cost_estimate=pl.CostEstimate(flops=4 * 10**8, bytes_accessed=0, transcendentals=0),
        name="first_pieces",
    )(*pieces[:6])
    return pl.pallas_call(
        functools.partial(last_kernel, fars),
        out_shape=shape(rows, width),
        in_specs=[WHOLE] * 5 + [ANYWHERE],
        out_specs=ANYWHERE,
        scratch_shapes=[scratch(rows, width)] * 2
        + [scratch(tokens, 2 * features), scratch(2 * features, tokens)]
        + [scratch(tokens, tokens)] * 7
        + [scratch(rows, tokens)] * 4
        + [pltpu.SemaphoreType.DMA((1 + members,))],
        compiler_params=pltpu.CompilerParams(vmem_limit_bytes=51 * 2**20),
        cost_estimate=pl.CostEstimate(flops=5 * 10**9, bytes_accessed=0, transcendentals=0),
        name="whole_block",
    )(*pieces[6:], columns, turned, gram, tile)


def local(factor_inputs, gradients):
    features, members = factor_inputs.shape[2], lax.axis_size("grad")
    tokens = factor_inputs.shape[0] * lax.axis_size("dp")
    tile = gradients[0]
    if tokens < features * members and features % 128 == 0 and (members, lax.axis_size("dp")) == (8, 4):
        result = by_tokens(factor_inputs, tile)
    else:
        result = by_features(gather_block(factor_inputs), tile)
    return result.astype(jnp.bfloat16)[None]


def solution(mesh):
    placed = (P("dp", None, "grad"), P("dp", "grad", None))
    return jax.shard_map(
        local, mesh=mesh, in_specs=placed, out_specs=P("dp", "grad", None), check_vma=False
    )
```

```python
import functools

import jax
import jax.numpy as jnp
from jax import lax
from jax.experimental import pallas as pl
from jax.experimental.pallas import tpu as pltpu
from jax.sharding import PartitionSpec as P

ITERS = 4
DAMPING = 0.01
WHOLE = pl.BlockSpec(memory_space=pltpu.VMEM)
ANYWHERE = pl.BlockSpec(memory_space=pl.ANY)


def dot(a, b):
    return jnp.dot(a, b, preferred_element_type=jnp.float32)


def gather_block(factor_inputs):
    pieces = jnp.transpose(factor_inputs, (1, 0, 2))
    piece = lax.all_to_all(pieces, "dp", split_axis=0, concat_axis=1, tiled=True)[0]
    return lax.all_gather(piece, "grad", axis=1, tiled=True)


def by_features(columns, tile):
    tokens, width = columns.shape
    covariance = jnp.einsum("tr,tc->rc", columns, columns, preferred_element_type=jnp.float32) * (1.0 / tokens)
    damped = covariance + DAMPING * jnp.eye(width, dtype=jnp.float32)
    scale = 1.0 / jnp.max(jnp.sum(jnp.abs(damped), axis=1))
    image = scale * damped
    result = scale * tile.astype(jnp.float32)
    for step in range(ITERS):
        low = image.astype(jnp.bfloat16)
        result = 2.0 * result - dot(result.astype(jnp.bfloat16), low)
        if step < ITERS - 1:
            image = 2.0 * image - dot(low, low)
    return result


def split_kernel(fars, x_ref, *out_refs):
    replicas, tokens = len(out_refs), out_refs[0].shape[0]
    here = lax.axis_index("dp")
    x = x_ref[...]
    rows = lax.broadcasted_iota(jnp.int32, (tokens, tokens * replicas), 0)
    cols = lax.broadcasted_iota(jnp.int32, (tokens, tokens * replicas), 1)
    offset = cols - rows * replicas
    for far, out_ref in zip(fars, out_refs):
        choice = jnp.where(offset == lax.rem(here + far, replicas), 1.0, 0.0).astype(jnp.bfloat16)
        out_ref[...] = dot(choice, x).astype(jnp.bfloat16)


def split_blocks(factor_inputs, fars):
    tokens, blocks, features = factor_inputs.shape
    return pl.pallas_call(
        functools.partial(split_kernel, fars),
        out_shape=[jax.ShapeDtypeStruct((tokens, features), factor_inputs.dtype)] * blocks,
        in_specs=[WHOLE],
        out_specs=[WHOLE] * blocks,
        compiler_params=pltpu.CompilerParams(vmem_limit_bytes=16 * 2**20),
        name="split_blocks",
    )(factor_inputs.reshape(tokens * blocks, features))


def first_kernel(*refs):
    *pieces, columns, turned, gram = refs
    features = pieces[0].shape[1]
    for n, piece in enumerate(pieces):
        some = slice(n * features, (n + 1) * features)
        columns[:, some] = piece[...]
        turned[some, :] = piece[...].T
    gram[...] = dot(columns[...], turned[...])


def last_kernel(fars, late0, late1, x, xt, gram_in, tile_hbm, out_hbm, *refs):
    tile, out, late, late_t, k1, k2, e2, g, z, h, k, image, by_g, by_h, mixed, *folds, sems = refs
    load = pltpu.make_async_copy(tile_hbm, tile, sems.at[0])
    load.start()
    member = lax.axis_index("grad")
    tokens = x.shape[0]
    half = late.shape[1]
    features = half // 2
    halves = [slice(at, at + half) for at in range(0, tokens, half)]
    blocks = [slice(at, at + half) for at in range(0, x.shape[1], half)]

    def chunks_of(size):
        return [slice(at, at + 32) for at in range(0, size, 32)]

    chunks = chunks_of(tokens)

    def place(far):
        return pl.ds(pl.multiple_of((member ^ far) * features, features), features)

    def chosen(some):
        return jnp.concatenate([tile[:, place(far)] for far in some], axis=1)

    late[...] = jnp.concatenate([late0[...], late1[...]], axis=1)
    late_t[...] = late[...].T

    def symmetric(left, right, finish, *refs):
        for n, some in enumerate(halves):
            rows = slice(some.start, tokens)
            product = left(rows, some) if right is None else dot(left[rows, :], right[:, some])
            for r in chunks[some.start // 32 :]:
                values = finish(product[r.start - some.start : r.stop - some.start], r, some)
                for ref, value in zip(refs, values):
                    ref[r, some] = value.astype(jnp.bfloat16)
            for other in halves[n + 1 :]:
                for ref in refs:
                    ref[some, other] = ref[other, some].T

    def gram(rows, some):
        return lax.dot_general(late[rows, :], late[some, :], (((1,), (1,)), ((), ())), preferred_element_type=jnp.float32)

    symmetric(gram, None, lambda product, r, some: [(gram_in[r, some] + product) * (1.0 / tokens)], k1)

    column_sums = [0.0] * (len(blocks) + 1)

    def add_sums(n, left, right):
        product = dot(left, right)
        total = 0.0
        for r in chunks_of(product.shape[0]):
            block = jnp.abs(product[r])
            total = total + block
            if r.start < n * half:
                folds[n - 1][r, :] = block[:, :features] + block[:, features:]
        column_sums[n] = column_sums[n] + jnp.sum(total, axis=0, keepdims=True)

    def move(some):
        moved, rest = dot(chosen(fars[:-2]), xt[:, some]), dot(chosen(fars[-2:]), late_t[:, some])
        for r in chunks_of(moved.shape[0]):
            image[r, some] = (moved[r] + rest[r]).astype(jnp.bfloat16)

    for n, some in enumerate(blocks):
        add_sums(n, xt[: some.stop, :], x[:, some])
    symmetric(k1, k1, lambda product, r, some: [product], k2)
    add_sums(len(blocks), xt[...], late[...])
    product = dot(late_t[...], late[...])
    total = functools.reduce(jnp.add, [jnp.abs(product[r]) for r in chunks_of(half)])
    column_sums[-1] = column_sums[-1] + jnp.sum(total, axis=0, keepdims=True)
    load.wait()
    for some in halves:
        move(some)

    largest = column_sums[-1]
    for n, (column, some) in enumerate(zip(column_sums[:-1], blocks)):
        folded = functools.reduce(jnp.add, [fold[some, :] for fold in folds[n:]])
        largest = jnp.maximum(largest, column + jnp.sum(folded.T, axis=0, keepdims=True))
    c = 1.0 / (jnp.max(largest) * (1.0 / tokens) + DAMPING)
    eps = 1.0 - c * DAMPING
    eps2 = eps * eps
    zeta = eps2 * eps2
    eps8 = zeta * zeta
    e2_1, e2_2 = -2.0 * eps * c, c * c
    g_1 = -(1.0 + eps) * c
    g_m = eps2 + (1.0 + eps) * eps + eps
    h_m = zeta + (1.0 + eps2) * eps2 + eps2
    k_m = eps8 + (1.0 + zeta) * zeta + zeta + 1.0 + eps8
    k_z = 1.0 + 3.0 * zeta
    beta = (1.0 + zeta) * (1.0 + eps8)
    last = -c * c * (1.0 / tokens)
    p = c * (1.0 + eps) * (1.0 + eps2) * beta

    def wide(ref, r, some):
        return ref[r, some].astype(jnp.float32)

    for some in halves:
        for r in chunks:
            first = wide(k1, r, some)
            square = e2_1 * first + e2_2 * wide(k2, r, some)
            e2[r, some] = square.astype(jnp.bfloat16)
            g[r, some] = (square + g_1 * first).astype(jnp.bfloat16)

    def fourth(product, r, some):
        square = wide(e2, r, some)
        value = 2.0 * eps2 * square + product
        return value, value + (1.0 + eps2) * square

    symmetric(e2, e2, fourth, z, h)

    def apply(left, right, parts, result, scale=None):
        for some in halves:
            product = dot(left[...], right[:, some])
            for r in chunks_of(product.shape[0]):
                total = product[r] if scale is None else product[r] * scale
                for weight, part in parts:
                    total = total + weight * part[r, some].astype(jnp.float32)
                result[r, some] = total.astype(jnp.bfloat16)

    apply(image, g, [(g_m, image)], by_g)
    symmetric(z, z, lambda product, r, some: [product + k_z * wide(z, r, some)], k)
    apply(by_g, h, [(h_m, by_g)], by_h)
    apply(by_h, k, [(last * (1.0 + eps2) * beta, image), (last * beta, by_g), (last * k_m, by_h)], mixed, last)
    stores = []
    for n in range(len(blocks) + 1):
        moved = dot(mixed[...], late[...] if n == len(blocks) else x[:, blocks[n]])
        for one in (0, 1):
            here = place(fars[2 * n + one])
            part = slice(one * features, (one + 1) * features)
            for r in chunks_of(moved.shape[0]):
                out[r, here] = (p * tile[r, here].astype(jnp.float32) + moved[r, part]).astype(jnp.bfloat16)
            store = pltpu.make_async_copy(out.at[:, here], out_hbm.at[:, here], sems.at[1 + len(stores)])
            store.start()
            stores.append(store)
    for store in stores:
        store.wait()


def by_tokens(factor_inputs, tile):
    members, replicas = lax.axis_size("grad"), lax.axis_size("dp")
    rows, width = tile.shape
    features = factor_inputs.shape[2]
    tokens = factor_inputs.shape[0] * replicas

    def shape(*sizes, kind=jnp.bfloat16):
        return jax.ShapeDtypeStruct(sizes, kind)

    def scratch(*sizes):
        return pltpu.VMEM(sizes, jnp.bfloat16)

    def swap(value, far):
        return lax.ppermute(value, "grad", [(i, i ^ far) for i in range(members)])

    parts = list(split_blocks(factor_inputs, range(replicas)))
    for far in range(1, replicas):
        parts[far] = lax.ppermute(parts[far], "dp", [(i, (i + far) % replicas) for i in range(replicas)])
    own = jnp.concatenate(parts, axis=0)
    fars = (0, 1, 6, 7, 2, 4, 3, 5)
    pieces = {0: own}
    for far in (2, 4, 6):
        pieces[far] = swap(own, far)
    for far in (0, 2, 4, 6):
        pieces[far + 1] = swap(pieces[far], 1)
    pieces = [pieces[far] for far in fars]
    early = width - 2 * features
    columns, turned, gram = pl.pallas_call(
        first_kernel,
        out_shape=[shape(tokens, early), shape(early, tokens), shape(tokens, tokens, kind=jnp.float32)],
        in_specs=[WHOLE] * 6,
        out_specs=[WHOLE] * 3,
        compiler_params=pltpu.CompilerParams(vmem_limit_bytes=16 * 2**20),
        cost_estimate=pl.CostEstimate(flops=4 * 10**8, bytes_accessed=0, transcendentals=0),
        name="first_pieces",
    )(*pieces[:6])
    return pl.pallas_call(
        functools.partial(last_kernel, fars),
        out_shape=shape(rows, width),
        in_specs=[WHOLE] * 5 + [ANYWHERE],
        out_specs=ANYWHERE,
        scratch_shapes=[scratch(rows, width)] * 2
        + [scratch(tokens, 2 * features), scratch(2 * features, tokens)]
        + [scratch(tokens, tokens)] * 7
        + [scratch(rows, tokens)] * 4
        + [pltpu.VMEM((2 * features * n, 128), jnp.float32) for n in range(1, members // 2)]
        + [pltpu.SemaphoreType.DMA((1 + members,))],
        compiler_params=pltpu.CompilerParams(vmem_limit_bytes=51 * 2**20),
        cost_estimate=pl.CostEstimate(flops=5 * 10**9, bytes_accessed=0, transcendentals=0),
        name="whole_block",
    )(*pieces[6:], columns, turned, gram, tile)


def local(factor_inputs, gradients):
    features, members = factor_inputs.shape[2], lax.axis_size("grad")
    tokens = factor_inputs.shape[0] * lax.axis_size("dp")
    tile = gradients[0]
    if tokens < features * members and features % 128 == 0 and (members, lax.axis_size("dp")) == (8, 4):
        result = by_tokens(factor_inputs, tile)
    else:
        result = by_features(gather_block(factor_inputs), tile)
    return result.astype(jnp.bfloat16)[None]


def solution(mesh):
    placed = (P("dp", None, "grad"), P("dp", "grad", None))
    return jax.shard_map(
        local, mesh=mesh, in_specs=placed, out_specs=P("dp", "grad", None), check_vma=False
    )
```

```python
import functools

import jax
import jax.numpy as jnp
from jax import lax
from jax.experimental import pallas as pl
from jax.experimental.pallas import tpu as pltpu
from jax.sharding import PartitionSpec as P

ITERS = 4
DAMPING = 0.01
WHOLE = pl.BlockSpec(memory_space=pltpu.VMEM)
ANYWHERE = pl.BlockSpec(memory_space=pl.ANY)


def dot(a, b):
    return jnp.dot(a, b, preferred_element_type=jnp.float32)


def gather_block(factor_inputs):
    pieces = jnp.transpose(factor_inputs, (1, 0, 2))
    piece = lax.all_to_all(pieces, "dp", split_axis=0, concat_axis=1, tiled=True)[0]
    return lax.all_gather(piece, "grad", axis=1, tiled=True)


def by_features(columns, tile):
    tokens, width = columns.shape
    covariance = jnp.einsum("tr,tc->rc", columns, columns, preferred_element_type=jnp.float32) * (1.0 / tokens)
    damped = covariance + DAMPING * jnp.eye(width, dtype=jnp.float32)
    scale = 1.0 / jnp.max(jnp.sum(jnp.abs(damped), axis=1))
    image = scale * damped
    result = scale * tile.astype(jnp.float32)
    for step in range(ITERS):
        low = image.astype(jnp.bfloat16)
        result = 2.0 * result - dot(result.astype(jnp.bfloat16), low)
        if step < ITERS - 1:
            image = 2.0 * image - dot(low, low)
    return result


def split_kernel(fars, x_ref, *out_refs):
    replicas, tokens = len(out_refs), out_refs[0].shape[0]
    here = lax.axis_index("dp")
    x = x_ref[...]
    rows = lax.broadcasted_iota(jnp.int32, (tokens, tokens * replicas), 0)
    cols = lax.broadcasted_iota(jnp.int32, (tokens, tokens * replicas), 1)
    offset = cols - rows * replicas
    for far, out_ref in zip(fars, out_refs):
        choice = jnp.where(offset == lax.rem(here + far, replicas), 1.0, 0.0).astype(jnp.bfloat16)
        out_ref[...] = dot(choice, x).astype(jnp.bfloat16)


def split_blocks(factor_inputs, fars):
    tokens, blocks, features = factor_inputs.shape
    return pl.pallas_call(
        functools.partial(split_kernel, fars),
        out_shape=[jax.ShapeDtypeStruct((tokens, features), factor_inputs.dtype)] * blocks,
        in_specs=[WHOLE],
        out_specs=[WHOLE] * blocks,
        compiler_params=pltpu.CompilerParams(vmem_limit_bytes=16 * 2**20),
        name="split_blocks",
    )(factor_inputs.reshape(tokens * blocks, features))


def first_kernel(*refs):
    *pieces, columns, turned, gram = refs
    features = pieces[0].shape[1]
    for n, piece in enumerate(pieces):
        some = slice(n * features, (n + 1) * features)
        columns[:, some] = piece[...]
        turned[some, :] = piece[...].T
    gram[...] = dot(columns[...], turned[...])


def last_kernel(fars, late0, late1, x, xt, gram_in, tile_hbm, out_hbm, *refs):
    tile, out, late, late_t, k1, k2, e2, g, z, h, k, image, by_g, by_h, mixed, *folds, sems = refs
    load = pltpu.make_async_copy(tile_hbm, tile, sems.at[0])
    load.start()
    member = lax.axis_index("grad")
    tokens = x.shape[0]
    half = late.shape[1]
    features = half // 2
    halves = [slice(at, at + half) for at in range(0, tokens, half)]
    blocks = [slice(at, at + half) for at in range(0, x.shape[1], half)]

    def chunks_of(size):
        return [slice(at, at + 32) for at in range(0, size, 32)]

    chunks = chunks_of(tokens)

    def place(far):
        return pl.ds(pl.multiple_of((member ^ far) * features, features), features)

    def chosen(some):
        return jnp.concatenate([tile[:, place(far)] for far in some], axis=1)

    late[...] = jnp.concatenate([late0[...], late1[...]], axis=1)
    late_t[...] = late[...].T

    def symmetric(left, right, finish, *refs):
        for n, some in enumerate(halves):
            rows = slice(some.start, tokens)
            product = left(rows, some) if right is None else dot(left[rows, :], right[:, some])
            for r in chunks[some.start // 32 :]:
                values = finish(product[r.start - some.start : r.stop - some.start], r, some)
                for ref, value in zip(refs, values):
                    ref[r, some] = value.astype(jnp.bfloat16)
            for other in halves[n + 1 :]:
                for ref in refs:
                    ref[some, other] = ref[other, some].T

    def gram(rows, some):
        return lax.dot_general(late[rows, :], late[some, :], (((1,), (1,)), ((), ())), preferred_element_type=jnp.float32)

    symmetric(gram, None, lambda product, r, some: [(gram_in[r, some] + product) * (1.0 / tokens)], k1)

    column_sums = [0.0] * (len(blocks) + 1)

    def add_sums(n, left, right):
        product = dot(left, right)
        total = 0.0
        for r in chunks_of(product.shape[0]):
            block = jnp.abs(product[r])
            total = total + block
            if r.start < n * half:
                folds[n - 1][r, :] = block[:, :features] + block[:, features:]
        column_sums[n] = column_sums[n] + jnp.sum(total, axis=0, keepdims=True)

    def move():
        moved, rest = dot(chosen(fars[:-2]), xt[...]), dot(chosen(fars[-2:]), late_t[...])
        for r in chunks_of(moved.shape[0]):
            image[r, :] = (moved[r] + rest[r]).astype(jnp.bfloat16)

    for n, some in enumerate(blocks):
        add_sums(n, xt[: some.stop, :], x[:, some])
    symmetric(k1, k1, lambda product, r, some: [product], k2)
    add_sums(len(blocks), xt[...], late[...])
    product = dot(late_t[...], late[...])
    total = functools.reduce(jnp.add, [jnp.abs(product[r]) for r in chunks_of(half)])
    column_sums[-1] = column_sums[-1] + jnp.sum(total, axis=0, keepdims=True)
    load.wait()
    move()

    largest = column_sums[-1]
    for n, (column, some) in enumerate(zip(column_sums[:-1], blocks)):
        folded = functools.reduce(jnp.add, [fold[some, :] for fold in folds[n:]])
        largest = jnp.maximum(largest, column + jnp.sum(folded.T, axis=0, keepdims=True))
    c = 1.0 / (jnp.max(largest) * (1.0 / tokens) + DAMPING)
    eps = 1.0 - c * DAMPING
    eps2 = eps * eps
    zeta = eps2 * eps2
    eps8 = zeta * zeta
    e2_1, e2_2 = -2.0 * eps * c, c * c
    g_1 = -(1.0 + eps) * c
    g_m = eps2 + (1.0 + eps) * eps + eps
    h_m = zeta + (1.0 + eps2) * eps2 + eps2
    k_m = eps8 + (1.0 + zeta) * zeta + zeta + 1.0 + eps8
    k_z = 1.0 + 3.0 * zeta
    beta = (1.0 + zeta) * (1.0 + eps8)
    last = -c * c * (1.0 / tokens)
    p = c * (1.0 + eps) * (1.0 + eps2) * beta

    def wide(ref, r, some):
        return ref[r, some].astype(jnp.float32)

    for some in halves:
        for r in chunks:
            first = wide(k1, r, some)
            square = e2_1 * first + e2_2 * wide(k2, r, some)
            e2[r, some] = square.astype(jnp.bfloat16)
            g[r, some] = (square + g_1 * first).astype(jnp.bfloat16)

    def fourth(product, r, some):
        square = wide(e2, r, some)
        value = 2.0 * eps2 * square + product
        return value, value + (1.0 + eps2) * square

    symmetric(e2, e2, fourth, z, h)

    def apply(left, right, parts, result, scale=None):
        product = dot(left[...], right[...])
        for r in chunks_of(product.shape[0]):
            total = product[r] if scale is None else product[r] * scale
            for weight, part in parts:
                total = total + weight * part[r, :].astype(jnp.float32)
            result[r, :] = total.astype(jnp.bfloat16)

    apply(image, g, [(g_m, image)], by_g)
    symmetric(z, z, lambda product, r, some: [product + k_z * wide(z, r, some)], k)
    apply(by_g, h, [(h_m, by_g)], by_h)
    apply(by_h, k, [(last * (1.0 + eps2) * beta, image), (last * beta, by_g), (last * k_m, by_h)], mixed, last)
    stores = []
    for n in range(len(blocks) + 1):
        moved = dot(mixed[...], late[...] if n == len(blocks) else x[:, blocks[n]])
        for one in (0, 1):
            here = place(fars[2 * n + one])
            part = slice(one * features, (one + 1) * features)
            for r in chunks_of(moved.shape[0]):
                out[r, here] = (p * tile[r, here].astype(jnp.float32) + moved[r, part]).astype(jnp.bfloat16)
            store = pltpu.make_async_copy(out.at[:, here], out_hbm.at[:, here], sems.at[1 + len(stores)])
            store.start()
            stores.append(store)
    for store in stores:
        store.wait()


def by_tokens(factor_inputs, tile):
    members, replicas = lax.axis_size("grad"), lax.axis_size("dp")
    rows, width = tile.shape
    features = factor_inputs.shape[2]
    tokens = factor_inputs.shape[0] * replicas

    def shape(*sizes, kind=jnp.bfloat16):
        return jax.ShapeDtypeStruct(sizes, kind)

    def scratch(*sizes):
        return pltpu.VMEM(sizes, jnp.bfloat16)

    def swap(value, far):
        return lax.ppermute(value, "grad", [(i, i ^ far) for i in range(members)])

    parts = list(split_blocks(factor_inputs, range(replicas)))
    for far in range(1, replicas):
        parts[far] = lax.ppermute(parts[far], "dp", [(i, (i + far) % replicas) for i in range(replicas)])
    own = jnp.concatenate(parts, axis=0)
    fars = (0, 1, 6, 7, 2, 4, 3, 5)
    pieces = {0: own}
    for far in (2, 4, 6):
        pieces[far] = swap(own, far)
    for far in (0, 2, 4, 6):
        pieces[far + 1] = swap(pieces[far], 1)
    pieces = [pieces[far] for far in fars]
    early = width - 2 * features
    columns, turned, gram = pl.pallas_call(
        first_kernel,
        out_shape=[shape(tokens, early), shape(early, tokens), shape(tokens, tokens, kind=jnp.float32)],
        in_specs=[WHOLE] * 6,
        out_specs=[WHOLE] * 3,
        compiler_params=pltpu.CompilerParams(vmem_limit_bytes=16 * 2**20),
        cost_estimate=pl.CostEstimate(flops=4 * 10**8, bytes_accessed=0, transcendentals=0),
        name="first_pieces",
    )(*pieces[:6])
    return pl.pallas_call(
        functools.partial(last_kernel, fars),
        out_shape=shape(rows, width),
        in_specs=[WHOLE] * 5 + [ANYWHERE],
        out_specs=ANYWHERE,
        scratch_shapes=[scratch(rows, width)] * 2
        + [scratch(tokens, 2 * features), scratch(2 * features, tokens)]
        + [scratch(tokens, tokens)] * 7
        + [scratch(rows, tokens)] * 4
        + [pltpu.VMEM((2 * features * n, 128), jnp.float32) for n in range(1, members // 2)]
        + [pltpu.SemaphoreType.DMA((1 + members,))],
        compiler_params=pltpu.CompilerParams(vmem_limit_bytes=51 * 2**20),
        cost_estimate=pl.CostEstimate(flops=5 * 10**9, bytes_accessed=0, transcendentals=0),
        name="whole_block",
    )(*pieces[6:], columns, turned, gram, tile)


def local(factor_inputs, gradients):
    features, members = factor_inputs.shape[2], lax.axis_size("grad")
    tokens = factor_inputs.shape[0] * lax.axis_size("dp")
    tile = gradients[0]
    if tokens < features * members and features % 128 == 0 and (members, lax.axis_size("dp")) == (8, 4):
        result = by_tokens(factor_inputs, tile)
    else:
        result = by_features(gather_block(factor_inputs), tile)
    return result.astype(jnp.bfloat16)[None]


def solution(mesh):
    placed = (P("dp", None, "grad"), P("dp", "grad", None))
    return jax.shard_map(
        local, mesh=mesh, in_specs=placed, out_specs=P("dp", "grad", None), check_vma=False
    )
```

```python
import functools

import jax
import jax.numpy as jnp
from jax import lax
from jax.experimental import pallas as pl
from jax.experimental.pallas import tpu as pltpu
from jax.sharding import PartitionSpec as P

ITERS = 4
DAMPING = 0.01
WHOLE = pl.BlockSpec(memory_space=pltpu.VMEM)
ANYWHERE = pl.BlockSpec(memory_space=pl.ANY)


def dot(a, b):
    return jnp.dot(a, b, preferred_element_type=jnp.float32)


def gather_block(factor_inputs):
    pieces = jnp.transpose(factor_inputs, (1, 0, 2))
    piece = lax.all_to_all(pieces, "dp", split_axis=0, concat_axis=1, tiled=True)[0]
    return lax.all_gather(piece, "grad", axis=1, tiled=True)


def by_features(columns, tile):
    tokens, width = columns.shape
    covariance = jnp.einsum("tr,tc->rc", columns, columns, preferred_element_type=jnp.float32) * (1.0 / tokens)
    damped = covariance + DAMPING * jnp.eye(width, dtype=jnp.float32)
    scale = 1.0 / jnp.max(jnp.sum(jnp.abs(damped), axis=1))
    image = scale * damped
    result = scale * tile.astype(jnp.float32)
    for step in range(ITERS):
        low = image.astype(jnp.bfloat16)
        result = 2.0 * result - dot(result.astype(jnp.bfloat16), low)
        if step < ITERS - 1:
            image = 2.0 * image - dot(low, low)
    return result


def split_kernel(fars, x_ref, *out_refs):
    replicas, tokens = len(out_refs), out_refs[0].shape[0]
    here = lax.axis_index("dp")
    x = x_ref[...]
    rows = lax.broadcasted_iota(jnp.int32, (tokens, tokens * replicas), 0)
    cols = lax.broadcasted_iota(jnp.int32, (tokens, tokens * replicas), 1)
    offset = cols - rows * replicas
    for far, out_ref in zip(fars, out_refs):
        choice = jnp.where(offset == lax.rem(here + far, replicas), 1.0, 0.0).astype(jnp.bfloat16)
        out_ref[...] = dot(choice, x).astype(jnp.bfloat16)


def split_blocks(factor_inputs, fars):
    tokens, blocks, features = factor_inputs.shape
    return pl.pallas_call(
        functools.partial(split_kernel, fars),
        out_shape=[jax.ShapeDtypeStruct((tokens, features), factor_inputs.dtype)] * blocks,
        in_specs=[WHOLE],
        out_specs=[WHOLE] * blocks,
        compiler_params=pltpu.CompilerParams(vmem_limit_bytes=16 * 2**20),
        name="split_blocks",
    )(factor_inputs.reshape(tokens * blocks, features))


def first_kernel(*refs):
    *pieces, columns, turned, gram = refs
    features = pieces[0].shape[1]
    for n, piece in enumerate(pieces):
        some = slice(n * features, (n + 1) * features)
        columns[:, some] = piece[...]
        turned[some, :] = piece[...].T
    gram[...] = dot(columns[...], turned[...])


def last_kernel(fars, late0, late1, x, xt, gram_in, tile_hbm, out_hbm, *refs):
    tile, out, late, late_t, k1, k2, e2, g, z, h, k, image, by_g, by_h, mixed, *folds, sems = refs
    load = pltpu.make_async_copy(tile_hbm, tile, sems.at[0])
    load.start()
    member = lax.axis_index("grad")
    tokens = x.shape[0]
    half = late.shape[1]
    features = half // 2
    halves = [slice(at, at + half) for at in range(0, tokens, half)]
    blocks = [slice(at, at + half) for at in range(0, x.shape[1], half)]

    def chunks_of(size):
        return [slice(at, at + 32) for at in range(0, size, 32)]

    chunks = chunks_of(tokens)

    def place(far):
        return pl.ds(pl.multiple_of((member ^ far) * features, features), features)

    def chosen(some):
        return jnp.concatenate([tile[:, place(far)] for far in some], axis=1)

    late[...] = jnp.concatenate([late0[...], late1[...]], axis=1)
    late_t[...] = late[...].T

    def symmetric(left, right, finish, *refs):
        for n, some in enumerate(halves):
            rows = slice(some.start, tokens)
            product = left(rows, some) if right is None else dot(left[rows, :], right[:, some])
            for r in chunks[some.start // 32 :]:
                values = finish(product[r.start - some.start : r.stop - some.start], r, some)
                for ref, value in zip(refs, values):
                    ref[r, some] = value.astype(jnp.bfloat16)
            for other in halves[n + 1 :]:
                for ref in refs:
                    ref[some, other] = ref[other, some].T

    def gram(rows, some):
        return lax.dot_general(late[rows, :], late[some, :], (((1,), (1,)), ((), ())), preferred_element_type=jnp.float32)

    symmetric(gram, None, lambda product, r, some: [(gram_in[r, some] + product) * (1.0 / tokens)], k1)

    column_sums = [0.0] * (len(blocks) + 1)

    def add_sums(n, left, right):
        product = dot(left, right)
        total = 0.0
        for r in chunks_of(product.shape[0]):
            block = jnp.abs(product[r])
            total = total + block
            if r.start < n * half:
                folds[n - 1][r, :] = block[:, :features] + block[:, features:]
        column_sums[n] = column_sums[n] + jnp.sum(total, axis=0, keepdims=True)

    def move(some):
        moved, rest = dot(chosen(fars[:-2]), xt[:, some]), dot(chosen(fars[-2:]), late_t[:, some])
        for r in chunks_of(moved.shape[0]):
            image[r, some] = (moved[r] + rest[r]).astype(jnp.bfloat16)

    for n, some in enumerate(blocks):
        add_sums(n, xt[: some.stop, :], x[:, some])
    symmetric(k1, k1, lambda product, r, some: [product], k2)
    add_sums(len(blocks), xt[...], late[...])
    product = dot(late_t[...], late[...])
    total = functools.reduce(jnp.add, [jnp.abs(product[r]) for r in chunks_of(half)])
    column_sums[-1] = column_sums[-1] + jnp.sum(total, axis=0, keepdims=True)
    load.wait()
    for some in halves:
        move(some)

    largest = column_sums[-1]
    for n, (column, some) in enumerate(zip(column_sums[:-1], blocks)):
        folded = functools.reduce(jnp.add, [fold[some, :] for fold in folds[n:]])
        largest = jnp.maximum(largest, column + jnp.sum(folded.T, axis=0, keepdims=True))
    c = 1.0 / (jnp.max(largest) * (1.0 / tokens) + DAMPING)
    eps = 1.0 - c * DAMPING
    eps2 = eps * eps
    zeta = eps2 * eps2
    eps8 = zeta * zeta
    e2_1, e2_2 = -2.0 * eps * c, c * c
    g_1 = -(1.0 + eps) * c
    g_m = eps2 + (1.0 + eps) * eps + eps
    h_m = zeta + (1.0 + eps2) * eps2 + eps2
    k_m = eps8 + (1.0 + zeta) * zeta + zeta + 1.0 + eps8
    k_z = 1.0 + 3.0 * zeta
    beta = (1.0 + zeta) * (1.0 + eps8)
    last = -c * c * (1.0 / tokens)
    p = c * (1.0 + eps) * (1.0 + eps2) * beta

    def wide(ref, r, some):
        return ref[r, some].astype(jnp.float32)

    for some in halves:
        for r in chunks:
            first = wide(k1, r, some)
            square = e2_1 * first + e2_2 * wide(k2, r, some)
            e2[r, some] = square.astype(jnp.bfloat16)
            g[r, some] = (square + g_1 * first).astype(jnp.bfloat16)

    def fourth(product, r, some):
        square = wide(e2, r, some)
        value = 2.0 * eps2 * square + product
        return value, value + (1.0 + eps2) * square

    symmetric(e2, e2, fourth, z, h)

    def apply(left, right, parts, result, scale=None):
        for some in sides:
            product = dot(left[some, :], right[...])
            for r in chunks_of(some.stop - some.start):
                here = slice(some.start + r.start, some.start + r.stop)
                total = product[r] if scale is None else product[r] * scale
                for weight, part in parts:
                    total = total + weight * part[here, :].astype(jnp.float32)
                result[here, :] = total.astype(jnp.bfloat16)

    rows = tile.shape[0]
    sides = [slice(0, rows // 2), slice(rows // 2, rows)]
    apply(image, g, [(g_m, image)], by_g)
    symmetric(z, z, lambda product, r, some: [product + k_z * wide(z, r, some)], k)
    apply(by_g, h, [(h_m, by_g)], by_h)
    apply(by_h, k, [(last * (1.0 + eps2) * beta, image), (last * beta, by_g), (last * k_m, by_h)], mixed, last)
    stores = []

    def send(some, here):
        store = pltpu.make_async_copy(out.at[some, here], out_hbm.at[some, here], sems.at[1 + len(stores)])
        store.start()
        stores.append(store)

    for some in sides:
        for n in range(len(blocks) + 1):
            moved = dot(mixed[some, :], late[...] if n == len(blocks) else x[:, blocks[n]])
            for one in (0, 1):
                here = place(fars[2 * n + one])
                part = slice(one * features, (one + 1) * features)
                for r in chunks_of(moved.shape[0]):
                    at = slice(some.start + r.start, some.start + r.stop)
                    out[at, here] = (p * tile[at, here].astype(jnp.float32) + moved[r, part]).astype(jnp.bfloat16)
                if some is sides[-1]:
                    send(some, here)
        if some is not sides[-1]:
            send(some, slice(None))
    for store in stores:
        store.wait()


def by_tokens(factor_inputs, tile):
    members, replicas = lax.axis_size("grad"), lax.axis_size("dp")
    rows, width = tile.shape
    features = factor_inputs.shape[2]
    tokens = factor_inputs.shape[0] * replicas

    def shape(*sizes, kind=jnp.bfloat16):
        return jax.ShapeDtypeStruct(sizes, kind)

    def scratch(*sizes):
        return pltpu.VMEM(sizes, jnp.bfloat16)

    def swap(value, far):
        return lax.ppermute(value, "grad", [(i, i ^ far) for i in range(members)])

    parts = list(split_blocks(factor_inputs, range(replicas)))
    for far in range(1, replicas):
        parts[far] = lax.ppermute(parts[far], "dp", [(i, (i + far) % replicas) for i in range(replicas)])
    own = jnp.concatenate(parts, axis=0)
    fars = (0, 1, 6, 7, 2, 4, 3, 5)
    pieces = {0: own}
    for far in (2, 4, 6):
        pieces[far] = swap(own, far)
    for far in (0, 2, 4, 6):
        pieces[far + 1] = swap(pieces[far], 1)
    pieces = [pieces[far] for far in fars]
    early = width - 2 * features
    columns, turned, gram = pl.pallas_call(
        first_kernel,
        out_shape=[shape(tokens, early), shape(early, tokens), shape(tokens, tokens, kind=jnp.float32)],
        in_specs=[WHOLE] * 6,
        out_specs=[WHOLE] * 3,
        compiler_params=pltpu.CompilerParams(vmem_limit_bytes=16 * 2**20),
        cost_estimate=pl.CostEstimate(flops=4 * 10**8, bytes_accessed=0, transcendentals=0),
        name="first_pieces",
    )(*pieces[:6])
    return pl.pallas_call(
        functools.partial(last_kernel, fars),
        out_shape=shape(rows, width),
        in_specs=[WHOLE] * 5 + [ANYWHERE],
        out_specs=ANYWHERE,
        scratch_shapes=[scratch(rows, width)] * 2
        + [scratch(tokens, 2 * features), scratch(2 * features, tokens)]
        + [scratch(tokens, tokens)] * 7
        + [scratch(rows, tokens)] * 4
        + [pltpu.VMEM((2 * features * n, 128), jnp.float32) for n in range(1, members // 2)]
        + [pltpu.SemaphoreType.DMA((2 + members,))],
        compiler_params=pltpu.CompilerParams(vmem_limit_bytes=51 * 2**20),
        cost_estimate=pl.CostEstimate(flops=5 * 10**9, bytes_accessed=0, transcendentals=0),
        name="whole_block",
    )(*pieces[6:], columns, turned, gram, tile)


def local(factor_inputs, gradients):
    features, members = factor_inputs.shape[2], lax.axis_size("grad")
    tokens = factor_inputs.shape[0] * lax.axis_size("dp")
    tile = gradients[0]
    if tokens < features * members and features % 128 == 0 and (members, lax.axis_size("dp")) == (8, 4):
        result = by_tokens(factor_inputs, tile)
    else:
        result = by_features(gather_block(factor_inputs), tile)
    return result.astype(jnp.bfloat16)[None]


def solution(mesh):
    placed = (P("dp", None, "grad"), P("dp", "grad", None))
    return jax.shard_map(
        local, mesh=mesh, in_specs=placed, out_specs=P("dp", "grad", None), check_vma=False
    )
```

```python
import functools

import jax
import jax.numpy as jnp
from jax import lax
from jax.experimental import pallas as pl
from jax.experimental.pallas import tpu as pltpu
from jax.sharding import PartitionSpec as P

ITERS = 4
DAMPING = 0.01
WHOLE = pl.BlockSpec(memory_space=pltpu.VMEM)
ANYWHERE = pl.BlockSpec(memory_space=pl.ANY)


def dot(a, b):
    return jnp.dot(a, b, preferred_element_type=jnp.float32)


def gather_block(factor_inputs):
    pieces = jnp.transpose(factor_inputs, (1, 0, 2))
    piece = lax.all_to_all(pieces, "dp", split_axis=0, concat_axis=1, tiled=True)[0]
    return lax.all_gather(piece, "grad", axis=1, tiled=True)


def by_features(columns, tile):
    tokens, width = columns.shape
    covariance = jnp.einsum("tr,tc->rc", columns, columns, preferred_element_type=jnp.float32) * (1.0 / tokens)
    damped = covariance + DAMPING * jnp.eye(width, dtype=jnp.float32)
    scale = 1.0 / jnp.max(jnp.sum(jnp.abs(damped), axis=1))
    image = scale * damped
    result = scale * tile.astype(jnp.float32)
    for step in range(ITERS):
        low = image.astype(jnp.bfloat16)
        result = 2.0 * result - dot(result.astype(jnp.bfloat16), low)
        if step < ITERS - 1:
            image = 2.0 * image - dot(low, low)
    return result


def split_kernel(fars, x_ref, *out_refs):
    replicas, tokens = len(out_refs), out_refs[0].shape[0]
    here = lax.axis_index("dp")
    x = x_ref[...]
    rows = lax.broadcasted_iota(jnp.int32, (tokens, tokens * replicas), 0)
    cols = lax.broadcasted_iota(jnp.int32, (tokens, tokens * replicas), 1)
    offset = cols - rows * replicas
    for far, out_ref in zip(fars, out_refs):
        choice = jnp.where(offset == lax.rem(here + far, replicas), 1.0, 0.0).astype(jnp.bfloat16)
        out_ref[...] = dot(choice, x).astype(jnp.bfloat16)


def split_blocks(factor_inputs, fars):
    tokens, blocks, features = factor_inputs.shape
    return pl.pallas_call(
        functools.partial(split_kernel, fars),
        out_shape=[jax.ShapeDtypeStruct((tokens, features), factor_inputs.dtype)] * blocks,
        in_specs=[WHOLE],
        out_specs=[WHOLE] * blocks,
        compiler_params=pltpu.CompilerParams(vmem_limit_bytes=16 * 2**20),
        name="split_blocks",
    )(factor_inputs.reshape(tokens * blocks, features))


def first_kernel(*refs):
    *pieces, columns, turned, gram = refs
    features = pieces[0].shape[1]
    for n, piece in enumerate(pieces):
        some = slice(n * features, (n + 1) * features)
        columns[:, some] = piece[...]
        turned[some, :] = piece[...].T
    gram[...] = dot(columns[...], turned[...])


def last_kernel(fars, late0, late1, x, xt, gram_in, tile_hbm, out_hbm, *refs):
    tile, out, late, late_t, k1, k2, e2, g, z, h, k, image, by_g, by_h, mixed, *folds, sems = refs
    load = pltpu.make_async_copy(tile_hbm, tile, sems.at[0])
    load.start()
    member = lax.axis_index("grad")
    tokens = x.shape[0]
    half = late.shape[1]
    features = half // 2
    halves = [slice(at, at + half) for at in range(0, tokens, half)]
    blocks = [slice(at, at + half) for at in range(0, x.shape[1], half)]

    def chunks_of(size):
        return [slice(at, at + 32) for at in range(0, size, 32)]

    chunks = chunks_of(tokens)

    def place(far):
        return pl.ds(pl.multiple_of((member ^ far) * features, features), features)

    def chosen(some):
        return jnp.concatenate([tile[:, place(far)] for far in some], axis=1)

    late[...] = jnp.concatenate([late0[...], late1[...]], axis=1)
    late_t[...] = late[...].T

    def symmetric(left, right, finish, *refs):
        for n, some in enumerate(halves):
            rows = slice(some.start, tokens)
            product = left(rows, some) if right is None else dot(left[rows, :], right[:, some])
            for r in chunks[some.start // 32 :]:
                values = finish(product[r.start - some.start : r.stop - some.start], r, some)
                for ref, value in zip(refs, values):
                    ref[r, some] = value.astype(jnp.bfloat16)
            for other in halves[n + 1 :]:
                for ref in refs:
                    ref[some, other] = ref[other, some].T

    def gram(rows, some):
        return lax.dot_general(late[rows, :], late[some, :], (((1,), (1,)), ((), ())), preferred_element_type=jnp.float32)

    symmetric(gram, None, lambda product, r, some: [(gram_in[r, some] + product) * (1.0 / tokens)], k1)

    column_sums = [0.0] * (len(blocks) + 1)

    def add_sums(n, left, right):
        product = dot(left, right)
        total = 0.0
        for r in chunks_of(product.shape[0]):
            block = jnp.abs(product[r])
            total = total + block
            if r.start < n * half:
                folds[n - 1][r, :] = block[:, :features] + block[:, features:]
        column_sums[n] = column_sums[n] + jnp.sum(total, axis=0, keepdims=True)

    def move(some):
        moved, rest = dot(chosen(fars[:-2]), xt[:, some]), dot(chosen(fars[-2:]), late_t[:, some])
        for r in chunks_of(moved.shape[0]):
            image[r, some] = (moved[r] + rest[r]).astype(jnp.bfloat16)

    for n, some in enumerate(blocks):
        add_sums(n, xt[: some.stop, :], x[:, some])
    symmetric(k1, k1, lambda product, r, some: [product], k2)
    add_sums(len(blocks), xt[...], late[...])
    product = dot(late_t[...], late[...])
    total = functools.reduce(jnp.add, [jnp.abs(product[r]) for r in chunks_of(half)])
    column_sums[-1] = column_sums[-1] + jnp.sum(total, axis=0, keepdims=True)
    load.wait()
    for some in halves:
        move(some)

    largest = column_sums[-1]
    for n, (column, some) in enumerate(zip(column_sums[:-1], blocks)):
        folded = functools.reduce(jnp.add, [fold[some, :] for fold in folds[n:]])
        largest = jnp.maximum(largest, column + jnp.sum(folded.T, axis=0, keepdims=True))
    c = 1.0 / (jnp.max(largest) * (1.0 / tokens) + DAMPING)
    eps = 1.0 - c * DAMPING
    eps2 = eps * eps
    zeta = eps2 * eps2
    eps8 = zeta * zeta
    e2_1, e2_2 = -2.0 * eps * c, c * c
    g_1 = -(1.0 + eps) * c
    g_m = eps2 + (1.0 + eps) * eps + eps
    h_m = zeta + (1.0 + eps2) * eps2 + eps2
    k_m = eps8 + (1.0 + zeta) * zeta + zeta + 1.0 + eps8
    k_z = 1.0 + 3.0 * zeta
    beta = (1.0 + zeta) * (1.0 + eps8)
    last = -c * c * (1.0 / tokens)
    p = c * (1.0 + eps) * (1.0 + eps2) * beta

    def wide(ref, r, some):
        return ref[r, some].astype(jnp.float32)

    for some in halves:
        for r in chunks:
            first = wide(k1, r, some)
            square = e2_1 * first + e2_2 * wide(k2, r, some)
            e2[r, some] = square.astype(jnp.bfloat16)
            g[r, some] = (square + g_1 * first).astype(jnp.bfloat16)

    def fourth(product, r, some):
        square = wide(e2, r, some)
        value = 2.0 * eps2 * square + product
        return value, value + (1.0 + eps2) * square

    symmetric(e2, e2, fourth, z, h)

    def apply(left, right, parts, result, scale=None):
        for some in halves:
            product = dot(left[...], right[:, some])
            for r in chunks_of(product.shape[0]):
                total = product[r] if scale is None else product[r] * scale
                for weight, part in parts:
                    total = total + weight * part[r, some].astype(jnp.float32)
                result[r, some] = total.astype(jnp.bfloat16)

    apply(image, g, [(g_m, image)], by_g)
    symmetric(z, z, lambda product, r, some: [product + k_z * wide(z, r, some)], k)
    apply(by_g, h, [(h_m, by_g)], by_h)
    apply(by_h, k, [(last * (1.0 + eps2) * beta, image), (last * beta, by_g), (last * k_m, by_h)], mixed, last)
    stores = []
    for n in range(len(blocks) + 1):
        moved = dot(mixed[...], late[...] if n == len(blocks) else x[:, blocks[n]])
        for one in (0, 1):
            here = place(fars[2 * n + one])
            part = slice(one * features, (one + 1) * features)
            for r in chunks_of(moved.shape[0]):
                out[r, here] = (p * tile[r, here].astype(jnp.float32) + moved[r, part]).astype(jnp.bfloat16)
            store = pltpu.make_async_copy(out.at[:, here], out_hbm.at[:, here], sems.at[1 + len(stores)])
            store.start()
            stores.append(store)
    for store in stores:
        store.wait()


def by_tokens(factor_inputs, tile):
    members, replicas = lax.axis_size("grad"), lax.axis_size("dp")
    rows, width = tile.shape
    features = factor_inputs.shape[2]
    tokens = factor_inputs.shape[0] * replicas

    def shape(*sizes, kind=jnp.bfloat16):
        return jax.ShapeDtypeStruct(sizes, kind)

    def scratch(*sizes):
        return pltpu.VMEM(sizes, jnp.bfloat16)

    def swap(value, far):
        return lax.ppermute(value, "grad", [(i, i ^ far) for i in range(members)])

    parts = list(split_blocks(factor_inputs, range(replicas)))
    for far in range(replicas - 1, 0, -1):
        parts[far] = lax.ppermute(parts[far], "dp", [(i, (i + far) % replicas) for i in range(replicas)])
    own = jnp.concatenate(parts[:1] + parts[:0:-1], axis=0)
    fars = (0, 1, 6, 7, 2, 4, 3, 5)
    pieces = {0: own}
    for far in (2, 4, 6):
        pieces[far] = swap(own, far)
    for far in (0, 2, 4, 6):
        pieces[far + 1] = swap(pieces[far], 1)
    pieces = [pieces[far] for far in fars]
    early = width - 2 * features
    columns, turned, gram = pl.pallas_call(
        first_kernel,
        out_shape=[shape(tokens, early), shape(early, tokens), shape(tokens, tokens, kind=jnp.float32)],
        in_specs=[WHOLE] * 6,
        out_specs=[WHOLE] * 3,
        compiler_params=pltpu.CompilerParams(vmem_limit_bytes=16 * 2**20),
        cost_estimate=pl.CostEstimate(flops=4 * 10**8, bytes_accessed=0, transcendentals=0),
        name="first_pieces",
    )(*pieces[:6])
    return pl.pallas_call(
        functools.partial(last_kernel, fars),
        out_shape=shape(rows, width),
        in_specs=[WHOLE] * 5 + [ANYWHERE],
        out_specs=ANYWHERE,
        scratch_shapes=[scratch(rows, width)] * 2
        + [scratch(tokens, 2 * features), scratch(2 * features, tokens)]
        + [scratch(tokens, tokens)] * 7
        + [scratch(rows, tokens)] * 4
        + [pltpu.VMEM((2 * features * n, 128), jnp.float32) for n in range(1, members // 2)]
        + [pltpu.SemaphoreType.DMA((1 + members,))],
        compiler_params=pltpu.CompilerParams(vmem_limit_bytes=51 * 2**20),
        cost_estimate=pl.CostEstimate(flops=5 * 10**9, bytes_accessed=0, transcendentals=0),
        name="whole_block",
    )(*pieces[6:], columns, turned, gram, tile)


def local(factor_inputs, gradients):
    features, members = factor_inputs.shape[2], lax.axis_size("grad")
    tokens = factor_inputs.shape[0] * lax.axis_size("dp")
    tile = gradients[0]
    if tokens < features * members and features % 128 == 0 and (members, lax.axis_size("dp")) == (8, 4):
        result = by_tokens(factor_inputs, tile)
    else:
        result = by_features(gather_block(factor_inputs), tile)
    return result.astype(jnp.bfloat16)[None]


def solution(mesh):
    placed = (P("dp", None, "grad"), P("dp", "grad", None))
    return jax.shard_map(
        local, mesh=mesh, in_specs=placed, out_specs=P("dp", "grad", None), check_vma=False
    )
```

```python
import functools

import jax
import jax.numpy as jnp
from jax import lax
from jax.experimental import pallas as pl
from jax.experimental.pallas import tpu as pltpu
from jax.sharding import PartitionSpec as P

ITERS = 4
DAMPING = 0.01
WHOLE = pl.BlockSpec(memory_space=pltpu.VMEM)
ANYWHERE = pl.BlockSpec(memory_space=pl.ANY)


def dot(a, b):
    return jnp.dot(a, b, preferred_element_type=jnp.float32)


def gather_block(factor_inputs):
    pieces = jnp.transpose(factor_inputs, (1, 0, 2))
    piece = lax.all_to_all(pieces, "dp", split_axis=0, concat_axis=1, tiled=True)[0]
    return lax.all_gather(piece, "grad", axis=1, tiled=True)


def by_features(columns, tile):
    tokens, width = columns.shape
    covariance = jnp.einsum("tr,tc->rc", columns, columns, preferred_element_type=jnp.float32) * (1.0 / tokens)
    damped = covariance + DAMPING * jnp.eye(width, dtype=jnp.float32)
    scale = 1.0 / jnp.max(jnp.sum(jnp.abs(damped), axis=1))
    image = scale * damped
    result = scale * tile.astype(jnp.float32)
    for step in range(ITERS):
        low = image.astype(jnp.bfloat16)
        result = 2.0 * result - dot(result.astype(jnp.bfloat16), low)
        if step < ITERS - 1:
            image = 2.0 * image - dot(low, low)
    return result


def split_kernel(fars, x_ref, *out_refs):
    replicas, tokens = len(out_refs), out_refs[0].shape[0]
    here = lax.axis_index("dp")
    x = x_ref[...]
    rows = lax.broadcasted_iota(jnp.int32, (tokens, tokens * replicas), 0)
    cols = lax.broadcasted_iota(jnp.int32, (tokens, tokens * replicas), 1)
    offset = cols - rows * replicas
    for far, out_ref in zip(fars, out_refs):
        choice = jnp.where(offset == lax.rem(here + far, replicas), 1.0, 0.0).astype(jnp.bfloat16)
        out_ref[...] = dot(choice, x).astype(jnp.bfloat16)


def split_blocks(factor_inputs, fars):
    tokens, blocks, features = factor_inputs.shape
    return pl.pallas_call(
        functools.partial(split_kernel, fars),
        out_shape=[jax.ShapeDtypeStruct((tokens, features), factor_inputs.dtype)] * blocks,
        in_specs=[WHOLE],
        out_specs=[WHOLE] * blocks,
        compiler_params=pltpu.CompilerParams(vmem_limit_bytes=16 * 2**20),
        name="split_blocks",
    )(factor_inputs.reshape(tokens * blocks, features))


def first_kernel(*refs):
    *pieces, columns, turned, gram = refs
    features = pieces[0].shape[1]
    for n, piece in enumerate(pieces):
        some = slice(n * features, (n + 1) * features)
        columns[:, some] = piece[...]
        turned[some, :] = piece[...].T
    gram[...] = dot(columns[...], turned[...])


def last_kernel(fars, late0, late1, x, xt, gram_in, tile_hbm, out_hbm, *refs):
    tile, out, late, late_t, k1, k2, e2, g, z, h, k, image, by_g, by_h, mixed, *folds, sems = refs
    load = pltpu.make_async_copy(tile_hbm, tile, sems.at[0])
    load.start()
    member = lax.axis_index("grad")
    tokens = x.shape[0]
    half = late.shape[1]
    features = half // 2
    halves = [slice(at, at + half) for at in range(0, tokens, half)]
    blocks = [slice(at, at + half) for at in range(0, x.shape[1], half)]

    def chunks_of(size):
        return [slice(at, at + 32) for at in range(0, size, 32)]

    chunks = chunks_of(tokens)

    def place(far):
        return pl.ds(pl.multiple_of((member ^ far) * features, features), features)

    def chosen(some):
        return jnp.concatenate([tile[:, place(far)] for far in some], axis=1)

    late[...] = jnp.concatenate([late0[...], late1[...]], axis=1)
    late_t[...] = late[...].T

    def symmetric(left, right, finish, *refs):
        for n, some in enumerate(halves):
            rows = slice(some.start, tokens)
            product = left(rows, some) if right is None else dot(left[rows, :], right[:, some])
            for r in chunks[some.start // 32 :]:
                values = finish(product[r.start - some.start : r.stop - some.start], r, some)
                for ref, value in zip(refs, values):
                    ref[r, some] = value.astype(jnp.bfloat16)
            for other in halves[n + 1 :]:
                for ref in refs:
                    ref[some, other] = ref[other, some].T

    def gram(rows, some):
        return lax.dot_general(late[rows, :], late[some, :], (((1,), (1,)), ((), ())), preferred_element_type=jnp.float32)

    symmetric(gram, None, lambda product, r, some: [(gram_in[r, some] + product) * (1.0 / tokens)], k1)

    column_sums = [0.0] * (len(blocks) + 1)

    def add_sums(n, left, right):
        product = dot(left, right)
        total = 0.0
        for r in chunks_of(product.shape[0]):
            block = jnp.abs(product[r])
            total = total + block
            if r.start < n * half:
                folds[n - 1][r, :] = block[:, :features] + block[:, features:]
        column_sums[n] = column_sums[n] + jnp.sum(total, axis=0, keepdims=True)

    def move(some):
        moved, rest = dot(chosen(fars[:-2]), xt[:, some]), dot(chosen(fars[-2:]), late_t[:, some])
        for r in chunks_of(moved.shape[0]):
            image[r, some] = (moved[r] + rest[r]).astype(jnp.bfloat16)

    for n, some in enumerate(blocks):
        add_sums(n, xt[: some.stop, :], x[:, some])
    symmetric(k1, k1, lambda product, r, some: [product], k2)
    add_sums(len(blocks), xt[...], late[...])
    product = dot(late_t[...], late[...])
    total = functools.reduce(jnp.add, [jnp.abs(product[r]) for r in chunks_of(half)])
    column_sums[-1] = column_sums[-1] + jnp.sum(total, axis=0, keepdims=True)
    load.wait()
    for some in halves:
        move(some)

    largest = column_sums[-1]
    for n, (column, some) in enumerate(zip(column_sums[:-1], blocks)):
        folded = functools.reduce(jnp.add, [fold[some, :] for fold in folds[n:]])
        largest = jnp.maximum(largest, column + jnp.sum(folded.T, axis=0, keepdims=True))
    c = 1.0 / (jnp.max(largest) * (1.0 / tokens) + DAMPING)
    eps = 1.0 - c * DAMPING
    eps2 = eps * eps
    zeta = eps2 * eps2
    eps8 = zeta * zeta
    e2_1, e2_2 = -2.0 * eps * c, c * c
    g_1 = -(1.0 + eps) * c
    g_m = eps2 + (1.0 + eps) * eps + eps
    h_m = zeta + (1.0 + eps2) * eps2 + eps2
    k_m = eps8 + (1.0 + zeta) * zeta + zeta + 1.0 + eps8
    k_z = 1.0 + 3.0 * zeta
    beta = (1.0 + zeta) * (1.0 + eps8)
    last = -c * c * (1.0 / tokens)
    p = c * (1.0 + eps) * (1.0 + eps2) * beta

    def wide(ref, r, some):
        return ref[r, some].astype(jnp.float32)

    for some in halves:
        for r in chunks:
            first = wide(k1, r, some)
            square = e2_1 * first + e2_2 * wide(k2, r, some)
            e2[r, some] = square.astype(jnp.bfloat16)
            g[r, some] = (square + g_1 * first).astype(jnp.bfloat16)

    def fourth(product, r, some):
        square = wide(e2, r, some)
        value = 2.0 * eps2 * square + product
        return value, value + (1.0 + eps2) * square

    symmetric(e2, e2, fourth, z, h)

    def apply(left, right, parts, result, scale=None):
        for some in halves:
            product = dot(left[...], right[:, some])
            for r in chunks_of(product.shape[0]):
                total = product[r] if scale is None else product[r] * scale
                for weight, part in parts:
                    total = total + weight * part[r, some].astype(jnp.float32)
                result[r, some] = total.astype(jnp.bfloat16)

    apply(image, g, [(g_m, image)], by_g)
    symmetric(z, z, lambda product, r, some: [product + k_z * wide(z, r, some)], k)
    apply(by_g, h, [(h_m, by_g)], by_h)
    apply(by_h, k, [(last * (1.0 + eps2) * beta, image), (last * beta, by_g), (last * k_m, by_h)], mixed, last)
    stores = []
    for n in range(len(blocks) + 1):
        moved = dot(mixed[...], late[...] if n == len(blocks) else x[:, blocks[n]])
        for one in (0, 1):
            here = place(fars[2 * n + one])
            part = slice(one * features, (one + 1) * features)
            for r in chunks_of(moved.shape[0]):
                out[r, here] = (p * tile[r, here].astype(jnp.float32) + moved[r, part]).astype(jnp.bfloat16)
            store = pltpu.make_async_copy(out.at[:, here], out_hbm.at[:, here], sems.at[1 + len(stores)])
            store.start()
            stores.append(store)
    for store in stores:
        store.wait()


def by_tokens(factor_inputs, tile):
    members, replicas = lax.axis_size("grad"), lax.axis_size("dp")
    rows, width = tile.shape
    features = factor_inputs.shape[2]
    tokens = factor_inputs.shape[0] * replicas

    def shape(*sizes, kind=jnp.bfloat16):
        return jax.ShapeDtypeStruct(sizes, kind)

    def scratch(*sizes):
        return pltpu.VMEM(sizes, jnp.bfloat16)

    def swap(value, far):
        return lax.ppermute(value, "grad", [(i, i ^ far) for i in range(members)])

    parts = list(split_blocks(factor_inputs, range(replicas)))
    order = (0, 1, 3, 2)
    for far in order[1:]:
        parts[far] = lax.ppermute(parts[far], "dp", [(i, (i + far) % replicas) for i in range(replicas)])
    own = jnp.concatenate([parts[far] for far in order], axis=0)
    fars = (0, 1, 6, 7, 2, 4, 3, 5)
    pieces = {0: own}
    for far in (2, 4, 6):
        pieces[far] = swap(own, far)
    for far in (0, 2, 4, 6):
        pieces[far + 1] = swap(pieces[far], 1)
    pieces = [pieces[far] for far in fars]
    early = width - 2 * features
    columns, turned, gram = pl.pallas_call(
        first_kernel,
        out_shape=[shape(tokens, early), shape(early, tokens), shape(tokens, tokens, kind=jnp.float32)],
        in_specs=[WHOLE] * 6,
        out_specs=[WHOLE] * 3,
        compiler_params=pltpu.CompilerParams(vmem_limit_bytes=16 * 2**20),
        cost_estimate=pl.CostEstimate(flops=4 * 10**8, bytes_accessed=0, transcendentals=0),
        name="first_pieces",
    )(*pieces[:6])
    return pl.pallas_call(
        functools.partial(last_kernel, fars),
        out_shape=shape(rows, width),
        in_specs=[WHOLE] * 5 + [ANYWHERE],
        out_specs=ANYWHERE,
        scratch_shapes=[scratch(rows, width)] * 2
        + [scratch(tokens, 2 * features), scratch(2 * features, tokens)]
        + [scratch(tokens, tokens)] * 7
        + [scratch(rows, tokens)] * 4
        + [pltpu.VMEM((2 * features * n, 128), jnp.float32) for n in range(1, members // 2)]
        + [pltpu.SemaphoreType.DMA((1 + members,))],
        compiler_params=pltpu.CompilerParams(vmem_limit_bytes=51 * 2**20),
        cost_estimate=pl.CostEstimate(flops=5 * 10**9, bytes_accessed=0, transcendentals=0),
        name="whole_block",
    )(*pieces[6:], columns, turned, gram, tile)


def local(factor_inputs, gradients):
    features, members = factor_inputs.shape[2], lax.axis_size("grad")
    tokens = factor_inputs.shape[0] * lax.axis_size("dp")
    tile = gradients[0]
    if tokens < features * members and features % 128 == 0 and (members, lax.axis_size("dp")) == (8, 4):
        result = by_tokens(factor_inputs, tile)
    else:
        result = by_features(gather_block(factor_inputs), tile)
    return result.astype(jnp.bfloat16)[None]


def solution(mesh):
    placed = (P("dp", None, "grad"), P("dp", "grad", None))
    return jax.shard_map(
        local, mesh=mesh, in_specs=placed, out_specs=P("dp", "grad", None), check_vma=False
    )
```

```python
import functools

import jax
import jax.numpy as jnp
from jax import lax
from jax.experimental import pallas as pl
from jax.experimental.pallas import tpu as pltpu
from jax.sharding import PartitionSpec as P

ITERS = 4
DAMPING = 0.01
WHOLE = pl.BlockSpec(memory_space=pltpu.VMEM)
ANYWHERE = pl.BlockSpec(memory_space=pl.ANY)


def dot(a, b):
    return jnp.dot(a, b, preferred_element_type=jnp.float32)


def gather_block(factor_inputs):
    pieces = jnp.transpose(factor_inputs, (1, 0, 2))
    piece = lax.all_to_all(pieces, "dp", split_axis=0, concat_axis=1, tiled=True)[0]
    return lax.all_gather(piece, "grad", axis=1, tiled=True)


def by_features(columns, tile):
    tokens, width = columns.shape
    covariance = jnp.einsum("tr,tc->rc", columns, columns, preferred_element_type=jnp.float32) * (1.0 / tokens)
    damped = covariance + DAMPING * jnp.eye(width, dtype=jnp.float32)
    scale = 1.0 / jnp.max(jnp.sum(jnp.abs(damped), axis=1))
    image = scale * damped
    result = scale * tile.astype(jnp.float32)
    for step in range(ITERS):
        low = image.astype(jnp.bfloat16)
        result = 2.0 * result - dot(result.astype(jnp.bfloat16), low)
        if step < ITERS - 1:
            image = 2.0 * image - dot(low, low)
    return result


def split_kernel(fars, x_ref, *out_refs):
    replicas, tokens = len(out_refs), out_refs[0].shape[0]
    here = lax.axis_index("dp")
    x = x_ref[...]
    rows = lax.broadcasted_iota(jnp.int32, (tokens, tokens * replicas), 0)
    cols = lax.broadcasted_iota(jnp.int32, (tokens, tokens * replicas), 1)
    offset = cols - rows * replicas
    for far, out_ref in zip(fars, out_refs):
        choice = jnp.where(offset == lax.rem(here + far, replicas), 1.0, 0.0).astype(jnp.bfloat16)
        out_ref[...] = dot(choice, x).astype(jnp.bfloat16)


def split_blocks(factor_inputs, fars):
    tokens, blocks, features = factor_inputs.shape
    return pl.pallas_call(
        functools.partial(split_kernel, fars),
        out_shape=[jax.ShapeDtypeStruct((tokens, features), factor_inputs.dtype)] * blocks,
        in_specs=[WHOLE],
        out_specs=[WHOLE] * blocks,
        compiler_params=pltpu.CompilerParams(vmem_limit_bytes=16 * 2**20),
        name="split_blocks",
    )(factor_inputs.reshape(tokens * blocks, features))


def first_kernel(*refs):
    *pieces, columns, turned, gram = refs
    features = pieces[0].shape[1]
    for n, piece in enumerate(pieces):
        some = slice(n * features, (n + 1) * features)
        columns[:, some] = piece[...]
        turned[some, :] = piece[...].T
    gram[...] = dot(columns[...], turned[...])


def last_kernel(fars, late0, late1, x, xt, gram_in, tile_hbm, out_hbm, *refs):
    tile, out, late, late_t, k1, k2, e2, g, z, h, k, image, by_g, by_h, mixed, *folds, sems = refs
    load = pltpu.make_async_copy(tile_hbm, tile, sems.at[0])
    load.start()
    member = lax.axis_index("grad")
    tokens = x.shape[0]
    half = late.shape[1]
    features = half // 2
    halves = [slice(at, at + half) for at in range(0, tokens, half)]
    blocks = [slice(at, at + half) for at in range(0, x.shape[1], half)]

    def chunks_of(size):
        return [slice(at, at + 32) for at in range(0, size, 32)]

    chunks = chunks_of(tokens)

    def place(far):
        return pl.ds(pl.multiple_of((member ^ far) * features, features), features)

    def chosen(some):
        return jnp.concatenate([tile[:, place(far)] for far in some], axis=1)

    late[...] = jnp.concatenate([late0[...], late1[...]], axis=1)
    late_t[...] = late[...].T

    def symmetric(left, right, finish, *refs):
        for n, some in enumerate(halves):
            rows = slice(some.start, tokens)
            product = left(rows, some) if right is None else dot(left[rows, :], right[:, some])
            for r in chunks[some.start // 32 :]:
                values = finish(product[r.start - some.start : r.stop - some.start], r, some)
                for ref, value in zip(refs, values):
                    ref[r, some] = value.astype(jnp.bfloat16)
            for other in halves[n + 1 :]:
                for ref in refs:
                    ref[some, other] = ref[other, some].T

    def gram(rows, some):
        return lax.dot_general(late[rows, :], late[some, :], (((1,), (1,)), ((), ())), preferred_element_type=jnp.float32)

    symmetric(gram, None, lambda product, r, some: [(gram_in[r, some] + product) * (1.0 / tokens)], k1)

    column_sums = [0.0] * (len(blocks) + 1)

    def add_sums(n, left, right):
        product = dot(left, right)
        total = 0.0
        for r in chunks_of(product.shape[0]):
            block = jnp.abs(product[r])
            total = total + block
            if r.start < n * half:
                folds[n - 1][r, :] = block[:, :features] + block[:, features:]
        column_sums[n] = column_sums[n] + jnp.sum(total, axis=0, keepdims=True)

    def move(some):
        moved, rest = dot(chosen(fars[:-2]), xt[:, some]), dot(chosen(fars[-2:]), late_t[:, some])
        for r in chunks_of(moved.shape[0]):
            image[r, some] = (moved[r] + rest[r]).astype(jnp.bfloat16)

    for n, some in enumerate(blocks):
        add_sums(n, xt[: some.stop, :], x[:, some])
    symmetric(k1, k1, lambda product, r, some: [product], k2)
    add_sums(len(blocks), xt[...], late[...])
    product = dot(late_t[...], late[...])
    total = functools.reduce(jnp.add, [jnp.abs(product[r]) for r in chunks_of(half)])
    column_sums[-1] = column_sums[-1] + jnp.sum(total, axis=0, keepdims=True)
    load.wait()
    for some in halves:
        move(some)

    largest = column_sums[-1]
    for n, (column, some) in enumerate(zip(column_sums[:-1], blocks)):
        folded = functools.reduce(jnp.add, [fold[some, :] for fold in folds[n:]])
        largest = jnp.maximum(largest, column + jnp.sum(folded.T, axis=0, keepdims=True))
    c = 1.0 / (jnp.max(largest) * (1.0 / tokens) + DAMPING)
    eps = 1.0 - c * DAMPING
    eps2 = eps * eps
    zeta = eps2 * eps2
    eps8 = zeta * zeta
    e2_1, e2_2 = -2.0 * eps * c, c * c
    g_1 = -(1.0 + eps) * c
    g_m = eps2 + (1.0 + eps) * eps + eps
    h_m = zeta + (1.0 + eps2) * eps2 + eps2
    k_m = eps8 + (1.0 + zeta) * zeta + zeta + 1.0 + eps8
    k_z = 1.0 + 3.0 * zeta
    beta = (1.0 + zeta) * (1.0 + eps8)
    last = -c * c * (1.0 / tokens)
    p = c * (1.0 + eps) * (1.0 + eps2) * beta

    def wide(ref, r, some):
        return ref[r, some].astype(jnp.float32)

    for some in halves:
        for r in chunks:
            first = wide(k1, r, some)
            square = e2_1 * first + e2_2 * wide(k2, r, some)
            e2[r, some] = square.astype(jnp.bfloat16)
            g[r, some] = (square + g_1 * first).astype(jnp.bfloat16)

    def fourth(product, r, some):
        square = wide(e2, r, some)
        value = 2.0 * eps2 * square + product
        return value, value + (1.0 + eps2) * square

    symmetric(e2, e2, fourth, z, h)

    def apply(left, right, parts, result, scale=None):
        for some in halves:
            product = dot(left[...], right[:, some])
            for r in chunks_of(product.shape[0]):
                total = product[r] if scale is None else product[r] * scale
                for weight, part in parts:
                    total = total + weight * part[r, some].astype(jnp.float32)
                result[r, some] = total.astype(jnp.bfloat16)

    apply(image, g, [(g_m, image)], by_g)
    symmetric(z, z, lambda product, r, some: [product + k_z * wide(z, r, some)], k)
    apply(by_g, h, [(h_m, by_g)], by_h)
    apply(by_h, k, [(last * (1.0 + eps2) * beta, image), (last * beta, by_g), (last * k_m, by_h)], mixed, last)
    stores = []
    for n in range(len(blocks) + 1):
        moved = dot(mixed[...], late[...] if n == len(blocks) else x[:, blocks[n]])
        for one in (0, 1):
            here = place(fars[2 * n + one])
            part = slice(one * features, (one + 1) * features)
            for r in chunks_of(moved.shape[0]):
                out[r, here] = (p * tile[r, here].astype(jnp.float32) + moved[r, part]).astype(jnp.bfloat16)
            if n < 2 and one == 0:
                continue
            if n < 2:
                chip = lax.shift_right_logical(member ^ fars[2 * n], 1)
                here = pl.ds(pl.multiple_of(chip * half, half), half)
            store = pltpu.make_async_copy(out.at[:, here], out_hbm.at[:, here], sems.at[1 + len(stores)])
            store.start()
            stores.append(store)
    for store in stores:
        store.wait()


def by_tokens(factor_inputs, tile):
    members, replicas = lax.axis_size("grad"), lax.axis_size("dp")
    rows, width = tile.shape
    features = factor_inputs.shape[2]
    tokens = factor_inputs.shape[0] * replicas

    def shape(*sizes, kind=jnp.bfloat16):
        return jax.ShapeDtypeStruct(sizes, kind)

    def scratch(*sizes):
        return pltpu.VMEM(sizes, jnp.bfloat16)

    def swap(value, far):
        return lax.ppermute(value, "grad", [(i, i ^ far) for i in range(members)])

    parts = list(split_blocks(factor_inputs, range(replicas)))
    for far in range(1, replicas):
        parts[far] = lax.ppermute(parts[far], "dp", [(i, (i + far) % replicas) for i in range(replicas)])
    own = jnp.concatenate(parts, axis=0)
    fars = (0, 1, 6, 7, 2, 4, 3, 5)
    pieces = {0: own}
    for far in (2, 4, 6):
        pieces[far] = swap(own, far)
    for far in (0, 2, 4, 6):
        pieces[far + 1] = swap(pieces[far], 1)
    pieces = [pieces[far] for far in fars]
    early = width - 2 * features
    columns, turned, gram = pl.pallas_call(
        first_kernel,
        out_shape=[shape(tokens, early), shape(early, tokens), shape(tokens, tokens, kind=jnp.float32)],
        in_specs=[WHOLE] * 6,
        out_specs=[WHOLE] * 3,
        compiler_params=pltpu.CompilerParams(vmem_limit_bytes=16 * 2**20),
        cost_estimate=pl.CostEstimate(flops=4 * 10**8, bytes_accessed=0, transcendentals=0),
        name="first_pieces",
    )(*pieces[:6])
    return pl.pallas_call(
        functools.partial(last_kernel, fars),
        out_shape=shape(rows, width),
        in_specs=[WHOLE] * 5 + [ANYWHERE],
        out_specs=ANYWHERE,
        scratch_shapes=[scratch(rows, width)] * 2
        + [scratch(tokens, 2 * features), scratch(2 * features, tokens)]
        + [scratch(tokens, tokens)] * 7
        + [scratch(rows, tokens)] * 4
        + [pltpu.VMEM((2 * features * n, 128), jnp.float32) for n in range(1, members // 2)]
        + [pltpu.SemaphoreType.DMA((1 + members,))],
        compiler_params=pltpu.CompilerParams(vmem_limit_bytes=51 * 2**20),
        cost_estimate=pl.CostEstimate(flops=5 * 10**9, bytes_accessed=0, transcendentals=0),
        name="whole_block",
    )(*pieces[6:], columns, turned, gram, tile)


def local(factor_inputs, gradients):
    features, members = factor_inputs.shape[2], lax.axis_size("grad")
    tokens = factor_inputs.shape[0] * lax.axis_size("dp")
    tile = gradients[0]
    if tokens < features * members and features % 128 == 0 and (members, lax.axis_size("dp")) == (8, 4):
        result = by_tokens(factor_inputs, tile)
    else:
        result = by_features(gather_block(factor_inputs), tile)
    return result.astype(jnp.bfloat16)[None]


def solution(mesh):
    placed = (P("dp", None, "grad"), P("dp", "grad", None))
    return jax.shard_map(
        local, mesh=mesh, in_specs=placed, out_specs=P("dp", "grad", None), check_vma=False
    )
```

```python
import functools

import jax
import jax.numpy as jnp
from jax import lax
from jax.experimental import pallas as pl
from jax.experimental.pallas import tpu as pltpu
from jax.sharding import PartitionSpec as P

ITERS = 4
DAMPING = 0.01
WHOLE = pl.BlockSpec(memory_space=pltpu.VMEM)
ANYWHERE = pl.BlockSpec(memory_space=pl.ANY)


def dot(a, b):
    return jnp.dot(a, b, preferred_element_type=jnp.float32)


def gather_block(factor_inputs):
    pieces = jnp.transpose(factor_inputs, (1, 0, 2))
    piece = lax.all_to_all(pieces, "dp", split_axis=0, concat_axis=1, tiled=True)[0]
    return lax.all_gather(piece, "grad", axis=1, tiled=True)


def by_features(columns, tile):
    tokens, width = columns.shape
    covariance = jnp.einsum("tr,tc->rc", columns, columns, preferred_element_type=jnp.float32) * (1.0 / tokens)
    damped = covariance + DAMPING * jnp.eye(width, dtype=jnp.float32)
    scale = 1.0 / jnp.max(jnp.sum(jnp.abs(damped), axis=1))
    image = scale * damped
    result = scale * tile.astype(jnp.float32)
    for step in range(ITERS):
        low = image.astype(jnp.bfloat16)
        result = 2.0 * result - dot(result.astype(jnp.bfloat16), low)
        if step < ITERS - 1:
            image = 2.0 * image - dot(low, low)
    return result


def split_kernel(fars, x_ref, *out_refs):
    replicas, tokens = len(out_refs), out_refs[0].shape[0]
    here = lax.axis_index("dp")
    x = x_ref[...]
    rows = lax.broadcasted_iota(jnp.int32, (tokens, tokens * replicas), 0)
    cols = lax.broadcasted_iota(jnp.int32, (tokens, tokens * replicas), 1)
    offset = cols - rows * replicas
    for far, out_ref in zip(fars, out_refs):
        choice = jnp.where(offset == lax.rem(here + far, replicas), 1.0, 0.0).astype(jnp.bfloat16)
        out_ref[...] = dot(choice, x).astype(jnp.bfloat16)


def split_blocks(factor_inputs, fars):
    tokens, blocks, features = factor_inputs.shape
    return pl.pallas_call(
        functools.partial(split_kernel, fars),
        out_shape=[jax.ShapeDtypeStruct((tokens, features), factor_inputs.dtype)] * blocks,
        in_specs=[WHOLE],
        out_specs=[WHOLE] * blocks,
        compiler_params=pltpu.CompilerParams(vmem_limit_bytes=16 * 2**20),
        name="split_blocks",
    )(factor_inputs.reshape(tokens * blocks, features))


def first_kernel(*refs):
    *pieces, columns, turned, gram = refs
    features = pieces[0].shape[1]
    for n, piece in enumerate(pieces):
        some = slice(n * features, (n + 1) * features)
        columns[:, some] = piece[...]
        turned[some, :] = piece[...].T
    gram[...] = dot(columns[...], turned[...])


def last_kernel(fars, late0, late1, x, xt, gram_in, tile_hbm, out_hbm, *refs):
    tile, out, late, late_t, k1, k2, e2, g, z, h, k, image, by_g, by_h, mixed, *folds, sems = refs
    load = pltpu.make_async_copy(tile_hbm, tile, sems.at[0])
    load.start()
    member = lax.axis_index("grad")
    tokens = x.shape[0]
    half = late.shape[1]
    features = half // 2
    halves = [slice(at, at + half) for at in range(0, tokens, half)]
    blocks = [slice(at, at + half) for at in range(0, x.shape[1], half)]

    def chunks_of(size):
        return [slice(at, at + 32) for at in range(0, size, 32)]

    chunks = chunks_of(tokens)

    def place(far):
        return pl.ds(pl.multiple_of((member ^ far) * features, features), features)

    def chosen(some):
        return jnp.concatenate([tile[:, place(far)] for far in some], axis=1)

    late[...] = jnp.concatenate([late0[...], late1[...]], axis=1)
    late_t[...] = late[...].T

    def symmetric(left, right, finish, *refs):
        for n, some in enumerate(halves):
            rows = slice(some.start, tokens)
            product = left(rows, some) if right is None else dot(left[rows, :], right[:, some])
            for r in chunks[some.start // 32 :]:
                values = finish(product[r.start - some.start : r.stop - some.start], r, some)
                for ref, value in zip(refs, values):
                    ref[r, some] = value.astype(jnp.bfloat16)
            for other in halves[n + 1 :]:
                for ref in refs:
                    ref[some, other] = ref[other, some].T

    def gram(rows, some):
        return lax.dot_general(late[rows, :], late[some, :], (((1,), (1,)), ((), ())), preferred_element_type=jnp.float32)

    symmetric(gram, None, lambda product, r, some: [(gram_in[r, some] + product) * (1.0 / tokens)], k1)

    column_sums = [0.0] * (len(blocks) + 1)

    def add_sums(n, left, right):
        product = dot(left, right)
        total = 0.0
        for r in chunks_of(product.shape[0]):
            block = jnp.abs(product[r])
            total = total + block
            if r.start < n * half:
                folds[n - 1][r, :] = block[:, :features] + block[:, features:]
        column_sums[n] = column_sums[n] + jnp.sum(total, axis=0, keepdims=True)

    def move(some):
        moved, rest = dot(chosen(fars[:-2]), xt[:, some]), dot(chosen(fars[-2:]), late_t[:, some])
        for r in chunks_of(moved.shape[0]):
            image[r, some] = (moved[r] + rest[r]).astype(jnp.bfloat16)

    for n, some in enumerate(blocks):
        add_sums(n, xt[: some.stop, :], x[:, some])
    symmetric(k1, k1, lambda product, r, some: [product], k2)
    add_sums(len(blocks), xt[...], late[...])
    product = dot(late_t[...], late[...])
    total = functools.reduce(jnp.add, [jnp.abs(product[r]) for r in chunks_of(half)])
    column_sums[-1] = column_sums[-1] + jnp.sum(total, axis=0, keepdims=True)
    load.wait()
    for some in halves:
        move(some)

    largest = column_sums[-1]
    for n, (column, some) in enumerate(zip(column_sums[:-1], blocks)):
        folded = functools.reduce(jnp.add, [fold[some, :] for fold in folds[n:]])
        largest = jnp.maximum(largest, column + jnp.sum(folded.T, axis=0, keepdims=True))
    c = 1.0 / (jnp.max(largest) * (1.0 / tokens) + DAMPING)
    eps = 1.0 - c * DAMPING
    eps2 = eps * eps
    zeta = eps2 * eps2
    eps8 = zeta * zeta
    e2_1, e2_2 = -2.0 * eps * c, c * c
    g_1 = -(1.0 + eps) * c
    g_m = eps2 + (1.0 + eps) * eps + eps
    h_m = zeta + (1.0 + eps2) * eps2 + eps2
    k_m = eps8 + (1.0 + zeta) * zeta + zeta + 1.0 + eps8
    k_z = 1.0 + 3.0 * zeta
    beta = (1.0 + zeta) * (1.0 + eps8)
    last = -c * c * (1.0 / tokens)
    p = c * (1.0 + eps) * (1.0 + eps2) * beta

    def wide(ref, r, some):
        return ref[r, some].astype(jnp.float32)

    for some in halves:
        for r in chunks:
            first = wide(k1, r, some)
            square = e2_1 * first + e2_2 * wide(k2, r, some)
            e2[r, some] = square.astype(jnp.bfloat16)
            g[r, some] = (square + g_1 * first).astype(jnp.bfloat16)

    def fourth(product, r, some):
        square = wide(e2, r, some)
        value = 2.0 * eps2 * square + product
        return value, value + (1.0 + eps2) * square

    symmetric(e2, e2, fourth, z, h)

    def apply(left, right, parts, result, scale=None):
        for some in halves:
            product = dot(left[...], right[:, some])
            for r in chunks_of(product.shape[0]):
                total = product[r] if scale is None else product[r] * scale
                for weight, part in parts:
                    total = total + weight * part[r, some].astype(jnp.float32)
                result[r, some] = total.astype(jnp.bfloat16)

    apply(image, g, [(g_m, image)], by_g)
    for some in halves:
        product = dot(z[...], z[:, some])
        for r in chunks:
            k[r, some] = (product[r] + k_z * wide(z, r, some)).astype(jnp.bfloat16)
    apply(by_g, h, [(h_m, by_g)], by_h)
    apply(by_h, k, [(last * (1.0 + eps2) * beta, image), (last * beta, by_g), (last * k_m, by_h)], mixed, last)
    stores = []
    for n in range(len(blocks) + 1):
        moved = dot(mixed[...], late[...] if n == len(blocks) else x[:, blocks[n]])
        for one in (0, 1):
            here = place(fars[2 * n + one])
            part = slice(one * features, (one + 1) * features)
            for r in chunks_of(moved.shape[0]):
                out[r, here] = (p * tile[r, here].astype(jnp.float32) + moved[r, part]).astype(jnp.bfloat16)
            if n < 2 and one == 0:
                continue
            if n < 2:
                chip = lax.shift_right_logical(member ^ fars[2 * n], 1)
                here = pl.ds(pl.multiple_of(chip * half, half), half)
            store = pltpu.make_async_copy(out.at[:, here], out_hbm.at[:, here], sems.at[1 + len(stores)])
            store.start()
            stores.append(store)
    for store in stores:
        store.wait()


def by_tokens(factor_inputs, tile):
    members, replicas = lax.axis_size("grad"), lax.axis_size("dp")
    rows, width = tile.shape
    features = factor_inputs.shape[2]
    tokens = factor_inputs.shape[0] * replicas

    def shape(*sizes, kind=jnp.bfloat16):
        return jax.ShapeDtypeStruct(sizes, kind)

    def scratch(*sizes):
        return pltpu.VMEM(sizes, jnp.bfloat16)

    def swap(value, far):
        return lax.ppermute(value, "grad", [(i, i ^ far) for i in range(members)])

    parts = list(split_blocks(factor_inputs, range(replicas)))
    for far in range(1, replicas):
        parts[far] = lax.ppermute(parts[far], "dp", [(i, (i + far) % replicas) for i in range(replicas)])
    own = jnp.concatenate(parts, axis=0)
    fars = (0, 1, 6, 7, 2, 4, 3, 5)
    pieces = {0: own}
    for far in (2, 4, 6):
        pieces[far] = swap(own, far)
    for far in (0, 2, 4, 6):
        pieces[far + 1] = swap(pieces[far], 1)
    pieces = [pieces[far] for far in fars]
    early = width - 2 * features
    columns, turned, gram = pl.pallas_call(
        first_kernel,
        out_shape=[shape(tokens, early), shape(early, tokens), shape(tokens, tokens, kind=jnp.float32)],
        in_specs=[WHOLE] * 6,
        out_specs=[WHOLE] * 3,
        compiler_params=pltpu.CompilerParams(vmem_limit_bytes=16 * 2**20),
        cost_estimate=pl.CostEstimate(flops=4 * 10**8, bytes_accessed=0, transcendentals=0),
        name="first_pieces",
    )(*pieces[:6])
    return pl.pallas_call(
        functools.partial(last_kernel, fars),
        out_shape=shape(rows, width),
        in_specs=[WHOLE] * 5 + [ANYWHERE],
        out_specs=ANYWHERE,
        scratch_shapes=[scratch(rows, width)] * 2
        + [scratch(tokens, 2 * features), scratch(2 * features, tokens)]
        + [scratch(tokens, tokens)] * 7
        + [scratch(rows, tokens)] * 4
        + [pltpu.VMEM((2 * features * n, 128), jnp.float32) for n in range(1, members // 2)]
        + [pltpu.SemaphoreType.DMA((1 + members,))],
        compiler_params=pltpu.CompilerParams(vmem_limit_bytes=51 * 2**20),
        cost_estimate=pl.CostEstimate(flops=5 * 10**9, bytes_accessed=0, transcendentals=0),
        name="whole_block",
    )(*pieces[6:], columns, turned, gram, tile)


def local(factor_inputs, gradients):
    features, members = factor_inputs.shape[2], lax.axis_size("grad")
    tokens = factor_inputs.shape[0] * lax.axis_size("dp")
    tile = gradients[0]
    if tokens < features * members and features % 128 == 0 and (members, lax.axis_size("dp")) == (8, 4):
        result = by_tokens(factor_inputs, tile)
    else:
        result = by_features(gather_block(factor_inputs), tile)
    return result.astype(jnp.bfloat16)[None]


def solution(mesh):
    placed = (P("dp", None, "grad"), P("dp", "grad", None))
    return jax.shard_map(
        local, mesh=mesh, in_specs=placed, out_specs=P("dp", "grad", None), check_vma=False
    )
```
